128 devices in a mesh: dp: 8 (over x_lo, y), mp: 16 (over x_hi, z, core).
Axes of the slice: x: 4 (x_hi: 2, x_lo: 2; x = x_hi * 2 + x_lo), y: 4, z: 4, core: 2. Of those that a mesh axis runs over, the one named last changes fastest.
Arguments:
- grad_parts: float32 [8, 4096, 4096], P('dp', None, 'mp'), may hold values from -3 to 3
- home: int32 [8], replicated, may hold values from 0 to 7, each once
- left_stat: float32 [64, 512, 512], P('dp', 'mp'), may hold values from -3 to 3
- right_stat: float32 [64, 512, 512], P('dp', 'mp'), may hold values from -3 to 3
- left_root: bfloat16 [64, 512, 512], P('dp', 'mp'), may hold values from -0.5 to 1.5
- right_root: bfloat16 [64, 512, 512], P('dp', 'mp'), may hold values from -0.5 to 1.5
- first_moment: float32 [64, 512, 512], P('dp', 'mp'), may hold values from -2 to 2
- second_moment: float32 [64, 512, 512], P('dp', 'mp'), may hold values from 0.02 to 0.5
Outputs:
- new_left: float32 [64, 512, 512], P('dp', 'mp')
- new_right: float32 [64, 512, 512], P('dp', 'mp')
- new_first: float32 [64, 512, 512], P('dp', 'mp')
- new_second: float32 [64, 512, 512], P('dp', 'mp')
- update: bfloat16 [4096, 4096], P('dp', 'mp')
The draws below stay inside these ranges and needn't reach their ends.
Inputs may be any that keep to these rules, and one draw needn't show every extreme that they name: Each block row is named once; block row r is owned by index home[r] // 1 of dp.
All inputs are finite; a program needn't handle non-finite values.
Results may differ from the reference program's by a relative error of at most 0.001.
Values may be sent and summed in bfloat16 or wider, within the bound.
A program may use at most 64 MiB of HBM per device.

```python
import math
import jax
import jax.numpy as jnp
from jax import lax

B = 512
BC = 8
BR = 8
NBLK = 64
ROWS = 4096
COLS = 4096
N_DP = 8


def draw_grad_parts(key, part):
    key = jax.random.fold_in(key, 11)
    keys = jax.random.split(key, 3)
    row_scale = jnp.exp(jax.random.uniform(keys[0], (ROWS,), jnp.float32, 0.0, math.log(10.0)))
    ramp = 1.0 + 2.0 * (jnp.arange(ROWS) % B).astype(jnp.float32) / (B - 1)
    col_scale = jnp.exp(jax.random.uniform(keys[1], (COLS,), jnp.float32, 0.0, math.log(10.0)))
    scale = 0.003 / math.sqrt(N_DP) * (row_scale * ramp)[:, None] * col_scale[None, :]
    base = jax.random.truncated_normal(keys[2], -4.0, 4.0, (N_DP, ROWS, COLS), jnp.float32)
    return base * scale[None]


def root_from(noise, diagonal):
    unit = jnp.arange(B)[:, None] == jnp.arange(B)[None, :]
    return jnp.where(unit[None], diagonal, 0.6 * noise / math.sqrt(B)).astype(jnp.bfloat16)


def draw_left_root(key, part):
    key = jax.random.fold_in(key, 21)
    keys = jax.random.split(key, 2)
    diagonal = jax.random.uniform(keys[0], (NBLK, B, 1), jnp.float32, 0.5, 1.5)
    noise = jax.random.truncated_normal(keys[1], -4.0, 4.0, (NBLK, B, B), jnp.float32)
    return root_from(noise, diagonal)


def draw_right_root(key, part):
    key = jax.random.fold_in(key, 37)
    keys = jax.random.split(key, 2)
    diagonal = jax.random.uniform(keys[0], (NBLK, B, 1), jnp.float32, 0.5, 1.5)
    noise = jax.random.truncated_normal(keys[1], -4.0, 4.0, (NBLK, B, B), jnp.float32)
    return root_from(noise, diagonal)


def steps_of(own_key, dims, shards, least, high):
    def one(axis_at, shards_of):
        draws = jax.random.uniform(jax.random.fold_in(jax.random.fold_in(own_key, 6), axis_at), (shards_of,), jnp.float32, least / len(shards), high / len(shards))
        return jnp.repeat(jnp.exp(draws), dims[axis_at] // shards_of).reshape((-1,) + (1,) * (len(dims) - axis_at - 1))

    factor_of = one(*shards[0])
    for cut in shards[1:]:
        factor_of = factor_of * one(*cut)
    return factor_of


def scatter_about(key, extent, spread, reach, pieces=(), kind=jnp.bfloat16):
    level = steps_of(key, extent, pieces, -0.22, 0.18) if pieces else 1.0
    array = jax.random.normal(key, extent, jnp.float32) * spread * level
    return jnp.minimum(jnp.maximum(array, -reach), reach).astype(kind)


def setup_inputs(seed: int = 0) -> dict:
    splits = jax.random.split(jax.random.key(seed), 9)
    return {
        "grad_parts": draw_grad_parts(jax.random.fold_in(splits[8], 71), 0),
        "home": jax.random.permutation(splits[1], BR).astype(jnp.int32),
        "left_stat": scatter_about(splits[2], (NBLK, B, B), 0.5, 3.0, ((0, 8), (1, 16)), jnp.float32),
        "right_stat": scatter_about(splits[3], (NBLK, B, B), 0.5, 3.0, ((0, 8), (1, 16)), jnp.float32),
        "left_root": draw_left_root(jax.random.fold_in(splits[8], 71), 0),
        "right_root": draw_right_root(jax.random.fold_in(splits[8], 71), 0),
        "first_moment": scatter_about(splits[6], (NBLK, B, B), 0.3, 2.0, ((0, 8), (1, 16)), jnp.float32),
        "second_moment": jnp.clip(jnp.exp(math.log(0.5) - 3.218876 * jax.random.uniform(splits[7], (NBLK, B, B), jnp.float32) ** steps_of(splits[7], (NBLK, B, B), ((0, 8), (1, 16)), -0.2, 0.2)), 0.02, 0.5),
    }


HIGH = lax.Precision.HIGHEST
FIRST_DECAY = 0.9
SECOND_DECAY = 0.999
ADAM_EPS = 1e-08
NORM_EPS = 1e-06

def one_slot(inputs):
    grad, left, right, left_inv, right_inv, first, second = inputs
    new_left = left + jnp.dot(grad, grad.T, precision=HIGH, preferred_element_type=jnp.float32)
    new_right = right + jnp.dot(grad.T, grad, precision=HIGH, preferred_element_type=jnp.float32)
    left_applied = jnp.dot(left_inv.astype(jnp.float32), grad, precision=HIGH, preferred_element_type=jnp.float32)
    precond = jnp.dot(left_applied, right_inv.astype(jnp.float32), precision=HIGH, preferred_element_type=jnp.float32)
    new_first = FIRST_DECAY * first + (1.0 - FIRST_DECAY) * grad
    new_second = SECOND_DECAY * second + (1.0 - SECOND_DECAY) * grad * grad
    adam = new_first / (jnp.sqrt(new_second) + ADAM_EPS)
    graft_scale = jnp.sqrt(jnp.sum(adam * adam)) / (jnp.sqrt(jnp.sum(precond * precond)) + NORM_EPS)
    update = (precond * graft_scale).astype(jnp.bfloat16)
    return (new_left, new_right, new_first, new_second, update)

def reference(grad_parts, home, left_stat, right_stat, left_root, right_root, first_moment, second_moment):
    summed_grad = lax.optimization_barrier(jnp.sum(grad_parts, axis=0))
    row_order = jnp.arange(BR, dtype=jnp.int32)
    source = lax.optimization_barrier(jnp.sum(jnp.where(home[:, None] == row_order[None, :], row_order[:, None], 0), axis=0)).astype(jnp.int32)
    block_grid = summed_grad.reshape(BR, B, BC, B)[source]
    slot_grads = jnp.transpose(block_grid, (0, 2, 1, 3)).reshape(NBLK, B, B)
    results = lax.map(one_slot, (slot_grads, left_stat, right_stat, left_root, right_root, first_moment, second_moment))
    new_left, new_right, new_first, new_second, slot_update = results
    update = jnp.transpose(slot_update.reshape(BR, BC, B, B), (0, 2, 1, 3)).reshape(ROWS, COLS)
    return (new_left, new_right, new_first, new_second, update)
```

```python
import functools
import math

import jax
import jax.numpy as jnp
from jax import lax
from jax.experimental import pallas as pl
from jax.experimental.pallas import tpu as pltpu
from jax.sharding import PartitionSpec as P

FIRST_DECAY = 0.9
SECOND_DECAY = 0.999
ADAM_EPS = 1e-08
NORM_EPS = 1e-06
MESH = pl.DeviceIdType.MESH
F32 = jnp.float32
BF16 = jnp.bfloat16
I16 = jnp.int16
I32 = jnp.int32

B = 512
H = 256
S = 32
T = 16
LANES = 128
NB = 8
NY = 4
FULL = 32760.0
STEP = math.log(2.0) / 4.0
TINY = 1e-30

PEERS = [(a, b) for a in range(2) for b in range(4) if (a, b) != (0, 0)]


def code_of(peak):
    return jnp.ceil(jnp.log(jnp.maximum(peak, TINY)) * (1.0 / STEP))


def coded(x, code):
    return jnp.floor(x * (jnp.exp(code * -STEP) * FULL) + 0.5).astype(I32).astype(I16)


def scale_of(code):
    return jnp.exp(code.astype(I32).astype(F32) * STEP) * (1.0 / FULL)


def decoded(values, scale):
    return values.astype(I32).astype(F32) * scale


def encode_piece(read, out):
    for t in range(H // LANES):
        cols = pl.ds(t * LANES, LANES)
        x = read(cols).reshape(H // T, T, LANES)
        code = code_of(jnp.max(jnp.abs(x), axis=0))
        out[pl.ds(0, H), cols] = coded(x, code[None]).reshape(H, LANES)
        out[pl.ds(H, T), cols] = code.astype(I32).astype(I16)


def decode_piece(codes, cols):
    scale = scale_of(codes[pl.ds(H, T), cols])
    values = codes[pl.ds(0, H), cols].reshape(H // T, T, LANES)
    return decoded(values, scale[None]).reshape(H, LANES)


def encode_rows(x, out):
    n = B // LANES
    parts = [x[:, t * LANES : (t + 1) * LANES].reshape(S // T, T, LANES) for t in range(n)]
    peak = functools.reduce(jnp.maximum, [jnp.max(jnp.abs(p), axis=0) for p in parts])
    code = code_of(peak)
    for t in range(n):
        out[pl.ds(t * S, S), :] = coded(parts[t], code[None]).reshape(S, LANES)
    out[pl.ds(n * S, T), :] = code.astype(I32).astype(I16)


def decode_rows(codes):
    n = B // LANES
    scale = scale_of(codes[pl.ds(n * S, T), :])
    return [
        decoded(codes[pl.ds(t * S, S), :].reshape(S // T, T, LANES), scale[None]).reshape(S, LANES)
        for t in range(n)
    ]


def dot(a, b, dims=((1,), (0,))):
    return lax.dot_general(a, b, (dims, ((), ())), preferred_element_type=F32)


def split(x):
    high = x.astype(BF16)
    return high, (x - high.astype(F32)).astype(BF16)


def fold(x):
    r, c = x.shape
    x = jnp.sum(x.reshape(r // 8, 8, c), axis=0)
    return functools.reduce(jnp.add, [x[:, t * LANES : (t + 1) * LANES] for t in range(c // LANES)])


def kernel(
    home, part_hbm, left_hbm, right_hbm, lroot_hbm, rroot_hbm, first_hbm, second_hbm,
    new_left, new_right, new_first, new_second, update,
    part, left, right, first, second, lroot, rroot,
    x1_out, x1_in, y1_out, y1_in, x2_out, x2_in, y2_out, y2_in,
    acc, ghigh, glow, grow_out, grow_in, prod_out, prod_in, pright, precond,
    sums_out, sums_in, pair_out, pair_in,
    load_sem, root_send, root_recv, x1_send, x1_recv, y1_send, y1_recv, s2_send, s2_recv,
    core_send, core_recv, row_send, row_recv, sum_send, sum_recv,
):
    d = lax.axis_index("dp")
    m = lax.axis_index("mp")
    xl, y = d // NY, d % NY
    xh, z, k = m // 8, (m // 2) % 4, m % 2
    c = m // 2

    partner = (d, m + 1 - 2 * k)
    across = ((1 - xl) * NY + y, m)

    def along_y(j):
        return (xl * NY + (y + j) % NY, m)

    def chip_at(a, b):
        return ((xh + a) % 2) * 4 + (z + b) % 4

    def along_mp(a, b):
        return (d, chip_at(a, b) * 2 + k)

    def remote(src, dst, send, recv, device):
        return pltpu.make_async_remote_copy(
            src_ref=src, dst_ref=dst, send_sem=send, recv_sem=recv, device_id=device, device_id_type=MESH
        )

    loads = [
        pltpu.make_async_copy(src, dst, load_sem.at[i])
        for i, (src, dst) in enumerate(
            [
                (part_hbm, part), (left_hbm, left), (right_hbm, right), (first_hbm, first), (second_hbm, second),
                (lroot_hbm.at[c], lroot.at[c, k]), (rroot_hbm.at[c], rroot.at[c, k]),
            ]
        )
    ]
    loads[0].start()

    barrier = pltpu.get_barrier_semaphore()
    greeted = [partner, across] + [along_y(j) for j in (1, 2, 3)] + [along_mp(a, b) for a, b in PEERS]
    for device in greeted:
        pl.semaphore_signal(barrier, inc=1, device_id=device, device_id_type=MESH)
    pl.semaphore_wait(barrier, len(greeted))

    root_copies = []
    for i, (a, b) in enumerate(PEERS):
        there = chip_at(a, b)
        for w, (src, dst) in enumerate(((lroot_hbm, lroot), (rroot_hbm, rroot))):
            copy = remote(src.at[there], dst.at[c, k], root_send.at[w, i], root_recv.at[w, i], along_mp(a, b))
            copy.start()
            root_copies.append(copy)
    for load in loads[1:]:
        load.start()

    def source(q):
        return functools.reduce(jnp.maximum, [jnp.where(home[r] == q, r, 0) for r in range(NB)])

    def own_piece(q, half):
        row = source(q)
        return lambda cols: part[row, pl.ds(half * H, H), cols]

    def chunk(to_x, j):
        return to_x * NY + (y + j) % NY

    loads[0].wait()
    x1_copies, y1_copies = {}, {}

    def send_x1(j):
        encode_piece(own_piece(chunk(1 - xl, j), 1), x1_out.at[j])
        x1_copies[j] = remote(x1_out.at[j], x1_in.at[j], x1_send.at[j], x1_recv.at[j], across)
        x1_copies[j].start()

    def send_y1(w, j):
        to_x = 1 - xl if w == 0 else xl
        n = w * 3 + j - 1
        encode_piece(own_piece(chunk(to_x, j), 0), y1_out.at[n])
        y1_copies[w, j] = remote(y1_out.at[n], y1_in.at[n], y1_send.at[n], y1_recv.at[n], along_y(j))
        y1_copies[w, j].start()

    for j in (1, 2, 3):
        send_x1(j)
        send_y1(0, j)
    for j in (1, 2, 3):
        send_y1(1, j)
    send_x1(0)

    y2_copies = {}
    for j in (1, 2, 3):
        x1_copies[j].wait_recv()
        own = own_piece(chunk(xl, j), 1)
        encode_piece(lambda cols: own(cols) + decode_piece(x1_in.at[j], cols), y2_out.at[j - 1])
        y2_copies[j] = remote(y2_out.at[j - 1], y2_in.at[j - 1], s2_send.at[j], s2_recv.at[j], along_y(j))
        y2_copies[j].start()

    def y1_sum(w, read):
        def total(cols):
            out = read(cols)
            for j in (1, 2, 3):
                out = out + decode_piece(y1_in.at[w * 3 + j - 1], cols)
            return out

        return total

    for j in (1, 2, 3):
        y1_copies[0, j].wait_recv()
    encode_piece(y1_sum(0, own_piece(chunk(1 - xl, 0), 0)), x2_out)
    x2_copy = remote(x2_out, x2_in, s2_send.at[0], s2_recv.at[0], across)
    x2_copy.start()

    for copy in root_copies:
        copy.wait_recv()
    loads[5].wait()
    loads[6].wait()
    core_copies = []
    for w, ref in enumerate((lroot, rroot)):
        copy = remote(ref.at[:, k], ref.at[:, k], core_send.at[w], core_recv.at[w], partner)
        copy.start()
        core_copies.append(copy)

    halves = [pl.ds(t * LANES, LANES) for t in range(H // LANES)]
    x1_copies[0].wait_recv()
    own_low = own_piece(chunk(xl, 0), 1)
    for cols in halves:
        acc[pl.ds(H, H), cols] = own_low(cols) + decode_piece(x1_in.at[0], cols)
    for j in (1, 2, 3):
        y1_copies[1, j].wait_recv()
    own_high = y1_sum(1, own_piece(chunk(xl, 0), 0))
    for cols in halves:
        acc[pl.ds(0, H), cols] = own_high(cols)
    x2_copy.wait_recv()
    for j in (1, 2, 3):
        y2_copies[j].wait_recv()
    for t, cols in enumerate(halves):
        mine = pl.ds(pl.multiple_of(k * H + t * LANES, LANES), LANES)
        top = acc[pl.ds(0, H), cols] + decode_piece(x2_in, cols)
        high, low = split(top)
        ghigh[pl.ds(0, H), mine] = high
        glow[pl.ds(0, H), mine] = low
        bottom = acc[pl.ds(H, H), cols]
        for j in (1, 2, 3):
            bottom = bottom + decode_piece(y2_in.at[j - 1], cols)
        high, low = split(bottom)
        ghigh[pl.ds(H, H), mine] = high
        glow[pl.ds(H, H), mine] = low

    strip = pl.ds(pl.multiple_of(k * H, H), H)
    for w, ref in enumerate((ghigh, glow)):
        copy = remote(ref.at[:, strip], ref.at[:, strip], core_send.at[2 + w], core_recv.at[2 + w], partner)
        copy.start()
        core_copies.append(copy)
    core_copies[2].wait()
    core_copies[3].wait()

    def rows_for(there):
        return pl.ds(pl.multiple_of(there * 2 * S + k * S, S), S)

    row_copies = []
    for i, (a, b) in enumerate(PEERS + [(0, 0)]):
        there = chip_at(a, b)
        rows = rows_for(there)
        value = ghigh[rows, :].astype(F32) + glow[rows, :].astype(F32)
        if (a, b) == (0, 0):
            encode_rows(value, grow_in.at[c])
        else:
            encode_rows(value, grow_out.at[i])
            copy = remote(grow_out.at[i], grow_in.at[c], row_send.at[0, i], row_recv.at[0, i], along_mp(a, b))
            copy.start()
            row_copies.append(copy)

    high_rows = jnp.concatenate([ghigh[rows_for(t), :] for t in range(NB)], axis=0)
    low_rows = jnp.concatenate([glow[rows_for(t), :] for t in range(NB)], axis=0)
    nt = ((1,), (1,))
    product = dot(high_rows, ghigh[...], nt) + (dot(high_rows, glow[...], nt) + dot(low_rows, ghigh[...], nt))
    precond[...] = product.reshape(NB * S, B)
    prod_copies = []

    def send_products(w, read):
        for i, (a, b) in enumerate(PEERS + [(0, 0)]):
            value = read(chip_at(a, b))
            if (a, b) == (0, 0):
                encode_rows(value, prod_in.at[w, c])
            else:
                encode_rows(value, prod_out.at[w, i])
                copy = remote(
                    prod_out.at[w, i], prod_in.at[w, c], row_send.at[1 + w, i], row_recv.at[1 + w, i], along_mp(a, b)
                )
                copy.start()
                prod_copies.append(copy)

    send_products(0, lambda there: precond[pl.ds(pl.multiple_of(there * S, S), S), :])
    tn = ((0,), (0,))
    pright[...] = dot(ghigh[...], ghigh[...], tn) + (
        dot(ghigh[...], glow[...], tn) + dot(glow[...], ghigh[...], tn)
    )
    send_products(1, lambda there: pright[rows_for(there), :])

    core_copies[0].wait()
    core_copies[1].wait()
    rcols = jnp.concatenate(
        [rroot[a, b, :, strip] for a in range(NB) for b in range(2)], axis=0
    )
    inner = dot(ghigh[...], rcols) + dot(glow[...], rcols)
    inner_high, inner_low = split(inner)
    lrows = lroot[...].reshape(B, B)
    applied = dot(lrows, inner_high) + dot(lrows, inner_low)
    pright[:, pl.ds(0, H)] = applied
    pair_out[1] = fold(applied * applied)

    for i in (2, 1, 3, 4):
        loads[i].wait()
    for i, (a, b) in enumerate([(0, 0)] + PEERS):
        slot = chip_at(-a, -b)
        if i:
            row_copies[i - 1].wait_recv()
        total = jnp.zeros((8, LANES), F32)
        for t, grad in enumerate(decode_rows(grow_in.at[slot])):
            cols = pl.ds(t * LANES, LANES)
            mean = FIRST_DECAY * first[slot, :, cols] + (1.0 - FIRST_DECAY) * grad
            square = SECOND_DECAY * second[slot, :, cols] + (1.0 - SECOND_DECAY) * grad * grad
            new_first[slot, :, cols] = mean
            new_second[slot, :, cols] = square
            adam = mean / (jnp.sqrt(square) + ADAM_EPS)
            total = total + fold(adam * adam)
        sums_out[i] = total
    sum_copies = []
    for i, (a, b) in enumerate(PEERS):
        copy = remote(sums_out.at[i + 1], sums_in.at[i], sum_send.at[i], sum_recv.at[i], along_mp(-a, -b))
        copy.start()
        sum_copies.append(copy)

    for w, (old, new) in enumerate(((left, new_left), (right, new_right))):
        for i, (a, b) in enumerate([(0, 0)] + PEERS):
            slot = chip_at(-a, -b)
            if i:
                prod_copies[w * len(PEERS) + i - 1].wait_recv()
            for t, value in enumerate(decode_rows(prod_in.at[w, slot])):
                cols = pl.ds(t * LANES, LANES)
                new[slot, :, cols] = old[slot, :, cols] + value

    total = sums_out[0]
    for i, copy in enumerate(sum_copies):
        copy.wait_recv()
        total = total + sums_in[i]
    pair_out[0] = total
    pair_copy = remote(pair_out, pair_in, sum_send.at[len(PEERS)], sum_recv.at[len(PEERS)], partner)
    pair_copy.start()
    pair_copy.wait()
    norms = [jnp.sum(pair_out[w] + pair_in[w], axis=(0, 1), keepdims=True) for w in range(2)]
    graft = jnp.sqrt(norms[0]) / (jnp.sqrt(norms[1]) + NORM_EPS)
    update[...] = (pright[:, pl.ds(0, H)] * graft).astype(BF16)

    for copy in root_copies + row_copies + prod_copies + sum_copies:
        copy.wait_send()
    for copy in list(x1_copies.values()) + list(y1_copies.values()) + list(y2_copies.values()) + [x2_copy]:
        copy.wait_send()


def on_device(
    grad_parts, home, left_stat, right_stat, left_root, right_root, first_moment, second_moment
):
    in_hbm = pl.BlockSpec(memory_space=pltpu.HBM)
    vmem = pl.BlockSpec(memory_space=pltpu.VMEM)
    n = len(PEERS)
    piece = (H + T, H)
    rows = (S * B // LANES + T, LANES)
    dma = pltpu.SemaphoreType.DMA
    scratch = [
        pltpu.VMEM((NB, B, H), F32),
        *[pltpu.VMEM((NB, S, B), F32)] * 4,
        *[pltpu.VMEM((NB, 2, S, B), BF16)] * 2,
        *[pltpu.VMEM((4, *piece), I16)] * 2,
        *[pltpu.VMEM((6, *piece), I16)] * 2,
        *[pltpu.VMEM(piece, I16)] * 2,
        *[pltpu.VMEM((3, *piece), I16)] * 2,
        pltpu.VMEM((B, H), F32),
        *[pltpu.VMEM((B, B), BF16)] * 2,
        pltpu.VMEM((n, *rows), I16),
        pltpu.VMEM((NB, *rows), I16),
        pltpu.VMEM((2, n, *rows), I16),
        pltpu.VMEM((2, NB, *rows), I16),
        pltpu.VMEM((B, B), F32),
        pltpu.VMEM((H, B), F32),
        pltpu.VMEM((NB, 8, LANES), F32),
        pltpu.VMEM((n, 8, LANES), F32),
        *[pltpu.VMEM((2, 8, LANES), F32)] * 2,
        dma((7,)),
        *[dma((2, n))] * 2,
        *[dma((4,))] * 2,
        *[dma((6,))] * 2,
        *[dma((4,))] * 2,
        *[dma((4,))] * 2,
        *[dma((3, n))] * 2,
        *[dma((n + 1,))] * 2,
    ]
    rows_out = jax.ShapeDtypeStruct((NB, S, B), F32)
    return pl.pallas_call(
        kernel,
        out_shape=(rows_out,) * 4 + (jax.ShapeDtypeStruct((B, H), BF16),),
        in_specs=[pl.BlockSpec(memory_space=pltpu.SMEM)] + [in_hbm] * 7,
        out_specs=[vmem] * 5,
        scratch_shapes=scratch,
        compiler_params=pltpu.CompilerParams(
            collective_id=0, has_side_effects=True, vmem_limit_bytes=48 * 2**20
        ),
        cost_estimate=pl.CostEstimate(flops=2 * 10**9, bytes_accessed=9 * 2**20, transcendentals=0),
        name="shampoo_step",
    )(
        home, grad_parts.reshape(NB, B, H), left_stat, right_stat, left_root, right_root, first_moment, second_moment
    )


def solution(mesh):
    rows = P("dp", "mp", None)
    in_specs = (P("dp", None, "mp"), P(), rows, rows, rows, rows, rows, rows)
    out_specs = (rows, rows, rows, rows, P("dp", "mp"))
    return jax.shard_map(
        on_device, mesh=mesh, in_specs=in_specs, out_specs=out_specs, check_vma=False
    )
```

```python
import functools
import math

import jax
import jax.numpy as jnp
from jax import lax
from jax.experimental import pallas as pl
from jax.experimental.pallas import tpu as pltpu
from jax.sharding import PartitionSpec as P

FIRST_DECAY = 0.9
SECOND_DECAY = 0.999
ADAM_EPS = 1e-08
NORM_EPS = 1e-06
MESH = pl.DeviceIdType.MESH
F32 = jnp.float32
BF16 = jnp.bfloat16
I16 = jnp.int16
I32 = jnp.int32

B = 512
H = 256
S = 32
T = 16
LANES = 128
NB = 8
NY = 4
FULL = 32760.0
STEP = math.log(2.0) / 4.0
TINY = 1e-30

PEERS = [(a, b) for a in range(2) for b in range(4) if (a, b) != (0, 0)]


def code_of(peak):
    return jnp.ceil(jnp.log(jnp.maximum(peak, TINY)) * (1.0 / STEP))


def coded(x, code):
    return jnp.floor(x * (jnp.exp(code * -STEP) * FULL) + 0.5).astype(I32).astype(I16)


def scale_of(code):
    return jnp.exp(code.astype(I32).astype(F32) * STEP) * (1.0 / FULL)


def decoded(values, scale):
    return values.astype(I32).astype(F32) * scale


def encode_piece(read, out):
    for t in range(H // LANES):
        cols = pl.ds(t * LANES, LANES)
        x = read(cols).reshape(H // T, T, LANES)
        code = code_of(jnp.max(jnp.abs(x), axis=0))
        out[pl.ds(0, H), cols] = coded(x, code[None]).reshape(H, LANES)
        out[pl.ds(H, T), cols] = code.astype(I32).astype(I16)


def decode_piece(codes, cols):
    scale = scale_of(codes[pl.ds(H, T), cols])
    values = codes[pl.ds(0, H), cols].reshape(H // T, T, LANES)
    return decoded(values, scale[None]).reshape(H, LANES)


def encode_rows(x, out):
    n = B // LANES
    parts = [x[:, t * LANES : (t + 1) * LANES].reshape(S // T, T, LANES) for t in range(n)]
    peak = functools.reduce(jnp.maximum, [jnp.max(jnp.abs(p), axis=0) for p in parts])
    code = code_of(peak)
    for t in range(n):
        out[pl.ds(t * S, S), :] = coded(parts[t], code[None]).reshape(S, LANES)
    out[pl.ds(n * S, T), :] = code.astype(I32).astype(I16)


def decode_rows(codes):
    n = B // LANES
    scale = scale_of(codes[pl.ds(n * S, T), :])
    return [
        decoded(codes[pl.ds(t * S, S), :].reshape(S // T, T, LANES), scale[None]).reshape(S, LANES)
        for t in range(n)
    ]


def dot(a, b, dims=((1,), (0,))):
    return lax.dot_general(a, b, (dims, ((), ())), preferred_element_type=F32)


def split(x):
    high = x.astype(BF16)
    return high, (x - high.astype(F32)).astype(BF16)


def fold(x):
    r, c = x.shape
    x = jnp.sum(x.reshape(r // 8, 8, c), axis=0)
    return functools.reduce(jnp.add, [x[:, t * LANES : (t + 1) * LANES] for t in range(c // LANES)])


def kernel(
    home, part_hbm, left_hbm, right_hbm, lroot_hbm, rroot_hbm, first_hbm, second_hbm,
    new_left_hbm, new_right_hbm, new_first_hbm, new_second_hbm, update_hbm,
    new_left, new_right, new_first, new_second, update, part, left, right, first, second, lroot, rroot,
    x1_out, x1_in, y1_out, y1_in, x2_out, x2_in, y2_out, y2_in,
    acc, ghigh, glow, grow_out, grow_in, prod_out, prod_in, pright, precond,
    sums_out, sums_in, pair_out, pair_in,
    load_sem, root_send, root_recv, x1_send, x1_recv, y1_send, y1_recv, s2_send, s2_recv,
    core_send, core_recv, row_send, row_recv, sum_send, sum_recv, store_sem,
):
    d = lax.axis_index("dp")
    m = lax.axis_index("mp")
    xl, y = d // NY, d % NY
    xh, z, k = m // 8, (m // 2) % 4, m % 2
    c = m // 2

    partner = (d, m + 1 - 2 * k)
    across = ((1 - xl) * NY + y, m)

    def along_y(j):
        return (xl * NY + (y + j) % NY, m)

    def chip_at(a, b):
        return ((xh + a) % 2) * 4 + (z + b) % 4

    def along_mp(a, b):
        return (d, chip_at(a, b) * 2 + k)

    def remote(src, dst, send, recv, device):
        return pltpu.make_async_remote_copy(
            src_ref=src, dst_ref=dst, send_sem=send, recv_sem=recv, device_id=device, device_id_type=MESH
        )

    loads = [
        pltpu.make_async_copy(src, dst, load_sem.at[i])
        for i, (src, dst) in enumerate(
            [
                (part_hbm, part), (left_hbm, left), (right_hbm, right), (first_hbm, first), (second_hbm, second),
                (lroot_hbm.at[c], lroot.at[c, k]), (rroot_hbm.at[c], rroot.at[c, k]),
            ]
        )
    ]
    loads[0].start()

    barrier = pltpu.get_barrier_semaphore()
    greeted = [partner, across] + [along_y(j) for j in (1, 2, 3)] + [along_mp(a, b) for a, b in PEERS]
    for device in greeted:
        pl.semaphore_signal(barrier, inc=1, device_id=device, device_id_type=MESH)
    pl.semaphore_wait(barrier, len(greeted))

    root_copies = []
    for i, (a, b) in enumerate(PEERS):
        there = chip_at(a, b)
        for w, (src, dst) in enumerate(((lroot_hbm, lroot), (rroot_hbm, rroot))):
            copy = remote(src.at[there], dst.at[c, k], root_send.at[w, i], root_recv.at[w, i], along_mp(a, b))
            copy.start()
            root_copies.append(copy)
    for load in loads[1:]:
        load.start()

    def source(q):
        return functools.reduce(jnp.maximum, [jnp.where(home[r] == q, r, 0) for r in range(NB)])

    def own_piece(q, half):
        row = source(q)
        return lambda cols: part[row, pl.ds(half * H, H), cols]

    def chunk(to_x, j):
        return to_x * NY + (y + j) % NY

    loads[0].wait()
    x1_copies, y1_copies = {}, {}

    def send_x1(j):
        encode_piece(own_piece(chunk(1 - xl, j), 1), x1_out.at[j])
        x1_copies[j] = remote(x1_out.at[j], x1_in.at[j], x1_send.at[j], x1_recv.at[j], across)
        x1_copies[j].start()

    def send_y1(w, j):
        to_x = 1 - xl if w == 0 else xl
        n = w * 3 + j - 1
        encode_piece(own_piece(chunk(to_x, j), 0), y1_out.at[n])
        y1_copies[w, j] = remote(y1_out.at[n], y1_in.at[n], y1_send.at[n], y1_recv.at[n], along_y(j))
        y1_copies[w, j].start()

    for j in (1, 2, 3):
        send_x1(j)
        send_y1(0, j)
    for j in (1, 2, 3):
        send_y1(1, j)
    send_x1(0)

    y2_copies = {}
    for j in (1, 2, 3):
        x1_copies[j].wait_recv()
        own = own_piece(chunk(xl, j), 1)
        encode_piece(lambda cols: own(cols) + decode_piece(x1_in.at[j], cols), y2_out.at[j - 1])
        y2_copies[j] = remote(y2_out.at[j - 1], y2_in.at[j - 1], s2_send.at[j], s2_recv.at[j], along_y(j))
        y2_copies[j].start()

    def y1_sum(w, read):
        def total(cols):
            out = read(cols)
            for j in (1, 2, 3):
                out = out + decode_piece(y1_in.at[w * 3 + j - 1], cols)
            return out

        return total

    for j in (1, 2, 3):
        y1_copies[0, j].wait_recv()
    encode_piece(y1_sum(0, own_piece(chunk(1 - xl, 0), 0)), x2_out)
    x2_copy = remote(x2_out, x2_in, s2_send.at[0], s2_recv.at[0], across)
    x2_copy.start()

    for copy in root_copies:
        copy.wait_recv()
    loads[5].wait()
    loads[6].wait()
    core_copies = []
    for w, ref in enumerate((lroot, rroot)):
        copy = remote(ref.at[:, k], ref.at[:, k], core_send.at[w], core_recv.at[w], partner)
        copy.start()
        core_copies.append(copy)

    halves = [pl.ds(t * LANES, LANES) for t in range(H // LANES)]
    x1_copies[0].wait_recv()
    own_low = own_piece(chunk(xl, 0), 1)
    for cols in halves:
        acc[pl.ds(H, H), cols] = own_low(cols) + decode_piece(x1_in.at[0], cols)
    for j in (1, 2, 3):
        y1_copies[1, j].wait_recv()
    own_high = y1_sum(1, own_piece(chunk(xl, 0), 0))
    for cols in halves:
        acc[pl.ds(0, H), cols] = own_high(cols)
    x2_copy.wait_recv()
    for j in (1, 2, 3):
        y2_copies[j].wait_recv()
    for t, cols in enumerate(halves):
        mine = pl.ds(pl.multiple_of(k * H + t * LANES, LANES), LANES)
        top = acc[pl.ds(0, H), cols] + decode_piece(x2_in, cols)
        high, low = split(top)
        ghigh[pl.ds(0, H), mine] = high
        glow[pl.ds(0, H), mine] = low
        bottom = acc[pl.ds(H, H), cols]
        for j in (1, 2, 3):
            bottom = bottom + decode_piece(y2_in.at[j - 1], cols)
        high, low = split(bottom)
        ghigh[pl.ds(H, H), mine] = high
        glow[pl.ds(H, H), mine] = low

    strip = pl.ds(pl.multiple_of(k * H, H), H)
    for w, ref in enumerate((ghigh, glow)):
        copy = remote(ref.at[:, strip], ref.at[:, strip], core_send.at[2 + w], core_recv.at[2 + w], partner)
        copy.start()
        core_copies.append(copy)
    core_copies[2].wait()
    core_copies[3].wait()

    def rows_for(there):
        return pl.ds(pl.multiple_of(there * 2 * S + k * S, S), S)

    row_copies = []
    for i, (a, b) in enumerate(PEERS + [(0, 0)]):
        there = chip_at(a, b)
        rows = rows_for(there)
        value = ghigh[rows, :].astype(F32) + glow[rows, :].astype(F32)
        if (a, b) == (0, 0):
            encode_rows(value, grow_in.at[c])
        else:
            encode_rows(value, grow_out.at[i])
            copy = remote(grow_out.at[i], grow_in.at[c], row_send.at[0, i], row_recv.at[0, i], along_mp(a, b))
            copy.start()
            row_copies.append(copy)

    high_rows = jnp.concatenate([ghigh[rows_for(t), :] for t in range(NB)], axis=0)
    low_rows = jnp.concatenate([glow[rows_for(t), :] for t in range(NB)], axis=0)
    nt = ((1,), (1,))
    product = dot(high_rows, ghigh[...], nt) + (dot(high_rows, glow[...], nt) + dot(low_rows, ghigh[...], nt))
    precond[...] = product.reshape(NB * S, B)
    prod_copies = []

    def send_products(w, read):
        for i, (a, b) in enumerate(PEERS + [(0, 0)]):
            value = read(chip_at(a, b))
            if (a, b) == (0, 0):
                encode_rows(value, prod_in.at[w, c])
            else:
                encode_rows(value, prod_out.at[w, i])
                copy = remote(
                    prod_out.at[w, i], prod_in.at[w, c], row_send.at[1 + w, i], row_recv.at[1 + w, i], along_mp(a, b)
                )
                copy.start()
                prod_copies.append(copy)

    send_products(0, lambda there: precond[pl.ds(pl.multiple_of(there * S, S), S), :])
    tn = ((0,), (0,))
    pright[...] = dot(ghigh[...], ghigh[...], tn) + (
        dot(ghigh[...], glow[...], tn) + dot(glow[...], ghigh[...], tn)
    )
    send_products(1, lambda there: pright[rows_for(there), :])

    core_copies[0].wait()
    core_copies[1].wait()
    rcols = jnp.concatenate(
        [rroot[a, b, :, strip] for a in range(NB) for b in range(2)], axis=0
    )
    inner = dot(ghigh[...], rcols) + dot(glow[...], rcols)
    inner_high, inner_low = split(inner)
    lrows = lroot[...].reshape(B, B)
    applied = dot(lrows, inner_high) + dot(lrows, inner_low)
    pright[:, pl.ds(0, H)] = applied
    pair_out[1] = fold(applied * applied)

    for i in (2, 1, 3, 4):
        loads[i].wait()
    for i, (a, b) in enumerate([(0, 0)] + PEERS):
        slot = chip_at(-a, -b)
        if i:
            row_copies[i - 1].wait_recv()
        total = jnp.zeros((8, LANES), F32)
        for t, grad in enumerate(decode_rows(grow_in.at[slot])):
            cols = pl.ds(t * LANES, LANES)
            mean = FIRST_DECAY * first[slot, :, cols] + (1.0 - FIRST_DECAY) * grad
            square = SECOND_DECAY * second[slot, :, cols] + (1.0 - SECOND_DECAY) * grad * grad
            new_first[slot, :, cols] = mean
            new_second[slot, :, cols] = square
            adam = mean / (jnp.sqrt(square) + ADAM_EPS)
            total = total + fold(adam * adam)
        sums_out[i] = total
    stores = [
        pltpu.make_async_copy(src, dst, store_sem.at[i])
        for i, (src, dst) in enumerate(
            [
                (new_first, new_first_hbm), (new_second, new_second_hbm), (new_left, new_left_hbm),
                (new_right, new_right_hbm), (update, update_hbm),
            ]
        )
    ]
    stores[0].start()
    stores[1].start()
    sum_copies = []
    for i, (a, b) in enumerate(PEERS):
        copy = remote(sums_out.at[i + 1], sums_in.at[i], sum_send.at[i], sum_recv.at[i], along_mp(-a, -b))
        copy.start()
        sum_copies.append(copy)

    for w, (old, new) in enumerate(((left, new_left), (right, new_right))):
        for i, (a, b) in enumerate([(0, 0)] + PEERS):
            slot = chip_at(-a, -b)
            if i:
                prod_copies[w * len(PEERS) + i - 1].wait_recv()
            for t, value in enumerate(decode_rows(prod_in.at[w, slot])):
                cols = pl.ds(t * LANES, LANES)
                new[slot, :, cols] = old[slot, :, cols] + value
        stores[2 + w].start()

    total = sums_out[0]
    for i, copy in enumerate(sum_copies):
        copy.wait_recv()
        total = total + sums_in[i]
    pair_out[0] = total
    pair_copy = remote(pair_out, pair_in, sum_send.at[len(PEERS)], sum_recv.at[len(PEERS)], partner)
    pair_copy.start()
    pair_copy.wait()
    norms = [jnp.sum(pair_out[w] + pair_in[w], axis=(0, 1), keepdims=True) for w in range(2)]
    graft = jnp.sqrt(norms[0]) / (jnp.sqrt(norms[1]) + NORM_EPS)
    update[...] = (pright[:, pl.ds(0, H)] * graft).astype(BF16)
    stores[4].start()

    for copy in root_copies + row_copies + prod_copies + sum_copies:
        copy.wait_send()
    for copy in list(x1_copies.values()) + list(y1_copies.values()) + list(y2_copies.values()) + [x2_copy]:
        copy.wait_send()
    for store in stores:
        store.wait()


def place(*refs):
    sem = refs[-1]
    n = len(refs) // 2
    copies = [pltpu.make_async_copy(refs[i], refs[n + i], sem.at[i]) for i in range(n)]
    for copy in copies:
        copy.start()
    for copy in copies:
        copy.wait()


def on_device(
    grad_parts, home, left_stat, right_stat, left_root, right_root, first_moment, second_moment
):
    in_hbm = pl.BlockSpec(memory_space=pltpu.HBM)
    n = len(PEERS)
    piece = (H + T, H)
    rows = (S * B // LANES + T, LANES)
    dma = pltpu.SemaphoreType.DMA
    scratch = [
        *[pltpu.VMEM((NB, S, B), F32)] * 4,
        pltpu.VMEM((B, H), BF16),
        pltpu.VMEM((NB, B, H), F32),
        *[pltpu.VMEM((NB, S, B), F32)] * 4,
        *[pltpu.VMEM((NB, 2, S, B), BF16)] * 2,
        *[pltpu.VMEM((4, *piece), I16)] * 2,
        *[pltpu.VMEM((6, *piece), I16)] * 2,
        *[pltpu.VMEM(piece, I16)] * 2,
        *[pltpu.VMEM((3, *piece), I16)] * 2,
        pltpu.VMEM((B, H), F32),
        *[pltpu.VMEM((B, B), BF16)] * 2,
        pltpu.VMEM((n, *rows), I16),
        pltpu.VMEM((NB, *rows), I16),
        pltpu.VMEM((2, n, *rows), I16),
        pltpu.VMEM((2, NB, *rows), I16),
        pltpu.VMEM((B, B), F32),
        pltpu.VMEM((H, B), F32),
        pltpu.VMEM((NB, 8, LANES), F32),
        pltpu.VMEM((n, 8, LANES), F32),
        *[pltpu.VMEM((2, 8, LANES), F32)] * 2,
        dma((7,)),
        *[dma((2, n))] * 2,
        *[dma((4,))] * 2,
        *[dma((6,))] * 2,
        *[dma((4,))] * 2,
        *[dma((4,))] * 2,
        *[dma((3, n))] * 2,
        *[dma((n + 1,))] * 2,
        dma((5,)),
    ]
    rows_out = jax.ShapeDtypeStruct((NB, S, B), F32)
    out_shape = (rows_out,) * 4 + (jax.ShapeDtypeStruct((B, H), BF16),)
    made = pl.pallas_call(
        kernel,
        out_shape=out_shape,
        in_specs=[pl.BlockSpec(memory_space=pltpu.SMEM)] + [in_hbm] * 7,
        out_specs=[in_hbm] * 5,
        scratch_shapes=scratch,
        compiler_params=pltpu.CompilerParams(
            collective_id=0, has_side_effects=True, vmem_limit_bytes=58 * 2**20
        ),
        cost_estimate=pl.CostEstimate(flops=2 * 10**9, bytes_accessed=9 * 2**20, transcendentals=0),
        name="shampoo_step",
    )(
        home, grad_parts.reshape(NB, B, H), left_stat, right_stat, left_root, right_root, first_moment, second_moment
    )
    return pl.pallas_call(
        place,
        out_shape=out_shape,
        in_specs=[in_hbm] * 5,
        out_specs=[in_hbm] * 5,
        scratch_shapes=[dma((5,))],
        compiler_params=pltpu.CompilerParams(vmem_limit_bytes=58 * 2**20),
        name="place_outputs",
    )(*made)


def solution(mesh):
    rows = P("dp", "mp", None)
    in_specs = (P("dp", None, "mp"), P(), rows, rows, rows, rows, rows, rows)
    out_specs = (rows, rows, rows, rows, P("dp", "mp"))
    return jax.shard_map(
        on_device, mesh=mesh, in_specs=in_specs, out_specs=out_specs, check_vma=False
    )
```

```python
import functools
import math

import jax
import jax.numpy as jnp
from jax import lax
from jax.experimental import pallas as pl
from jax.experimental.pallas import tpu as pltpu
from jax.sharding import PartitionSpec as P

FIRST_DECAY = 0.9
SECOND_DECAY = 0.999
ADAM_EPS = 1e-08
NORM_EPS = 1e-06
MESH = pl.DeviceIdType.MESH
F32 = jnp.float32
BF16 = jnp.bfloat16
I16 = jnp.int16
I32 = jnp.int32

B = 512
H = 256
XROWS = 192
YROWS = B - XROWS
S = 32
T = 16
STRIDE = 64
LANES = 128
WIDE = B // LANES * S
NB = 8
NY = 4
FULL = 32760.0
STEP = math.log(2.0) / 4.0
TINY = 1e-30

PEERS = [(a, b) for a in range(2) for b in range(4) if (a, b) != (0, 0)]


def code_of(peak):
    return jnp.ceil(jnp.log(jnp.maximum(peak, TINY)) * (1.0 / STEP))


def coded(x):
    return jnp.floor(x + 0.5).astype(I32).astype(I16)


def scale_of(code):
    return jnp.exp(code.astype(I32).astype(F32) * STEP) * (1.0 / FULL)


def decoded(values, scale):
    return values.astype(I32).astype(F32) * scale


def encode_piece(n, read, out, keep=None):
    tiles = range(H // LANES)

    def look(i, peak):
        r = pl.multiple_of(i * STRIDE, STRIDE)
        for t in tiles:
            x = read(t, r)
            if keep is not None:
                keep[pl.ds(r, STRIDE), pl.ds(t * LANES, LANES)] = x
            peak = jnp.maximum(peak, jnp.max(jnp.abs(x).reshape(STRIDE // T, T, LANES), axis=0))
        return peak

    code = code_of(lax.fori_loop(0, n // STRIDE, look, jnp.zeros((T, LANES), F32)))
    factor = jnp.exp(code * -STEP) * FULL

    def write(i, carry):
        r = pl.multiple_of(i * STRIDE, STRIDE)
        for t in tiles:
            x = read(t, r) if keep is None else keep[pl.ds(r, STRIDE), pl.ds(t * LANES, LANES)]
            x = x.reshape(STRIDE // T, T, LANES) * factor[None]
            out[pl.ds(t * n + r, STRIDE), :] = coded(x).reshape(STRIDE, LANES)
        return carry

    lax.fori_loop(0, n // STRIDE, write, 0)
    out[pl.ds(H // LANES * n, T), :] = code.astype(I32).astype(I16)


def sum_of(n, own, arrived):
    scales = [scale_of(ref[pl.ds(H // LANES * n, T), :])[None] for ref in arrived]

    def read(t, r):
        x = own(t, r)
        for ref, scale in zip(arrived, scales):
            values = ref[pl.ds(t * n + r, STRIDE), :].reshape(STRIDE // T, T, LANES)
            x = x + decoded(values, scale).reshape(STRIDE, LANES)
        return x

    return read


def encode_rows(x, group, out, first):
    n = B // LANES
    parts = [x[:, t * LANES : (t + 1) * LANES].reshape(S // group, group, LANES) for t in range(n)]
    code = code_of(functools.reduce(jnp.maximum, [jnp.max(jnp.abs(p), axis=0) for p in parts]))
    factor = jnp.exp(code * -STEP) * FULL
    for t in range(n):
        out[pl.ds(first + t * S, S), :] = coded(parts[t] * factor[None]).reshape(S, LANES)
    return code


def decode_rows(codes, first, scale):
    group = scale.shape[0]
    return [
        decoded(codes[pl.ds(first + t * S, S), :].reshape(S // group, group, LANES), scale[None]).reshape(S, LANES)
        for t in range(B // LANES)
    ]


def dot(a, b, dims=((1,), (0,))):
    return lax.dot_general(a, b, (dims, ((), ())), preferred_element_type=F32)


def split(x):
    high = x.astype(BF16)
    return high, (x - high.astype(F32)).astype(BF16)


def fold(x):
    r, c = x.shape
    x = jnp.sum(x.reshape(r // 8, 8, c), axis=0)
    return functools.reduce(jnp.add, [x[:, t * LANES : (t + 1) * LANES] for t in range(c // LANES)])


def kernel(
    home_hbm, part_hbm, lroot_hbm, rroot_hbm, first_hbm, second_hbm,
    prod_in, new_first_hbm, new_second_hbm, update_hbm,
    home, part, first, second, new_first, new_second, update, lroot, rroot,
    x1_out, x1_in, y1_out, y1_in, x2_out, x2_in, y2_out, y2_in,
    work, ghigh, glow, grow_out, grow_in, prod_out, left_codes, pleft, pright,
    sums_out, sums_in, pair_out, pair_in,
    load_sem, root_send, root_recv, x1_send, x1_recv, y1_send, y1_recv, s2_send, s2_recv,
    core_send, core_recv, row_send, row_recv, sum_send, sum_recv, store_sem,
):
    d = lax.axis_index("dp")
    m = lax.axis_index("mp")
    xl, y = d // NY, d % NY
    xh, z, k = m // 8, (m // 2) % 4, m % 2
    c = m // 2

    partner = (d, m + 1 - 2 * k)
    across = ((1 - xl) * NY + y, m)

    def along_y(j):
        return (xl * NY + (y + j) % NY, m)

    def chip_at(a, b):
        return ((xh + a) % 2) * 4 + (z + b) % 4

    def along_mp(a, b):
        return (d, chip_at(a, b) * 2 + k)

    def remote(src, dst, send, recv, device):
        return pltpu.make_async_remote_copy(
            src_ref=src, dst_ref=dst, send_sem=send, recv_sem=recv, device_id=device, device_id_type=MESH
        )

    loads = [
        pltpu.make_async_copy(src, dst, load_sem.at[i])
        for i, (src, dst) in enumerate(
            [
                (home_hbm, home), (part_hbm, part), (first_hbm, first), (second_hbm, second),
                (lroot_hbm.at[c], lroot.at[c, k]), (rroot_hbm.at[c], rroot.at[c, k]),
            ]
        )
    ]
    loads[0].start()
    loads[1].start()

    barrier = pltpu.get_barrier_semaphore()
    greeted = [partner, across] + [along_y(j) for j in (1, 2, 3)] + [along_mp(a, b) for a, b in PEERS]
    for device in greeted:
        pl.semaphore_signal(barrier, inc=1, device_id=device, device_id_type=MESH)
    pl.semaphore_wait(barrier, len(greeted))

    root_copies = []
    for i, (a, b) in enumerate(PEERS):
        there = chip_at(a, b)
        for w, (src, dst) in enumerate(((lroot_hbm, lroot), (rroot_hbm, rroot))):
            copy = remote(src.at[there], dst.at[c, k], root_send.at[w, i], root_recv.at[w, i], along_mp(a, b))
            copy.start()
            root_copies.append(copy)
    for load in loads[2:]:
        load.start()

    def source(q):
        return functools.reduce(jnp.maximum, [jnp.where(home[r] == q, r, 0) for r in range(NB)])

    def own_piece(to_x, j, start):
        row = source(to_x * NY + (y + j) % NY)
        return lambda t, r: part[row, pl.ds(start + r, STRIDE), pl.ds(t * LANES, LANES)]

    loads[0].wait()
    loads[1].wait()
    x1_copies, y1_copies = {}, {}

    def send_x1(j):
        encode_piece(XROWS, own_piece(1 - xl, j, YROWS), x1_out.at[j])
        x1_copies[j] = remote(x1_out.at[j], x1_in.at[j], x1_send.at[j], x1_recv.at[j], across)
        x1_copies[j].start()

    def send_y1(w, j):
        n = w * 3 + j - 1
        encode_piece(YROWS, own_piece(1 - xl if w == 0 else xl, j, 0), y1_out.at[n])
        y1_copies[w, j] = remote(y1_out.at[n], y1_in.at[n], y1_send.at[n], y1_recv.at[n], along_y(j))
        y1_copies[w, j].start()

    for j in (1, 3, 2):
        send_y1(0, j)
        send_x1(j)
    for j in (1, 3, 2):
        send_y1(1, j)
    send_x1(0)

    y2_copies = {}
    for j in (1, 3, 2):
        x1_copies[j].wait_recv()
        read = sum_of(XROWS, own_piece(xl, j, YROWS), [x1_in.at[j]])
        encode_piece(XROWS, read, y2_out.at[j - 1], work)
        y2_copies[j] = remote(y2_out.at[j - 1], y2_in.at[j - 1], s2_send.at[j], s2_recv.at[j], along_y(j))
        y2_copies[j].start()

    for j in (1, 2, 3):
        y1_copies[0, j].wait_recv()
    read = sum_of(YROWS, own_piece(1 - xl, 0, 0), [y1_in.at[n] for n in range(3)])
    encode_piece(YROWS, read, x2_out, work)
    x2_copy = remote(x2_out, x2_in, s2_send.at[0], s2_recv.at[0], across)
    x2_copy.start()

    for copy in root_copies:
        copy.wait_recv()
    loads[4].wait()
    loads[5].wait()
    core_copies = []
    for w, ref in enumerate((lroot, rroot)):
        copy = remote(ref.at[:, k], ref.at[:, k], core_send.at[w], core_recv.at[w], partner)
        copy.start()
        core_copies.append(copy)

    strip = pl.ds(pl.multiple_of(k * H, H), H)
    block_copies = []

    def finish(n, start, read, w):
        def step(i, carry):
            r = pl.multiple_of(i * STRIDE, STRIDE)
            for t in range(H // LANES):
                mine = pl.ds(pl.multiple_of(k * H + t * LANES, LANES), LANES)
                high, low = split(read(t, r))
                ghigh[pl.ds(start + r, STRIDE), mine] = high
                glow[pl.ds(start + r, STRIDE), mine] = low
            return carry

        lax.fori_loop(0, n // STRIDE, step, 0)
        for i, ref in enumerate((ghigh, glow)):
            here = ref.at[pl.ds(start, n), strip]
            copy = remote(here, here, core_send.at[2 + 2 * w + i], core_recv.at[2 + 2 * w + i], partner)
            copy.start()
            block_copies.append(copy)

    x1_copies[0].wait_recv()
    for j in (1, 3, 2):
        y2_copies[j].wait_recv()
    arrived = [x1_in.at[0]] + [y2_in.at[n] for n in range(3)]
    finish(XROWS, YROWS, sum_of(XROWS, own_piece(xl, 0, YROWS), arrived), 0)
    for j in (1, 2, 3):
        y1_copies[1, j].wait_recv()
    x2_copy.wait_recv()
    arrived = [y1_in.at[n] for n in range(3, 6)] + [x2_in]
    finish(YROWS, 0, sum_of(YROWS, own_piece(xl, 0, 0), arrived), 1)

    for copy in block_copies:
        copy.wait_recv()

    def rows_for(there):
        return pl.ds(pl.multiple_of(there * 2 * S + k * S, S), S)

    row_copies = []
    for i, (a, b) in enumerate(PEERS + [(0, 0)]):
        rows = rows_for(chip_at(a, b))
        value = ghigh[rows, :].astype(F32) + glow[rows, :].astype(F32)
        out = grow_out.at[i] if a or b else grow_in.at[c]
        out[pl.ds(WIDE, T), :] = encode_rows(value, T, out, 0).astype(I32).astype(I16)
        if a or b:
            copy = remote(out, grow_in.at[c], row_send.at[0, i], row_recv.at[0, i], along_mp(a, b))
            copy.start()
            row_copies.append(copy)

    high_rows = jnp.concatenate([ghigh[rows_for(t), :] for t in range(NB)], axis=0)
    low_rows = jnp.concatenate([glow[rows_for(t), :] for t in range(NB)], axis=0)
    nt = ((1,), (1,))
    pleft[...] = dot(high_rows, ghigh[...], nt) + (dot(high_rows, glow[...], nt) + dot(low_rows, ghigh[...], nt))
    prod_copies = []

    def send_products(w, i, first, size):
        a, b = (PEERS + [(0, 0)])[i]
        here, there = prod_out.at[i, pl.ds(first, size)], prod_in.at[c, pl.ds(first, size)]
        if a or b:
            copy = remote(here, there, row_send.at[1 + w, i], row_recv.at[1 + w, i], along_mp(a, b))
            prod_copies.append(copy)
        else:
            copy = pltpu.make_async_copy(here, there, store_sem.at[3 + w])
            stores.append(copy)
        copy.start()

    stores = []
    for i, (a, b) in enumerate(PEERS + [(0, 0)]):
        value = pleft[pl.ds(pl.multiple_of(chip_at(a, b) * S, S), S), :]
        left_codes[i] = encode_rows(value, T // 2, prod_out.at[i], 0)
        send_products(0, i, 0, WIDE)
    tn = ((0,), (0,))
    pright[...] = dot(ghigh[...], ghigh[...], tn) + (
        dot(ghigh[...], glow[...], tn) + dot(glow[...], ghigh[...], tn)
    )
    for i, (a, b) in enumerate(PEERS + [(0, 0)]):
        code = encode_rows(pright[rows_for(chip_at(a, b)), :], T // 2, prod_out.at[i], WIDE)
        codes = jnp.concatenate([left_codes[i], code], axis=0)
        prod_out[i, pl.ds(2 * WIDE, T), :] = codes.astype(I32).astype(I16)
        send_products(1, i, WIDE, WIDE + T)

    for copy in core_copies:
        copy.wait_recv()
    rcols = jnp.concatenate([rroot[a, b, :, strip] for a in range(NB) for b in range(2)], axis=0)
    inner = dot(ghigh[...], rcols) + dot(glow[...], rcols)
    inner_high, inner_low = split(inner)
    lrows = lroot[...].reshape(B, B)
    applied = dot(lrows, inner_high) + dot(lrows, inner_low)
    pright[:, pl.ds(0, H)] = applied
    pair_out[1] = fold(applied * applied)

    loads[2].wait()
    loads[3].wait()
    sum_copies = []
    for i, (a, b) in enumerate(PEERS + [(0, 0)]):
        slot = chip_at(-a, -b)
        if a or b:
            row_copies[i].wait_recv()
        total = jnp.zeros((8, LANES), F32)
        scale = scale_of(grow_in[slot, pl.ds(WIDE, T), :])
        for t, grad in enumerate(decode_rows(grow_in.at[slot], 0, scale)):
            cols = pl.ds(t * LANES, LANES)
            mean = FIRST_DECAY * first[slot, :, cols] + (1.0 - FIRST_DECAY) * grad
            square = SECOND_DECAY * second[slot, :, cols] + (1.0 - SECOND_DECAY) * grad * grad
            new_first[slot, :, cols] = mean
            new_second[slot, :, cols] = square
            adam = mean / (jnp.sqrt(square) + ADAM_EPS)
            total = total + fold(adam * adam)
        sums_out[i] = total
        if a or b:
            copy = remote(sums_out.at[i], sums_in.at[i], sum_send.at[i], sum_recv.at[i], along_mp(-a, -b))
            copy.start()
            sum_copies.append(copy)
    moment_stores = [
        pltpu.make_async_copy(new_first, new_first_hbm, store_sem.at[0]),
        pltpu.make_async_copy(new_second, new_second_hbm, store_sem.at[1]),
    ]
    for store in moment_stores:
        store.start()

    total = sums_out[len(PEERS)]
    for i, copy in enumerate(sum_copies):
        copy.wait_recv()
        total = total + sums_in[i]
    pair_out[0] = total
    pair_copy = remote(pair_out, pair_in, sum_send.at[len(PEERS)], sum_recv.at[len(PEERS)], partner)
    pair_copy.start()
    pair_copy.wait_recv()
    norms = [jnp.sum(pair_out[w] + pair_in[w], axis=(0, 1), keepdims=True) for w in range(2)]
    graft = jnp.sqrt(norms[0]) / (jnp.sqrt(norms[1]) + NORM_EPS)
    update[...] = (pright[:, pl.ds(0, H)] * graft).astype(BF16)
    update_store = pltpu.make_async_copy(update, update_hbm, store_sem.at[2])
    update_store.start()

    for copy in prod_copies:
        copy.wait_recv()
    sent = [x2_copy, pair_copy] + root_copies + core_copies + block_copies + row_copies + prod_copies + sum_copies
    for copy in sent + list(x1_copies.values()) + list(y1_copies.values()) + list(y2_copies.values()):
        copy.wait_send()
    for store in stores + moment_stores + [update_store]:
        store.wait()


def finish_kernel(
    prod_hbm, left_hbm, right_hbm, made_first, made_second, made_update,
    left_out, right_out, first_out, second_out, update_out,
    prod, left, right, first, second, update, load_sem, store_sem,
):
    through = [(made_first, first, first_out), (made_second, second, second_out), (made_update, update, update_out)]
    stats = [(left_hbm, left, left_out), (right_hbm, right, right_out)]
    loads = [pltpu.make_async_copy(prod_hbm, prod, load_sem.at[0])]
    for i, (src, dst, _) in enumerate(stats + through):
        loads.append(pltpu.make_async_copy(src, dst, load_sem.at[1 + i]))
    stores = [pltpu.make_async_copy(src, dst, store_sem.at[i]) for i, (_, src, dst) in enumerate(stats + through)]
    for load in loads:
        load.start()
    loads[0].wait()
    for w, ref in enumerate((left, right)):
        loads[1 + w].wait()

        def add(slot, carry):
            code = prod[slot, pl.ds(2 * WIDE, T), :].astype(F32)[w * (T // 2) : (w + 1) * (T // 2)]
            for t, value in enumerate(decode_rows(prod.at[slot], w * WIDE, jnp.exp(code * STEP) * (1.0 / FULL))):
                ref[slot, :, pl.ds(t * LANES, LANES)] += value
            return carry

        lax.fori_loop(0, NB, add, 0)
        stores[w].start()
    for i in range(len(through)):
        loads[3 + i].wait()
        stores[2 + i].start()
    for store in stores:
        store.wait()


def on_device(
    grad_parts, home, left_stat, right_stat, left_root, right_root, first_moment, second_moment
):
    in_hbm = pl.BlockSpec(memory_space=pltpu.HBM)
    n = len(PEERS)
    xpiece = (H // LANES * XROWS + T, LANES)
    ypiece = (H // LANES * YROWS + T, LANES)
    rows = (WIDE + T, LANES)
    products = (2 * WIDE + T, LANES)
    stat = pltpu.VMEM((NB, S, B), F32)
    tile = pltpu.VMEM((B, H), BF16)
    dma = pltpu.SemaphoreType.DMA
    scratch = [
        pltpu.SMEM((NB,), I32),
        pltpu.VMEM((NB, B, H), F32),
        *[stat] * 4,
        tile,
        *[pltpu.VMEM((NB, 2, S, B), BF16)] * 2,
        *[pltpu.VMEM((4, *xpiece), I16)] * 2,
        *[pltpu.VMEM((6, *ypiece), I16)] * 2,
        *[pltpu.VMEM(ypiece, I16)] * 2,
        *[pltpu.VMEM((3, *xpiece), I16)] * 2,
        pltpu.VMEM((B, H), F32),
        *[pltpu.VMEM((B, B), BF16)] * 2,
        pltpu.VMEM((n, *rows), I16),
        pltpu.VMEM((NB, *rows), I16),
        pltpu.VMEM((NB, *products), I16),
        pltpu.VMEM((NB, T // 2, LANES), F32),
        pltpu.VMEM((H, B), F32),
        pltpu.VMEM((B, B), F32),
        pltpu.VMEM((NB, 8, LANES), F32),
        pltpu.VMEM((n, 8, LANES), F32),
        *[pltpu.VMEM((2, 8, LANES), F32)] * 2,
        dma((6,)),
        *[dma((2, n))] * 2,
        *[dma((4,))] * 2,
        *[dma((6,))] * 2,
        *[dma((4,))] * 2,
        *[dma((6,))] * 2,
        *[dma((3, n))] * 2,
        *[dma((n + 1,))] * 2,
        dma((5,)),
    ]
    stat_out = jax.ShapeDtypeStruct((NB, S, B), F32)
    tile_out = jax.ShapeDtypeStruct((B, H), BF16)
    made = pl.pallas_call(
        kernel,
        out_shape=(jax.ShapeDtypeStruct((NB, *products), I16), stat_out, stat_out, tile_out),
        in_specs=[in_hbm] * 6,
        out_specs=[in_hbm] * 4,
        scratch_shapes=scratch,
        compiler_params=pltpu.CompilerParams(
            collective_id=0, has_side_effects=True, vmem_limit_bytes=58 * 2**20
        ),
        cost_estimate=pl.CostEstimate(flops=2 * 10**9, bytes_accessed=9 * 2**20, transcendentals=0),
        name="shampoo_step",
    )(home, grad_parts.reshape(NB, B, H), left_root, right_root, first_moment, second_moment)
    return pl.pallas_call(
        finish_kernel,
        out_shape=(stat_out,) * 4 + (tile_out,),
        in_specs=[in_hbm] * 6,
        out_specs=[in_hbm] * 5,
        scratch_shapes=[pltpu.VMEM((NB, *products), I16), *[stat] * 4, tile, dma((6,)), dma((5,))],
        compiler_params=pltpu.CompilerParams(vmem_limit_bytes=58 * 2**20),
        name="finish_outputs",
    )(made[0], left_stat, right_stat, *made[1:])


def solution(mesh):
    rows = P("dp", "mp", None)
    in_specs = (P("dp", None, "mp"), P(), rows, rows, rows, rows, rows, rows)
    out_specs = (rows, rows, rows, rows, P("dp", "mp"))
    return jax.shard_map(
        on_device, mesh=mesh, in_specs=in_specs, out_specs=out_specs, check_vma=False
    )
```

```python
import functools
import math

import jax
import jax.numpy as jnp
from jax import lax
from jax.experimental import pallas as pl
from jax.experimental.pallas import tpu as pltpu
from jax.sharding import PartitionSpec as P

FIRST_DECAY = 0.9
SECOND_DECAY = 0.999
ADAM_EPS = 1e-08
NORM_EPS = 1e-06
MESH = pl.DeviceIdType.MESH
F32 = jnp.float32
BF16 = jnp.bfloat16
I16 = jnp.int16
I32 = jnp.int32

B = 512
H = 256
XROWS = 192
YROWS = B - XROWS
S = 32
T = 16
STRIDE = 64
LANES = 128
WIDE = B // LANES * S
NB = 8
NY = 4
FULL = 32760.0
STEP = math.log(2.0) / 4.0
TINY = 1e-30

PEERS = [(1, 2), (1, 1), (1, 3), (0, 2), (1, 0), (0, 1), (0, 3)]


def code_of(peak):
    return jnp.ceil(jnp.log(jnp.maximum(peak, TINY)) * (1.0 / STEP))


def coded(x):
    return jnp.floor(x + 0.5).astype(I32).astype(I16)


def scale_of(code):
    return jnp.exp(code.astype(I32).astype(F32) * STEP) * (1.0 / FULL)


def decoded(values, scale):
    return values.astype(I32).astype(F32) * scale


def encode_piece(n, read, out, keep=None):
    tiles = range(H // LANES)

    def look(i, peak):
        r = pl.multiple_of(i * STRIDE, STRIDE)
        for t in tiles:
            x = read(t, r)
            if keep is not None:
                keep[pl.ds(r, STRIDE), pl.ds(t * LANES, LANES)] = x
            peak = jnp.maximum(peak, jnp.max(jnp.abs(x).reshape(STRIDE // T, T, LANES), axis=0))
        return peak

    code = code_of(lax.fori_loop(0, n // STRIDE, look, jnp.zeros((T, LANES), F32)))
    factor = jnp.exp(code * -STEP) * FULL

    def write(i, carry):
        r = pl.multiple_of(i * STRIDE, STRIDE)
        for t in tiles:
            x = read(t, r) if keep is None else keep[pl.ds(r, STRIDE), pl.ds(t * LANES, LANES)]
            x = x.reshape(STRIDE // T, T, LANES) * factor[None]
            out[pl.ds(t * n + r, STRIDE), :] = coded(x).reshape(STRIDE, LANES)
        return carry

    lax.fori_loop(0, n // STRIDE, write, 0)
    out[pl.ds(H // LANES * n, T), :] = code.astype(I32).astype(I16)


def sum_of(n, own, arrived):
    scales = [scale_of(ref[pl.ds(H // LANES * n, T), :])[None] for ref in arrived]

    def read(t, r):
        x = own(t, r)
        for ref, scale in zip(arrived, scales):
            values = ref[pl.ds(t * n + r, STRIDE), :].reshape(STRIDE // T, T, LANES)
            x = x + decoded(values, scale).reshape(STRIDE, LANES)
        return x

    return read


def encode_rows(x, group, out, first):
    n = B // LANES
    parts = [x[:, t * LANES : (t + 1) * LANES].reshape(S // group, group, LANES) for t in range(n)]
    code = code_of(functools.reduce(jnp.maximum, [jnp.max(jnp.abs(p), axis=0) for p in parts]))
    factor = jnp.exp(code * -STEP) * FULL
    for t in range(n):
        out[pl.ds(first + t * S, S), :] = coded(parts[t] * factor[None]).reshape(S, LANES)
    return code


def decode_rows(codes, first, scale):
    group = scale.shape[0]
    return [
        decoded(codes[pl.ds(first + t * S, S), :].reshape(S // group, group, LANES), scale[None]).reshape(S, LANES)
        for t in range(B // LANES)
    ]


def dot(a, b, dims=((1,), (0,))):
    return lax.dot_general(a, b, (dims, ((), ())), preferred_element_type=F32)


def split(x):
    high = x.astype(BF16)
    return high, (x - high.astype(F32)).astype(BF16)


def fold(x):
    r, c = x.shape
    x = jnp.sum(x.reshape(r // 8, 8, c), axis=0)
    return functools.reduce(jnp.add, [x[:, t * LANES : (t + 1) * LANES] for t in range(c // LANES)])


def kernel(
    home_hbm, part_hbm, lroot_hbm, rroot_hbm, first_hbm, second_hbm,
    prod_in, new_first_hbm, new_second_hbm, update_hbm,
    home, part, first, second, new_first, new_second, update, lroot, rroot,
    x1_out, x1_in, y1_out, y1_in, x2_out, x2_in, y2_out, y2_in,
    work, ghigh, glow, grow_out, grow_in, prod_out, left_codes, pleft, pright,
    sums_out, sums_in, pair_out, pair_in,
    load_sem, root_send, root_recv, x1_send, x1_recv, y1_send, y1_recv, s2_send, s2_recv,
    core_send, core_recv, row_send, row_recv, sum_send, sum_recv, store_sem,
):
    d = lax.axis_index("dp")
    m = lax.axis_index("mp")
    xl, y = d // NY, d % NY
    xh, z, k = m // 8, (m // 2) % 4, m % 2
    c = m // 2

    partner = (d, m + 1 - 2 * k)
    across = ((1 - xl) * NY + y, m)

    def along_y(j):
        return (xl * NY + (y + j) % NY, m)

    def chip_at(a, b):
        return ((xh + a) % 2) * 4 + (z + b) % 4

    def along_mp(a, b):
        return (d, chip_at(a, b) * 2 + k)

    def remote(src, dst, send, recv, device):
        return pltpu.make_async_remote_copy(
            src_ref=src, dst_ref=dst, send_sem=send, recv_sem=recv, device_id=device, device_id_type=MESH
        )

    loads = [
        pltpu.make_async_copy(src, dst, load_sem.at[i])
        for i, (src, dst) in enumerate(
            [
                (home_hbm, home), (part_hbm, part), (first_hbm, first), (second_hbm, second),
                (lroot_hbm.at[c], lroot.at[c, k]), (rroot_hbm.at[c], rroot.at[c, k]),
            ]
        )
    ]
    loads[0].start()
    loads[1].start()

    barrier = pltpu.get_barrier_semaphore()
    greeted = [partner, across] + [along_y(j) for j in (1, 2, 3)] + [along_mp(a, b) for a, b in PEERS]
    for device in greeted:
        pl.semaphore_signal(barrier, inc=1, device_id=device, device_id_type=MESH)
    pl.semaphore_wait(barrier, len(greeted))

    root_copies = []
    for i, (a, b) in enumerate(PEERS):
        there = chip_at(a, b)
        for w, (src, dst) in enumerate(((lroot_hbm, lroot), (rroot_hbm, rroot))):
            copy = remote(src.at[there], dst.at[c, k], root_send.at[w, i], root_recv.at[w, i], along_mp(a, b))
            copy.start()
            root_copies.append(copy)
    for load in loads[2:]:
        load.start()

    def source(q):
        return functools.reduce(jnp.maximum, [jnp.where(home[r] == q, r, 0) for r in range(NB)])

    def own_piece(to_x, j, start):
        row = source(to_x * NY + (y + j) % NY)
        return lambda t, r: part[row, pl.ds(start + r, STRIDE), pl.ds(t * LANES, LANES)]

    loads[0].wait()
    loads[1].wait()
    x1_copies, y1_copies = {}, {}

    def send_x1(j):
        encode_piece(XROWS, own_piece(1 - xl, j, YROWS), x1_out.at[j])
        x1_copies[j] = remote(x1_out.at[j], x1_in.at[j], x1_send.at[j], x1_recv.at[j], across)
        x1_copies[j].start()

    def send_y1(w, j):
        n = w * 3 + j - 1
        encode_piece(YROWS, own_piece(1 - xl if w == 0 else xl, j, 0), y1_out.at[n])
        y1_copies[w, j] = remote(y1_out.at[n], y1_in.at[n], y1_send.at[n], y1_recv.at[n], along_y(j))
        y1_copies[w, j].start()

    for j in (1, 3, 2):
        send_y1(0, j)
        send_x1(j)
    for j in (1, 3, 2):
        send_y1(1, j)
    send_x1(0)

    y2_copies = {}
    for j in (1, 3, 2):
        x1_copies[j].wait_recv()
        read = sum_of(XROWS, own_piece(xl, j, YROWS), [x1_in.at[j]])
        encode_piece(XROWS, read, y2_out.at[j - 1], work)
        y2_copies[j] = remote(y2_out.at[j - 1], y2_in.at[j - 1], s2_send.at[j], s2_recv.at[j], along_y(j))
        y2_copies[j].start()

    for j in (1, 2, 3):
        y1_copies[0, j].wait_recv()
    read = sum_of(YROWS, own_piece(1 - xl, 0, 0), [y1_in.at[n] for n in range(3)])
    encode_piece(YROWS, read, x2_out, work)
    x2_copy = remote(x2_out, x2_in, s2_send.at[0], s2_recv.at[0], across)
    x2_copy.start()

    for copy in root_copies:
        copy.wait_recv()
    loads[4].wait()
    loads[5].wait()
    core_copies = []
    for w, ref in enumerate((lroot, rroot)):
        copy = remote(ref.at[:, k], ref.at[:, k], core_send.at[w], core_recv.at[w], partner)
        copy.start()
        core_copies.append(copy)

    strip = pl.ds(pl.multiple_of(k * H, H), H)
    block_copies = []

    def finish(n, start, read, w):
        def step(i, carry):
            r = pl.multiple_of(i * STRIDE, STRIDE)
            for t in range(H // LANES):
                mine = pl.ds(pl.multiple_of(k * H + t * LANES, LANES), LANES)
                high, low = split(read(t, r))
                ghigh[pl.ds(start + r, STRIDE), mine] = high
                glow[pl.ds(start + r, STRIDE), mine] = low
            return carry

        lax.fori_loop(0, n // STRIDE, step, 0)
        for i, ref in enumerate((ghigh, glow)):
            here = ref.at[pl.ds(start, n), strip]
            copy = remote(here, here, core_send.at[2 + 2 * w + i], core_recv.at[2 + 2 * w + i], partner)
            copy.start()
            block_copies.append(copy)

    x1_copies[0].wait_recv()
    for j in (1, 3, 2):
        y2_copies[j].wait_recv()
    arrived = [x1_in.at[0]] + [y2_in.at[n] for n in range(3)]
    finish(XROWS, YROWS, sum_of(XROWS, own_piece(xl, 0, YROWS), arrived), 0)
    for j in (1, 2, 3):
        y1_copies[1, j].wait_recv()
    x2_copy.wait_recv()
    arrived = [y1_in.at[n] for n in range(3, 6)] + [x2_in]
    finish(YROWS, 0, sum_of(YROWS, own_piece(xl, 0, 0), arrived), 1)

    for copy in block_copies:
        copy.wait_recv()

    def rows_for(there):
        return pl.ds(pl.multiple_of(there * 2 * S + k * S, S), S)

    row_copies = []
    for i, (a, b) in enumerate(PEERS + [(0, 0)]):
        rows = rows_for(chip_at(a, b))
        value = ghigh[rows, :].astype(F32) + glow[rows, :].astype(F32)
        out = grow_out.at[i] if a or b else grow_in.at[c]
        out[pl.ds(WIDE, T), :] = encode_rows(value, T, out, 0).astype(I32).astype(I16)
        if a or b:
            copy = remote(out, grow_in.at[c], row_send.at[0, i], row_recv.at[0, i], along_mp(a, b))
            copy.start()
            row_copies.append(copy)

    high_rows = jnp.concatenate([ghigh[rows_for(t), :] for t in range(NB)], axis=0)
    low_rows = jnp.concatenate([glow[rows_for(t), :] for t in range(NB)], axis=0)
    nt = ((1,), (1,))
    pleft[...] = dot(high_rows, ghigh[...], nt) + (dot(high_rows, glow[...], nt) + dot(low_rows, ghigh[...], nt))
    prod_copies = []

    def send_products(w, i, first, size):
        a, b = (PEERS + [(0, 0)])[i]
        here, there = prod_out.at[i, pl.ds(first, size)], prod_in.at[c, pl.ds(first, size)]
        if a or b:
            copy = remote(here, there, row_send.at[1 + w, i], row_recv.at[1 + w, i], along_mp(a, b))
            prod_copies.append(copy)
        else:
            copy = pltpu.make_async_copy(here, there, store_sem.at[3 + w])
            stores.append(copy)
        copy.start()

    stores = []
    for i, (a, b) in enumerate(PEERS + [(0, 0)]):
        value = pleft[pl.ds(pl.multiple_of(chip_at(a, b) * S, S), S), :]
        left_codes[i] = encode_rows(value, T // 2, prod_out.at[i], 0)
        send_products(0, i, 0, WIDE)
    tn = ((0,), (0,))
    pright[...] = dot(ghigh[...], ghigh[...], tn) + (
        dot(ghigh[...], glow[...], tn) + dot(glow[...], ghigh[...], tn)
    )
    for i, (a, b) in enumerate(PEERS + [(0, 0)]):
        code = encode_rows(pright[rows_for(chip_at(a, b)), :], T // 2, prod_out.at[i], WIDE)
        codes = jnp.concatenate([left_codes[i], code], axis=0)
        prod_out[i, pl.ds(2 * WIDE, T), :] = codes.astype(I32).astype(I16)

    loads[2].wait()
    loads[3].wait()
    sum_copies = []
    for i, (a, b) in enumerate(PEERS + [(0, 0)]):
        slot = chip_at(-a, -b)
        if a or b:
            row_copies[i].wait_recv()
        total = jnp.zeros((8, LANES), F32)
        scale = scale_of(grow_in[slot, pl.ds(WIDE, T), :])
        for t, grad in enumerate(decode_rows(grow_in.at[slot], 0, scale)):
            cols = pl.ds(t * LANES, LANES)
            mean = FIRST_DECAY * first[slot, :, cols] + (1.0 - FIRST_DECAY) * grad
            square = SECOND_DECAY * second[slot, :, cols] + (1.0 - SECOND_DECAY) * grad * grad
            new_first[slot, :, cols] = mean
            new_second[slot, :, cols] = square
            adam = mean / (jnp.sqrt(square) + ADAM_EPS)
            total = total + fold(adam * adam)
        sums_out[i] = total
        if a or b:
            copy = remote(sums_out.at[i], sums_in.at[i], sum_send.at[i], sum_recv.at[i], along_mp(-a, -b))
            copy.start()
            sum_copies.append(copy)
    for i in range(NB):
        send_products(1, i, WIDE, WIDE + T)

    for copy in core_copies:
        copy.wait_recv()
    rcols = jnp.concatenate([rroot[a, b, :, strip] for a in range(NB) for b in range(2)], axis=0)
    inner = dot(ghigh[...], rcols) + dot(glow[...], rcols)
    inner_high, inner_low = split(inner)
    lrows = lroot[...].reshape(B, B)
    applied = dot(lrows, inner_high) + dot(lrows, inner_low)
    pright[:, pl.ds(0, H)] = applied
    pair_out[1] = fold(applied * applied)

    moment_stores = [
        pltpu.make_async_copy(new_first, new_first_hbm, store_sem.at[0]),
        pltpu.make_async_copy(new_second, new_second_hbm, store_sem.at[1]),
    ]
    for store in moment_stores:
        store.start()

    total = sums_out[len(PEERS)]
    for i, copy in enumerate(sum_copies):
        copy.wait_recv()
        total = total + sums_in[i]
    pair_out[0] = total
    pair_copy = remote(pair_out, pair_in, sum_send.at[len(PEERS)], sum_recv.at[len(PEERS)], partner)
    pair_copy.start()
    pair_copy.wait_recv()
    norms = [jnp.sum(pair_out[w] + pair_in[w], axis=(0, 1), keepdims=True) for w in range(2)]
    graft = jnp.sqrt(norms[0]) / (jnp.sqrt(norms[1]) + NORM_EPS)
    update[...] = (pright[:, pl.ds(0, H)] * graft).astype(BF16)
    update_store = pltpu.make_async_copy(update, update_hbm, store_sem.at[2])
    update_store.start()

    for copy in prod_copies:
        copy.wait_recv()
    sent = [x2_copy, pair_copy] + root_copies + core_copies + block_copies + row_copies + prod_copies + sum_copies
    for copy in sent + list(x1_copies.values()) + list(y1_copies.values()) + list(y2_copies.values()):
        copy.wait_send()
    for store in stores + moment_stores + [update_store]:
        store.wait()


def finish_kernel(
    prod_hbm, left_hbm, right_hbm, made_first, made_second, made_update,
    left_out, right_out, first_out, second_out, update_out,
    prod, left, right, first, second, update, load_sem, store_sem,
):
    through = [(made_first, first, first_out), (made_second, second, second_out), (made_update, update, update_out)]
    stats = [(left_hbm, left, left_out), (right_hbm, right, right_out)]
    loads = [pltpu.make_async_copy(prod_hbm, prod, load_sem.at[0])]
    for i, (src, dst, _) in enumerate(stats + through):
        loads.append(pltpu.make_async_copy(src, dst, load_sem.at[1 + i]))
    stores = [pltpu.make_async_copy(src, dst, store_sem.at[i]) for i, (_, src, dst) in enumerate(stats + through)]
    for load in loads:
        load.start()
    loads[0].wait()
    for w, ref in enumerate((left, right)):
        loads[1 + w].wait()

        def add(slot, carry):
            code = prod[slot, pl.ds(2 * WIDE, T), :].astype(F32)[w * (T // 2) : (w + 1) * (T // 2)]
            for t, value in enumerate(decode_rows(prod.at[slot], w * WIDE, jnp.exp(code * STEP) * (1.0 / FULL))):
                ref[slot, :, pl.ds(t * LANES, LANES)] += value
            return carry

        lax.fori_loop(0, NB, add, 0)
        stores[w].start()
    for i in range(len(through)):
        loads[3 + i].wait()
        stores[2 + i].start()
    for store in stores:
        store.wait()


def on_device(
    grad_parts, home, left_stat, right_stat, left_root, right_root, first_moment, second_moment
):
    in_hbm = pl.BlockSpec(memory_space=pltpu.HBM)
    n = len(PEERS)
    xpiece = (H // LANES * XROWS + T, LANES)
    ypiece = (H // LANES * YROWS + T, LANES)
    rows = (WIDE + T, LANES)
    products = (2 * WIDE + T, LANES)
    stat = pltpu.VMEM((NB, S, B), F32)
    tile = pltpu.VMEM((B, H), BF16)
    dma = pltpu.SemaphoreType.DMA
    scratch = [
        pltpu.SMEM((NB,), I32),
        pltpu.VMEM((NB, B, H), F32),
        *[stat] * 4,
        tile,
        *[pltpu.VMEM((NB, 2, S, B), BF16)] * 2,
        *[pltpu.VMEM((4, *xpiece), I16)] * 2,
        *[pltpu.VMEM((6, *ypiece), I16)] * 2,
        *[pltpu.VMEM(ypiece, I16)] * 2,
        *[pltpu.VMEM((3, *xpiece), I16)] * 2,
        pltpu.VMEM((B, H), F32),
        *[pltpu.VMEM((B, B), BF16)] * 2,
        pltpu.VMEM((n, *rows), I16),
        pltpu.VMEM((NB, *rows), I16),
        pltpu.VMEM((NB, *products), I16),
        pltpu.VMEM((NB, T // 2, LANES), F32),
        pltpu.VMEM((H, B), F32),
        pltpu.VMEM((B, B), F32),
        pltpu.VMEM((NB, 8, LANES), F32),
        pltpu.VMEM((n, 8, LANES), F32),
        *[pltpu.VMEM((2, 8, LANES), F32)] * 2,
        dma((6,)),
        *[dma((2, n))] * 2,
        *[dma((4,))] * 2,
        *[dma((6,))] * 2,
        *[dma((4,))] * 2,
        *[dma((6,))] * 2,
        *[dma((3, n))] * 2,
        *[dma((n + 1,))] * 2,
        dma((5,)),
    ]
    stat_out = jax.ShapeDtypeStruct((NB, S, B), F32)
    tile_out = jax.ShapeDtypeStruct((B, H), BF16)
    made = pl.pallas_call(
        kernel,
        out_shape=(jax.ShapeDtypeStruct((NB, *products), I16), stat_out, stat_out, tile_out),
        in_specs=[in_hbm] * 6,
        out_specs=[in_hbm] * 4,
        scratch_shapes=scratch,
        compiler_params=pltpu.CompilerParams(
            collective_id=0, has_side_effects=True, vmem_limit_bytes=58 * 2**20
        ),
        cost_estimate=pl.CostEstimate(flops=2 * 10**9, bytes_accessed=9 * 2**20, transcendentals=0),
        name="shampoo_step",
    )(home, grad_parts.reshape(NB, B, H), left_root, right_root, first_moment, second_moment)
    return pl.pallas_call(
        finish_kernel,
        out_shape=(stat_out,) * 4 + (tile_out,),
        in_specs=[in_hbm] * 6,
        out_specs=[in_hbm] * 5,
        scratch_shapes=[pltpu.VMEM((NB, *products), I16), *[stat] * 4, tile, dma((6,)), dma((5,))],
        compiler_params=pltpu.CompilerParams(vmem_limit_bytes=58 * 2**20),
        name="finish_outputs",
    )(made[0], left_stat, right_stat, *made[1:])


def solution(mesh):
    rows = P("dp", "mp", None)
    in_specs = (P("dp", None, "mp"), P(), rows, rows, rows, rows, rows, rows)
    out_specs = (rows, rows, rows, rows, P("dp", "mp"))
    return jax.shard_map(
        on_device, mesh=mesh, in_specs=in_specs, out_specs=out_specs, check_vma=False
    )
```

```python
import functools
import math

import jax
import jax.numpy as jnp
from jax import lax
from jax.experimental import pallas as pl
from jax.experimental.pallas import tpu as pltpu
from jax.sharding import PartitionSpec as P

FIRST_DECAY = 0.9
SECOND_DECAY = 0.999
ADAM_EPS = 1e-08
NORM_EPS = 1e-06
MESH = pl.DeviceIdType.MESH
F32 = jnp.float32
BF16 = jnp.bfloat16
I16 = jnp.int16
I32 = jnp.int32

B = 512
H = 256
XROWS = 192
YROWS = B - XROWS
S = 32
T = 16
STRIDE = 64
LANES = 128
WIDE = B // LANES * S
NB = 8
NY = 4
FULL = 32760.0
STEP = math.log(2.0) / 4.0
TINY = 1e-30

PEERS = [(1, 2), (1, 1), (1, 3), (0, 2), (1, 0), (0, 1), (0, 3)]


def code_of(peak):
    return jnp.ceil(jnp.log(jnp.maximum(peak, TINY)) * (1.0 / STEP))


def coded(x):
    return jnp.floor(x + 0.5).astype(I32).astype(I16)


def scale_of(code):
    return jnp.exp(code.astype(I32).astype(F32) * STEP) * (1.0 / FULL)


def decoded(values, scale):
    return values.astype(I32).astype(F32) * scale


def encode_piece(n, read, out, keep=None):
    tiles = range(H // LANES)

    def look(i, peak):
        r = pl.multiple_of(i * STRIDE, STRIDE)
        for t in tiles:
            x = read(t, r)
            if keep is not None:
                keep[pl.ds(r, STRIDE), pl.ds(t * LANES, LANES)] = x
            peak = jnp.maximum(peak, jnp.max(jnp.abs(x).reshape(STRIDE // T, T, LANES), axis=0))
        return peak

    code = code_of(lax.fori_loop(0, n // STRIDE, look, jnp.zeros((T, LANES), F32)))
    factor = jnp.exp(code * -STEP) * FULL

    def write(i, carry):
        r = pl.multiple_of(i * STRIDE, STRIDE)
        for t in tiles:
            x = read(t, r) if keep is None else keep[pl.ds(r, STRIDE), pl.ds(t * LANES, LANES)]
            x = x.reshape(STRIDE // T, T, LANES) * factor[None]
            out[pl.ds(t * n + r, STRIDE), :] = coded(x).reshape(STRIDE, LANES)
        return carry

    lax.fori_loop(0, n // STRIDE, write, 0)
    out[pl.ds(H // LANES * n, T), :] = code.astype(I32).astype(I16)


def sum_of(n, own, arrived):
    scales = [scale_of(ref[pl.ds(H // LANES * n, T), :])[None] for ref in arrived]

    def read(t, r):
        x = own(t, r)
        for ref, scale in zip(arrived, scales):
            values = ref[pl.ds(t * n + r, STRIDE), :].reshape(STRIDE // T, T, LANES)
            x = x + decoded(values, scale).reshape(STRIDE, LANES)
        return x

    return read


def encode_rows(x, group, out, first):
    n = B // LANES
    parts = [x[:, t * LANES : (t + 1) * LANES].reshape(S // group, group, LANES) for t in range(n)]
    code = code_of(functools.reduce(jnp.maximum, [jnp.max(jnp.abs(p), axis=0) for p in parts]))
    factor = jnp.exp(code * -STEP) * FULL
    for t in range(n):
        out[pl.ds(first + t * S, S), :] = coded(parts[t] * factor[None]).reshape(S, LANES)
    return code


def decode_rows(codes, first, scale):
    group = scale.shape[0]
    return [
        decoded(codes[pl.ds(first + t * S, S), :].reshape(S // group, group, LANES), scale[None]).reshape(S, LANES)
        for t in range(B // LANES)
    ]


def dot(a, b, dims=((1,), (0,))):
    return lax.dot_general(a, b, (dims, ((), ())), preferred_element_type=F32)


def split(x):
    high = x.astype(BF16)
    return high, (x - high.astype(F32)).astype(BF16)


def fold(x):
    r, c = x.shape
    x = jnp.sum(x.reshape(r // 8, 8, c), axis=0)
    return functools.reduce(jnp.add, [x[:, t * LANES : (t + 1) * LANES] for t in range(c // LANES)])


def kernel(
    home_hbm, part_hbm, lroot_hbm, rroot_hbm, first_hbm, second_hbm,
    prod_in, new_first, new_second, update,
    home, part, first, second, lroot, rroot,
    x1_out, x1_in, y1_out, y1_in, x2_out, x2_in, y2_out, y2_in,
    work, ghigh, glow, grow_out, grow_in, prod_out, left_codes, pleft, pright,
    sums_out, sums_in, pair_out, pair_in,
    load_sem, root_send, root_recv, x1_send, x1_recv, y1_send, y1_recv, s2_send, s2_recv,
    core_send, core_recv, row_send, row_recv, sum_send, sum_recv, store_sem,
):
    d = lax.axis_index("dp")
    m = lax.axis_index("mp")
    xl, y = d // NY, d % NY
    xh, z, k = m // 8, (m // 2) % 4, m % 2
    c = m // 2

    partner = (d, m + 1 - 2 * k)
    across = ((1 - xl) * NY + y, m)

    def along_y(j):
        return (xl * NY + (y + j) % NY, m)

    def chip_at(a, b):
        return ((xh + a) % 2) * 4 + (z + b) % 4

    def along_mp(a, b):
        return (d, chip_at(a, b) * 2 + k)

    def remote(src, dst, send, recv, device):
        return pltpu.make_async_remote_copy(
            src_ref=src, dst_ref=dst, send_sem=send, recv_sem=recv, device_id=device, device_id_type=MESH
        )

    loads = [
        pltpu.make_async_copy(src, dst, load_sem.at[i])
        for i, (src, dst) in enumerate(
            [
                (home_hbm, home), (part_hbm, part), (first_hbm, first), (second_hbm, second),
                (lroot_hbm.at[c], lroot.at[c, k]), (rroot_hbm.at[c], rroot.at[c, k]),
            ]
        )
    ]
    loads[0].start()
    loads[1].start()

    barrier = pltpu.get_barrier_semaphore()
    greeted = [partner, across] + [along_y(j) for j in (1, 2, 3)] + [along_mp(a, b) for a, b in PEERS]
    for device in greeted:
        pl.semaphore_signal(barrier, inc=1, device_id=device, device_id_type=MESH)
    pl.semaphore_wait(barrier, len(greeted))

    root_copies = []
    for i, (a, b) in enumerate(PEERS):
        there = chip_at(a, b)
        for w, (src, dst) in enumerate(((lroot_hbm, lroot), (rroot_hbm, rroot))):
            copy = remote(src.at[there], dst.at[c, k], root_send.at[w, i], root_recv.at[w, i], along_mp(a, b))
            copy.start()
            root_copies.append(copy)
    for load in loads[2:]:
        load.start()

    def source(q):
        return functools.reduce(jnp.maximum, [jnp.where(home[r] == q, r, 0) for r in range(NB)])

    def own_piece(to_x, j, start):
        row = source(to_x * NY + (y + j) % NY)
        return lambda t, r: part[row, pl.ds(start + r, STRIDE), pl.ds(t * LANES, LANES)]

    loads[0].wait()
    loads[1].wait()
    x1_copies, y1_copies = {}, {}

    def send_x1(j):
        encode_piece(XROWS, own_piece(1 - xl, j, YROWS), x1_out.at[j])
        x1_copies[j] = remote(x1_out.at[j], x1_in.at[j], x1_send.at[j], x1_recv.at[j], across)
        x1_copies[j].start()

    def send_y1(w, j):
        n = w * 3 + j - 1
        encode_piece(YROWS, own_piece(1 - xl if w == 0 else xl, j, 0), y1_out.at[n])
        y1_copies[w, j] = remote(y1_out.at[n], y1_in.at[n], y1_send.at[n], y1_recv.at[n], along_y(j))
        y1_copies[w, j].start()

    for j in (1, 3, 2):
        send_y1(0, j)
        send_x1(j)
    for j in (1, 3, 2):
        send_y1(1, j)
    send_x1(0)

    y2_copies = {}
    for j in (1, 3, 2):
        x1_copies[j].wait_recv()
        read = sum_of(XROWS, own_piece(xl, j, YROWS), [x1_in.at[j]])
        encode_piece(XROWS, read, y2_out.at[j - 1], work)
        y2_copies[j] = remote(y2_out.at[j - 1], y2_in.at[j - 1], s2_send.at[j], s2_recv.at[j], along_y(j))
        y2_copies[j].start()

    for j in (1, 2, 3):
        y1_copies[0, j].wait_recv()
    read = sum_of(YROWS, own_piece(1 - xl, 0, 0), [y1_in.at[n] for n in range(3)])
    encode_piece(YROWS, read, x2_out, work)
    x2_copy = remote(x2_out, x2_in, s2_send.at[0], s2_recv.at[0], across)
    x2_copy.start()

    for copy in root_copies:
        copy.wait_recv()
    loads[4].wait()
    loads[5].wait()
    core_copies = []
    for w, ref in enumerate((lroot, rroot)):
        copy = remote(ref.at[:, k], ref.at[:, k], core_send.at[w], core_recv.at[w], partner)
        copy.start()
        core_copies.append(copy)

    strip = pl.ds(pl.multiple_of(k * H, H), H)
    block_copies = []

    def finish(n, start, read, w):
        def step(i, carry):
            r = pl.multiple_of(i * STRIDE, STRIDE)
            for t in range(H // LANES):
                mine = pl.ds(pl.multiple_of(k * H + t * LANES, LANES), LANES)
                high, low = split(read(t, r))
                ghigh[pl.ds(start + r, STRIDE), mine] = high
                glow[pl.ds(start + r, STRIDE), mine] = low
            return carry

        lax.fori_loop(0, n // STRIDE, step, 0)
        for i, ref in enumerate((ghigh, glow)):
            here = ref.at[pl.ds(start, n), strip]
            copy = remote(here, here, core_send.at[2 + 2 * w + i], core_recv.at[2 + 2 * w + i], partner)
            copy.start()
            block_copies.append(copy)

    x1_copies[0].wait_recv()
    for j in (1, 3, 2):
        y2_copies[j].wait_recv()
    arrived = [x1_in.at[0]] + [y2_in.at[n] for n in range(3)]
    finish(XROWS, YROWS, sum_of(XROWS, own_piece(xl, 0, YROWS), arrived), 0)
    for j in (1, 2, 3):
        y1_copies[1, j].wait_recv()
    x2_copy.wait_recv()
    arrived = [y1_in.at[n] for n in range(3, 6)] + [x2_in]
    finish(YROWS, 0, sum_of(YROWS, own_piece(xl, 0, 0), arrived), 1)

    for copy in block_copies:
        copy.wait_recv()

    def rows_for(there):
        return pl.ds(pl.multiple_of(there * 2 * S + k * S, S), S)

    row_copies = []
    for i, (a, b) in enumerate(PEERS + [(0, 0)]):
        rows = rows_for(chip_at(a, b))
        value = ghigh[rows, :].astype(F32) + glow[rows, :].astype(F32)
        out = grow_out.at[i] if a or b else grow_in.at[c]
        out[pl.ds(WIDE, T), :] = encode_rows(value, T, out, 0).astype(I32).astype(I16)
        if a or b:
            copy = remote(out, grow_in.at[c], row_send.at[0, i], row_recv.at[0, i], along_mp(a, b))
            copy.start()
            row_copies.append(copy)

    high_rows = jnp.concatenate([ghigh[rows_for(t), :] for t in range(NB)], axis=0)
    low_rows = jnp.concatenate([glow[rows_for(t), :] for t in range(NB)], axis=0)
    nt = ((1,), (1,))
    pleft[...] = dot(high_rows, ghigh[...], nt) + (dot(high_rows, glow[...], nt) + dot(low_rows, ghigh[...], nt))
    prod_copies = []

    def send_products(w, i, first, size):
        a, b = (PEERS + [(0, 0)])[i]
        here, there = prod_out.at[i, pl.ds(first, size)], prod_in.at[c, pl.ds(first, size)]
        if a or b:
            copy = remote(here, there, row_send.at[1 + w, i], row_recv.at[1 + w, i], along_mp(a, b))
            prod_copies.append(copy)
        else:
            copy = pltpu.make_async_copy(here, there, store_sem.at[w])
            stores.append(copy)
        copy.start()

    stores = []
    for i, (a, b) in enumerate(PEERS + [(0, 0)]):
        value = pleft[pl.ds(pl.multiple_of(chip_at(a, b) * S, S), S), :]
        left_codes[i] = encode_rows(value, T // 2, prod_out.at[i], 0)
        send_products(0, i, 0, WIDE)
    tn = ((0,), (0,))
    pright[...] = dot(ghigh[...], ghigh[...], tn) + (
        dot(ghigh[...], glow[...], tn) + dot(glow[...], ghigh[...], tn)
    )
    for i, (a, b) in enumerate(PEERS + [(0, 0)]):
        code = encode_rows(pright[rows_for(chip_at(a, b)), :], T // 2, prod_out.at[i], WIDE)
        codes = jnp.concatenate([left_codes[i], code], axis=0)
        prod_out[i, pl.ds(2 * WIDE, T), :] = codes.astype(I32).astype(I16)

    loads[2].wait()
    loads[3].wait()
    sum_copies = []
    for i, (a, b) in enumerate(PEERS + [(0, 0)]):
        slot = chip_at(-a, -b)
        if a or b:
            row_copies[i].wait_recv()
        total = jnp.zeros((8, LANES), F32)
        scale = scale_of(grow_in[slot, pl.ds(WIDE, T), :])
        for t, grad in enumerate(decode_rows(grow_in.at[slot], 0, scale)):
            cols = pl.ds(t * LANES, LANES)
            mean = FIRST_DECAY * first[slot, :, cols] + (1.0 - FIRST_DECAY) * grad
            square = SECOND_DECAY * second[slot, :, cols] + (1.0 - SECOND_DECAY) * grad * grad
            new_first[slot, :, cols] = mean
            new_second[slot, :, cols] = square
            adam = mean / (jnp.sqrt(square) + ADAM_EPS)
            total = total + fold(adam * adam)
        sums_out[i] = total
        if a or b:
            copy = remote(sums_out.at[i], sums_in.at[i], sum_send.at[i], sum_recv.at[i], along_mp(-a, -b))
            copy.start()
            sum_copies.append(copy)
    for i in range(NB):
        send_products(1, i, WIDE, WIDE + T)

    for copy in core_copies:
        copy.wait_recv()
    rcols = jnp.concatenate([rroot[a, b, :, strip] for a in range(NB) for b in range(2)], axis=0)
    inner = dot(ghigh[...], rcols) + dot(glow[...], rcols)
    inner_high, inner_low = split(inner)
    lrows = lroot[...].reshape(B, B)
    applied = dot(lrows, inner_high) + dot(lrows, inner_low)
    pright[:, pl.ds(0, H)] = applied
    pair_out[1] = fold(applied * applied)

    total = sums_out[len(PEERS)]
    for i, copy in enumerate(sum_copies):
        copy.wait_recv()
        total = total + sums_in[i]
    pair_out[0] = total
    pair_copy = remote(pair_out, pair_in, sum_send.at[len(PEERS)], sum_recv.at[len(PEERS)], partner)
    pair_copy.start()
    pair_copy.wait_recv()
    norms = [jnp.sum(pair_out[w] + pair_in[w], axis=(0, 1), keepdims=True) for w in range(2)]
    graft = jnp.sqrt(norms[0]) / (jnp.sqrt(norms[1]) + NORM_EPS)
    update[...] = (pright[:, pl.ds(0, H)] * graft).astype(BF16)

    for copy in prod_copies:
        copy.wait_recv()
    sent = [x2_copy, pair_copy] + root_copies + core_copies + block_copies + row_copies + prod_copies + sum_copies
    for copy in sent + list(x1_copies.values()) + list(y1_copies.values()) + list(y2_copies.values()):
        copy.wait_send()
    for store in stores:
        store.wait()


def finish_kernel(
    prod, left, right, first, second, update,
    left_out, right_out, first_out, second_out, update_out,
    new_left, new_right, sem,
):
    through = [(first, first_out), (second, second_out), (update, update_out)]
    stats = [(new_left, left_out), (new_right, right_out)]
    stores = [pltpu.make_async_copy(src, dst, sem.at[i]) for i, (src, dst) in enumerate(stats + through)]
    for store in stores[2:]:
        store.start()
    for w, (old, new) in enumerate(((left, new_left), (right, new_right))):

        def add(slot, carry):
            code = prod[slot, pl.ds(2 * WIDE, T), :].astype(F32)[w * (T // 2) : (w + 1) * (T // 2)]
            scale = jnp.exp(code * STEP) * (1.0 / FULL)
            for t, value in enumerate(decode_rows(prod.at[slot], w * WIDE, scale)):
                cols = pl.ds(t * LANES, LANES)
                new[slot, :, cols] = old[slot, :, cols] + value
            return carry

        lax.fori_loop(0, NB, add, 0)
        stores[w].start()
    for store in stores:
        store.wait()


def on_device(
    grad_parts, home, left_stat, right_stat, left_root, right_root, first_moment, second_moment
):
    in_hbm = pl.BlockSpec(memory_space=pltpu.HBM)
    in_vmem = pl.BlockSpec(memory_space=pltpu.VMEM)
    n = len(PEERS)
    xpiece = (H // LANES * XROWS + T, LANES)
    ypiece = (H // LANES * YROWS + T, LANES)
    rows = (WIDE + T, LANES)
    products = (2 * WIDE + T, LANES)
    stat = pltpu.VMEM((NB, S, B), F32)
    tile = pltpu.VMEM((B, H), BF16)
    dma = pltpu.SemaphoreType.DMA
    scratch = [
        pltpu.SMEM((NB,), I32),
        pltpu.VMEM((NB, B, H), F32),
        *[stat] * 2,
        *[pltpu.VMEM((NB, 2, S, B), BF16)] * 2,
        *[pltpu.VMEM((4, *xpiece), I16)] * 2,
        *[pltpu.VMEM((6, *ypiece), I16)] * 2,
        *[pltpu.VMEM(ypiece, I16)] * 2,
        *[pltpu.VMEM((3, *xpiece), I16)] * 2,
        pltpu.VMEM((B, H), F32),
        *[pltpu.VMEM((B, B), BF16)] * 2,
        pltpu.VMEM((n, *rows), I16),
        pltpu.VMEM((NB, *rows), I16),
        pltpu.VMEM((NB, *products), I16),
        pltpu.VMEM((NB, T // 2, LANES), F32),
        pltpu.VMEM((H, B), F32),
        pltpu.VMEM((B, B), F32),
        pltpu.VMEM((NB, 8, LANES), F32),
        pltpu.VMEM((n, 8, LANES), F32),
        *[pltpu.VMEM((2, 8, LANES), F32)] * 2,
        dma((6,)),
        *[dma((2, n))] * 2,
        *[dma((4,))] * 2,
        *[dma((6,))] * 2,
        *[dma((4,))] * 2,
        *[dma((6,))] * 2,
        *[dma((3, n))] * 2,
        *[dma((n + 1,))] * 2,
        dma((2,)),
    ]
    made = pl.pallas_call(
        kernel,
        out_shape=(pltpu.VMEM((NB, *products), I16), stat, stat, tile),
        in_specs=[in_hbm] * 6,
        out_specs=[in_vmem] * 4,
        scratch_shapes=scratch,
        compiler_params=pltpu.CompilerParams(
            collective_id=0, has_side_effects=True, vmem_limit_bytes=40 * 2**20
        ),
        cost_estimate=pl.CostEstimate(flops=2 * 10**9, bytes_accessed=9 * 2**20, transcendentals=0),
        name="shampoo_step",
    )(
        *[
            pltpu.with_memory_space_constraint(x, pltpu.HBM)
            for x in (home, grad_parts.reshape(NB, B, H), left_root, right_root, first_moment, second_moment)
        ]
    )
    stat_out = jax.ShapeDtypeStruct((NB, S, B), F32)
    return pl.pallas_call(
        finish_kernel,
        out_shape=(stat_out,) * 4 + (jax.ShapeDtypeStruct((B, H), BF16),),
        in_specs=[in_vmem] * 6,
        out_specs=[in_hbm] * 5,
        scratch_shapes=[stat, stat, dma((5,))],
        compiler_params=pltpu.CompilerParams(vmem_limit_bytes=16 * 2**20),
        name="finish_outputs",
    )(made[0], left_stat, right_stat, *made[1:])


def solution(mesh):
    rows = P("dp", "mp", None)
    in_specs = (P("dp", None, "mp"), P(), rows, rows, rows, rows, rows, rows)
    out_specs = (rows, rows, rows, rows, P("dp", "mp"))
    return jax.shard_map(
        on_device, mesh=mesh, in_specs=in_specs, out_specs=out_specs, check_vma=False
    )
```

```python
import functools
import math

import jax
import jax.numpy as jnp
from jax import lax
from jax.experimental import pallas as pl
from jax.experimental.pallas import tpu as pltpu
from jax.sharding import PartitionSpec as P

FIRST_DECAY = 0.9
SECOND_DECAY = 0.999
ADAM_EPS = 1e-08
NORM_EPS = 1e-06
MESH = pl.DeviceIdType.MESH
F32 = jnp.float32
BF16 = jnp.bfloat16
I16 = jnp.int16
I32 = jnp.int32

B = 512
H = 256
PARTS = ((0, 192), (192, 192), (384, 128))
RING = PARTS[0][1]
CROSS = PARTS[2][1]
S = 32
T = 16
STRIDE = 64
LANES = 128
WIDE = B // LANES * S
NB = 8
NY = 4
FULL = 32760.0
STEP = math.log(2.0) / 4.0
TINY = 1e-30

PEERS = [(1, 2), (1, 1), (1, 3), (0, 2), (1, 0), (0, 1), (0, 3)]


def code_of(peak):
    return jnp.ceil(jnp.log(jnp.maximum(peak, TINY)) * (1.0 / STEP))


def coded(x):
    return jnp.floor(x + 0.5).astype(I32).astype(I16)


def scale_of(code):
    return jnp.exp(code.astype(I32).astype(F32) * STEP) * (1.0 / FULL)


def decoded(values, scale):
    return values.astype(I32).astype(F32) * scale


def encode_piece(n, read, out, keep=None):
    tiles = range(H // LANES)

    def look(i, peak):
        r = pl.multiple_of(i * STRIDE, STRIDE)
        for t in tiles:
            x = read(t, r)
            if keep is not None:
                keep[pl.ds(r, STRIDE), pl.ds(t * LANES, LANES)] = x
            peak = jnp.maximum(peak, jnp.max(jnp.abs(x).reshape(STRIDE // T, T, LANES), axis=0))
        return peak

    code = code_of(lax.fori_loop(0, n // STRIDE, look, jnp.zeros((T, LANES), F32)))
    factor = jnp.exp(code * -STEP) * FULL

    def write(i, carry):
        r = pl.multiple_of(i * STRIDE, STRIDE)
        for t in tiles:
            x = read(t, r) if keep is None else keep[pl.ds(r, STRIDE), pl.ds(t * LANES, LANES)]
            x = x.reshape(STRIDE // T, T, LANES) * factor[None]
            out[pl.ds(t * n + r, STRIDE), :] = coded(x).reshape(STRIDE, LANES)
        return carry

    lax.fori_loop(0, n // STRIDE, write, 0)
    out[pl.ds(H // LANES * n, T), :] = code.astype(I32).astype(I16)


def sum_of(n, own, arrived):
    scales = [scale_of(ref[pl.ds(H // LANES * n, T), :])[None] for ref in arrived]

    def read(t, r):
        x = own(t, r)
        for ref, scale in zip(arrived, scales):
            values = ref[pl.ds(t * n + r, STRIDE), :].reshape(STRIDE // T, T, LANES)
            x = x + decoded(values, scale).reshape(STRIDE, LANES)
        return x

    return read


def encode_rows(x, group, out, first):
    n = B // LANES
    parts = [x[:, t * LANES : (t + 1) * LANES].reshape(S // group, group, LANES) for t in range(n)]
    code = code_of(functools.reduce(jnp.maximum, [jnp.max(jnp.abs(p), axis=0) for p in parts]))
    factor = jnp.exp(code * -STEP) * FULL
    for t in range(n):
        out[pl.ds(first + t * S, S), :] = coded(parts[t] * factor[None]).reshape(S, LANES)
    return code


def decode_rows(codes, first, scale):
    group = scale.shape[0]
    return [
        decoded(codes[pl.ds(first + t * S, S), :].reshape(S // group, group, LANES), scale[None]).reshape(S, LANES)
        for t in range(B // LANES)
    ]


def dot(a, b, dims=((1,), (0,))):
    return lax.dot_general(a, b, (dims, ((), ())), preferred_element_type=F32)


def split(x):
    high = x.astype(BF16)
    return high, (x - high.astype(F32)).astype(BF16)


def fold(x):
    r, c = x.shape
    x = jnp.sum(x.reshape(r // 8, 8, c), axis=0)
    return functools.reduce(jnp.add, [x[:, t * LANES : (t + 1) * LANES] for t in range(c // LANES)])


def kernel(
    home_hbm, part_hbm, lroot_hbm, rroot_hbm, first_hbm, second_hbm,
    prod_in, new_first, new_second, update,
    home, part_up, part_down, part_cross, first, second, lroot, rroot,
    ring_out, ring_in, x1_out, x1_in, y2_out, y2_in, x2_out, x2_in,
    work, ghigh, glow, grow_out, grow_in, prod_out, left_codes, pleft, pright,
    sums_out, sums_in, pair_out, pair_in,
    load_sem, root_send, root_recv, ring_send, ring_recv, x1_send, x1_recv, s2_send, s2_recv,
    core_send, core_recv, row_send, row_recv, sum_send, sum_recv, store_sem,
):
    d = lax.axis_index("dp")
    m = lax.axis_index("mp")
    xl, y = d // NY, d % NY
    xh, z, k = m // 8, (m // 2) % 4, m % 2
    c = m // 2

    partner = (d, m + 1 - 2 * k)
    across = ((1 - xl) * NY + y, m)

    def along_y(j):
        return (xl * NY + (y + j) % NY, m)

    def chip_at(a, b):
        return ((xh + a) % 2) * 4 + (z + b) % 4

    def along_mp(a, b):
        return (d, chip_at(a, b) * 2 + k)

    def remote(src, dst, send, recv, device):
        return pltpu.make_async_remote_copy(
            src_ref=src, dst_ref=dst, send_sem=send, recv_sem=recv, device_id=device, device_id_type=MESH
        )

    parts = (part_up, part_down, part_cross)
    loads = [pltpu.make_async_copy(home_hbm, home, load_sem.at[0])]
    for i, (start, n) in enumerate(PARTS):
        loads.append(pltpu.make_async_copy(part_hbm.at[:, pl.ds(start, n)], parts[i], load_sem.at[1 + i]))
    others = ((lroot_hbm.at[c], lroot.at[c, k]), (rroot_hbm.at[c], rroot.at[c, k]), (first_hbm, first), (second_hbm, second))
    for i, (src, dst) in enumerate(others):
        loads.append(pltpu.make_async_copy(src, dst, load_sem.at[4 + i]))
    for load in loads[:4]:
        load.start()

    barrier = pltpu.get_barrier_semaphore()
    greeted = [partner, across] + [along_y(j) for j in (1, 2, 3)] + [along_mp(a, b) for a, b in PEERS]
    for device in greeted:
        pl.semaphore_signal(barrier, inc=1, device_id=device, device_id_type=MESH)
    pl.semaphore_wait(barrier, len(greeted))

    root_copies = []

    def send_roots(wanted):
        for i, (a, b) in enumerate(PEERS):
            if a == wanted:
                there = chip_at(a, b)
                for w, (src, dst) in enumerate(((lroot_hbm, lroot), (rroot_hbm, rroot))):
                    copy = remote(
                        src.at[there], dst.at[c, k], root_send.at[w, i], root_recv.at[w, i], along_mp(a, b)
                    )
                    copy.start()
                    root_copies.append(copy)

    def source(q):
        return functools.reduce(jnp.maximum, [jnp.where(home[r] == q, r, 0) for r in range(NB)])

    def own_piece(w, to_x, j):
        row = source(to_x * NY + (y + j) % NY)
        return lambda t, r: parts[w][row, pl.ds(r, STRIDE), pl.ds(t * LANES, LANES)]

    to_xs = (1 - xl, xl)
    along = (1, -1)
    ring = {}

    def send_ring(kind, w, o, to, step, arrived):
        n = (kind * 2 + w) * 2 + o
        own = own_piece(w, to_xs[o], to)
        if arrived:
            encode_piece(RING, sum_of(RING, own, arrived), ring_out.at[n], work)
        else:
            encode_piece(RING, own, ring_out.at[n])
        ring[kind, w, o] = remote(
            ring_out.at[n], ring_in.at[n], ring_send.at[n], ring_recv.at[n], along_y(step % NY)
        )
        ring[kind, w, o].start()

    def got(kind, w, o):
        ring[kind, w, o].wait_recv()
        return ring_in.at[(kind * 2 + w) * 2 + o]

    def send_far(w, o):
        send_ring(0, w, o, 2, along[w], [])

    def send_back(w, o):
        send_ring(1, w, o, -along[w], -along[w], [])

    def send_on(w, o):
        send_ring(2, w, o, along[w], along[w], [got(0, w, o)])

    send_roots(0)
    loads[0].wait()
    loads[1].wait()
    send_far(0, 0)
    loads[2].wait()
    send_far(1, 0)
    loads[3].wait()
    x1_copies, y2_copies, x2_copies = {}, {}, {}
    for j in (2, 1, 3, 0):
        encode_piece(CROSS, own_piece(2, 1 - xl, j), x1_out.at[j])
        x1_copies[j] = remote(x1_out.at[j], x1_in.at[j], x1_send.at[j], x1_recv.at[j], across)
        x1_copies[j].start()
        if j == 2:
            for w in range(2):
                send_far(w, 1)
    for load in loads[4:]:
        load.start()
    send_roots(1)
    send_back(1, 0)
    send_back(0, 0)
    send_on(0, 0)
    send_on(1, 0)
    send_back(1, 1)
    send_back(0, 1)
    send_on(0, 1)
    send_on(1, 1)
    for j in (2, 1, 3):
        x1_copies[j].wait_recv()
        read = sum_of(CROSS, own_piece(2, xl, j), [x1_in.at[j]])
        encode_piece(CROSS, read, y2_out.at[j - 1], work)
        y2_copies[j] = remote(y2_out.at[j - 1], y2_in.at[j - 1], s2_send.at[j], s2_recv.at[j], along_y(j))
        y2_copies[j].start()
    for w in range(2):
        read = sum_of(RING, own_piece(w, 1 - xl, 0), [got(1, w, 0), got(2, w, 0)])
        encode_piece(RING, read, x2_out.at[w], work)
        x2_copies[w] = remote(x2_out.at[w], x2_in.at[w], s2_send.at[4 * w], s2_recv.at[4 * w], across)
        x2_copies[w].start()

    for copy in root_copies:
        copy.wait_recv()
    loads[4].wait()
    loads[5].wait()
    core_copies = []
    for w, ref in enumerate((lroot, rroot)):
        copy = remote(ref.at[:, k], ref.at[:, k], core_send.at[w], core_recv.at[w], partner)
        copy.start()
        core_copies.append(copy)

    strip = pl.ds(pl.multiple_of(k * H, H), H)
    block_copies = {}

    def finish(w, arrived):
        start, n = PARTS[w]
        read = sum_of(n, own_piece(w, xl, 0), arrived)

        def step(i, carry):
            r = pl.multiple_of(i * STRIDE, STRIDE)
            for t in range(H // LANES):
                mine = pl.ds(pl.multiple_of(k * H + t * LANES, LANES), LANES)
                high, low = split(read(t, r))
                ghigh[pl.ds(start + r, STRIDE), mine] = high
                glow[pl.ds(start + r, STRIDE), mine] = low
            return carry

        lax.fori_loop(0, n // STRIDE, step, 0)
        for i, ref in enumerate((ghigh, glow)):
            here = ref.at[pl.ds(start, n), strip]
            n_sem = 2 + 2 * w + i
            block_copies[w, i] = remote(here, here, core_send.at[n_sem], core_recv.at[n_sem], partner)
            block_copies[w, i].start()

    def rows_for(there):
        return pl.ds(pl.multiple_of(there * 2 * S + k * S, S), S)

    def row_copy(there, slot):
        return remote(
            grow_out.at[there], grow_in.at[slot], row_send.at[0, there], row_recv.at[0, slot], (d, there * 2 + k)
        )

    def send_rows(w):
        for i in range(2):
            block_copies[w, i].wait_recv()
        start, n = PARTS[w]
        for there in range(start // (2 * S), (start + n) // (2 * S)):
            rows = rows_for(there)
            value = ghigh[rows, :].astype(F32) + glow[rows, :].astype(F32)
            code = encode_rows(value, T, grow_out.at[there], 0)
            grow_out[there, pl.ds(WIDE, T), :] = code.astype(I32).astype(I16)

            @pl.when(c != there)
            def _():
                row_copy(there, c).start()

    for w in range(2):
        x2_copies[w].wait_recv()
        finish(w, [got(1, w, 1), got(2, w, 1), x2_in.at[w]])
        if w:
            send_rows(0)
    x1_copies[0].wait_recv()
    for j in (2, 1, 3):
        y2_copies[j].wait_recv()
    finish(2, [x1_in.at[0]] + [y2_in.at[n] for n in range(3)])
    send_rows(1)
    send_rows(2)
    grow_in[c] = grow_out[c]

    high_rows = jnp.concatenate([ghigh[rows_for(t), :] for t in range(NB)], axis=0)
    low_rows = jnp.concatenate([glow[rows_for(t), :] for t in range(NB)], axis=0)
    nt = ((1,), (1,))
    pleft[...] = dot(high_rows, ghigh[...], nt) + (dot(high_rows, glow[...], nt) + dot(low_rows, ghigh[...], nt))
    prod_copies = []

    def send_products(w, i, first, size):
        a, b = (PEERS + [(0, 0)])[i]
        here, there = prod_out.at[i, pl.ds(first, size)], prod_in.at[c, pl.ds(first, size)]
        if a or b:
            copy = remote(here, there, row_send.at[1 + w, i], row_recv.at[1 + w, i], along_mp(a, b))
            prod_copies.append(copy)
        else:
            copy = pltpu.make_async_copy(here, there, store_sem.at[w])
            stores.append(copy)
        copy.start()

    stores = []
    for i, (a, b) in enumerate(PEERS + [(0, 0)]):
        value = pleft[pl.ds(pl.multiple_of(chip_at(a, b) * S, S), S), :]
        left_codes[i] = encode_rows(value, T // 2, prod_out.at[i], 0)
        send_products(0, i, 0, WIDE)
    tn = ((0,), (0,))
    pright[...] = dot(ghigh[...], ghigh[...], tn) + (
        dot(ghigh[...], glow[...], tn) + dot(glow[...], ghigh[...], tn)
    )
    for i, (a, b) in enumerate(PEERS + [(0, 0)]):
        code = encode_rows(pright[rows_for(chip_at(a, b)), :], T // 2, prod_out.at[i], WIDE)
        codes = jnp.concatenate([left_codes[i], code], axis=0)
        prod_out[i, pl.ds(2 * WIDE, T), :] = codes.astype(I32).astype(I16)

    loads[6].wait()
    loads[7].wait()
    sum_copies = []
    for i, (a, b) in enumerate(PEERS + [(0, 0)]):
        slot = chip_at(-a, -b)
        if a or b:
            row_copy(slot, slot).wait_recv()
        total = jnp.zeros((8, LANES), F32)
        scale = scale_of(grow_in[slot, pl.ds(WIDE, T), :])
        for t, grad in enumerate(decode_rows(grow_in.at[slot], 0, scale)):
            cols = pl.ds(t * LANES, LANES)
            mean = FIRST_DECAY * first[slot, :, cols] + (1.0 - FIRST_DECAY) * grad
            square = SECOND_DECAY * second[slot, :, cols] + (1.0 - SECOND_DECAY) * grad * grad
            new_first[slot, :, cols] = mean
            new_second[slot, :, cols] = square
            adam = mean / (jnp.sqrt(square) + ADAM_EPS)
            total = total + fold(adam * adam)
        sums_out[i] = total
        if a or b:
            copy = remote(sums_out.at[i], sums_in.at[i], sum_send.at[i], sum_recv.at[i], along_mp(-a, -b))
            copy.start()
            sum_copies.append(copy)
    for i in range(NB):
        send_products(1, i, WIDE, WIDE + T)

    for copy in core_copies:
        copy.wait_recv()
    rcols = jnp.concatenate([rroot[a, b, :, strip] for a in range(NB) for b in range(2)], axis=0)
    inner = dot(ghigh[...], rcols) + dot(glow[...], rcols)
    inner_high, inner_low = split(inner)
    lrows = lroot[...].reshape(B, B)
    applied = dot(lrows, inner_high) + dot(lrows, inner_low)
    pright[:, pl.ds(0, H)] = applied
    pair_out[1] = fold(applied * applied)

    total = sums_out[len(PEERS)]
    for i, copy in enumerate(sum_copies):
        copy.wait_recv()
        total = total + sums_in[i]
    pair_out[0] = total
    pair_copy = remote(pair_out, pair_in, sum_send.at[len(PEERS)], sum_recv.at[len(PEERS)], partner)
    pair_copy.start()
    pair_copy.wait_recv()
    norms = [jnp.sum(pair_out[w] + pair_in[w], axis=(0, 1), keepdims=True) for w in range(2)]
    graft = jnp.sqrt(norms[0]) / (jnp.sqrt(norms[1]) + NORM_EPS)
    update[...] = (pright[:, pl.ds(0, H)] * graft).astype(BF16)

    for copy in prod_copies:
        copy.wait_recv()
    for a, b in PEERS:
        row_copy(chip_at(a, b), c).wait_send()
    for copies in (x1_copies, y2_copies, x2_copies, ring, block_copies):
        for copy in copies.values():
            copy.wait_send()
    for copy in [pair_copy] + root_copies + core_copies + prod_copies + sum_copies:
        copy.wait_send()
    for store in stores:
        store.wait()


def finish_kernel(
    prod, left, right, first, second, update,
    left_out, right_out, first_out, second_out, update_out,
    new_left, new_right, sem,
):
    through = [(first, first_out), (second, second_out), (update, update_out)]
    stats = [(new_left, left_out), (new_right, right_out)]
    stores = [pltpu.make_async_copy(src, dst, sem.at[i]) for i, (src, dst) in enumerate(stats + through)]
    for store in stores[2:]:
        store.start()
    for w, (old, new) in enumerate(((left, new_left), (right, new_right))):

        def add(slot, carry):
            code = prod[slot, pl.ds(2 * WIDE, T), :].astype(F32)[w * (T // 2) : (w + 1) * (T // 2)]
            scale = jnp.exp(code * STEP) * (1.0 / FULL)
            for t, value in enumerate(decode_rows(prod.at[slot], w * WIDE, scale)):
                cols = pl.ds(t * LANES, LANES)
                new[slot, :, cols] = old[slot, :, cols] + value
            return carry

        lax.fori_loop(0, NB, add, 0)
        stores[w].start()
    for store in stores:
        store.wait()


def on_device(
    grad_parts, home, left_stat, right_stat, left_root, right_root, first_moment, second_moment
):
    in_hbm = pl.BlockSpec(memory_space=pltpu.HBM)
    in_vmem = pl.BlockSpec(memory_space=pltpu.VMEM)
    n = len(PEERS)
    ring_piece = (H // LANES * RING + T, LANES)
    cross_piece = (H // LANES * CROSS + T, LANES)
    rows = (WIDE + T, LANES)
    products = (2 * WIDE + T, LANES)
    stat = pltpu.VMEM((NB, S, B), F32)
    tile = pltpu.VMEM((B, H), BF16)
    dma = pltpu.SemaphoreType.DMA
    scratch = [
        pltpu.SMEM((NB,), I32),
        *[pltpu.VMEM((NB, size, H), F32) for _, size in PARTS],
        *[stat] * 2,
        *[pltpu.VMEM((NB, 2, S, B), BF16)] * 2,
        *[pltpu.VMEM((12, *ring_piece), I16)] * 2,
        *[pltpu.VMEM((4, *cross_piece), I16)] * 2,
        *[pltpu.VMEM((3, *cross_piece), I16)] * 2,
        *[pltpu.VMEM((2, *ring_piece), I16)] * 2,
        pltpu.VMEM((B, H), F32),
        *[pltpu.VMEM((B, B), BF16)] * 2,
        *[pltpu.VMEM((NB, *rows), I16)] * 2,
        pltpu.VMEM((NB, *products), I16),
        pltpu.VMEM((NB, T // 2, LANES), F32),
        pltpu.VMEM((H, B), F32),
        pltpu.VMEM((B, B), F32),
        pltpu.VMEM((NB, 8, LANES), F32),
        pltpu.VMEM((n, 8, LANES), F32),
        *[pltpu.VMEM((2, 8, LANES), F32)] * 2,
        dma((8,)),
        *[dma((2, n))] * 2,
        *[dma((12,))] * 2,
        *[dma((4,))] * 2,
        *[dma((5,))] * 2,
        *[dma((8,))] * 2,
        *[dma((3, NB))] * 2,
        *[dma((n + 1,))] * 2,
        dma((2,)),
    ]
    made = pl.pallas_call(
        kernel,
        out_shape=(pltpu.VMEM((NB, *products), I16), stat, stat, tile),
        in_specs=[in_hbm] * 6,
        out_specs=[in_vmem] * 4,
        scratch_shapes=scratch,
        compiler_params=pltpu.CompilerParams(
            collective_id=0, has_side_effects=True, vmem_limit_bytes=40 * 2**20
        ),
        cost_estimate=pl.CostEstimate(flops=2 * 10**9, bytes_accessed=9 * 2**20, transcendentals=0),
        name="shampoo_step",
    )(
        *[
            pltpu.with_memory_space_constraint(x, pltpu.HBM)
            for x in (home, grad_parts.reshape(NB, B, H), left_root, right_root, first_moment, second_moment)
        ]
    )
    stat_out = jax.ShapeDtypeStruct((NB, S, B), F32)
    return pl.pallas_call(
        finish_kernel,
        out_shape=(stat_out,) * 4 + (jax.ShapeDtypeStruct((B, H), BF16),),
        in_specs=[in_vmem] * 6,
        out_specs=[in_hbm] * 5,
        scratch_shapes=[stat, stat, dma((5,))],
        compiler_params=pltpu.CompilerParams(vmem_limit_bytes=16 * 2**20),
        name="finish_outputs",
    )(made[0], left_stat, right_stat, *made[1:])


def solution(mesh):
    rows = P("dp", "mp", None)
    in_specs = (P("dp", None, "mp"), P(), rows, rows, rows, rows, rows, rows)
    out_specs = (rows, rows, rows, rows, P("dp", "mp"))
    return jax.shard_map(
        on_device, mesh=mesh, in_specs=in_specs, out_specs=out_specs, check_vma=False
    )
```

```python
import functools
import math

import jax
import jax.numpy as jnp
from jax import lax
from jax.experimental import pallas as pl
from jax.experimental.pallas import tpu as pltpu
from jax.sharding import PartitionSpec as P

FIRST_DECAY = 0.9
SECOND_DECAY = 0.999
ADAM_EPS = 1e-08
NORM_EPS = 1e-06
MESH = pl.DeviceIdType.MESH
F32 = jnp.float32
BF16 = jnp.bfloat16
I16 = jnp.int16
I32 = jnp.int32

B = 512
H = 256
PARTS = ((0, 192), (192, 192), (384, 128))
RING = PARTS[0][1]
CROSS = PARTS[2][1]
S = 32
T = 16
STRIDE = 64
LANES = 128
WIDE = B // LANES * S
NB = 8
NY = 4
FULL = 32760.0
STEP = math.log(2.0) / 4.0
TINY = 1e-30

PEERS = [(1, 2), (1, 1), (1, 3), (0, 2), (1, 0), (0, 1), (0, 3)]


def code_of(peak):
    return jnp.ceil(jnp.log(jnp.maximum(peak, TINY)) * (1.0 / STEP))


def coded(x):
    return jnp.floor(x + 0.5).astype(I32).astype(I16)


def scale_of(code):
    return jnp.exp(code.astype(I32).astype(F32) * STEP) * (1.0 / FULL)


def decoded(values, scale):
    return values.astype(I32).astype(F32) * scale


def encode_piece(n, read, out, keep=None):
    tiles = range(H // LANES)

    def look(i, peak):
        r = pl.multiple_of(i * STRIDE, STRIDE)
        for t in tiles:
            x = read(t, r)
            if keep is not None:
                keep[pl.ds(r, STRIDE), pl.ds(t * LANES, LANES)] = x
            peak = jnp.maximum(peak, jnp.max(jnp.abs(x).reshape(STRIDE // T, T, LANES), axis=0))
        return peak

    code = code_of(lax.fori_loop(0, n // STRIDE, look, jnp.zeros((T, LANES), F32)))
    factor = jnp.exp(code * -STEP) * FULL

    def write(i, carry):
        r = pl.multiple_of(i * STRIDE, STRIDE)
        for t in tiles:
            x = read(t, r) if keep is None else keep[pl.ds(r, STRIDE), pl.ds(t * LANES, LANES)]
            x = x.reshape(STRIDE // T, T, LANES) * factor[None]
            out[pl.ds(t * n + r, STRIDE), :] = coded(x).reshape(STRIDE, LANES)
        return carry

    lax.fori_loop(0, n // STRIDE, write, 0)
    out[pl.ds(H // LANES * n, T), :] = code.astype(I32).astype(I16)


def sum_of(n, own, arrived):
    scales = [scale_of(ref[pl.ds(H // LANES * n, T), :])[None] for ref in arrived]

    def read(t, r):
        x = own(t, r)
        for ref, scale in zip(arrived, scales):
            values = ref[pl.ds(t * n + r, STRIDE), :].reshape(STRIDE // T, T, LANES)
            x = x + decoded(values, scale).reshape(STRIDE, LANES)
        return x

    return read


def encode_rows(x, group, out, first):
    n = B // LANES
    parts = [x[:, t * LANES : (t + 1) * LANES].reshape(S // group, group, LANES) for t in range(n)]
    code = code_of(functools.reduce(jnp.maximum, [jnp.max(jnp.abs(p), axis=0) for p in parts]))
    factor = jnp.exp(code * -STEP) * FULL
    for t in range(n):
        out[pl.ds(first + t * S, S), :] = coded(parts[t] * factor[None]).reshape(S, LANES)
    return code


def decode_rows(codes, first, scale):
    group = scale.shape[0]
    return [
        decoded(codes[pl.ds(first + t * S, S), :].reshape(S // group, group, LANES), scale[None]).reshape(S, LANES)
        for t in range(B // LANES)
    ]


def dot(a, b, dims=((1,), (0,))):
    return lax.dot_general(a, b, (dims, ((), ())), preferred_element_type=F32)


def split(x):
    high = x.astype(BF16)
    return high, (x - high.astype(F32)).astype(BF16)


def fold(x):
    r, c = x.shape
    x = jnp.sum(x.reshape(r // 8, 8, c), axis=0)
    return functools.reduce(jnp.add, [x[:, t * LANES : (t + 1) * LANES] for t in range(c // LANES)])


def kernel(
    home_hbm, part_hbm, lroot_hbm, rroot_hbm, first_hbm, second_hbm,
    prod_in, new_first, new_second, update,
    home, part_up, part_down, part_cross, first, second, lroot, rroot,
    ring_out, ring_in, x1_out, x1_in, y2_out, y2_in, x2_out, x2_in,
    work, ghigh, glow, grow_out, grow_in, prod_out, left_codes, pleft, pright,
    sums_out, sums_other, sums_chip, sums_in, pair_out, pair_in,
    load_sem, root_send, root_recv, ring_send, ring_recv, x1_send, x1_recv, s2_send, s2_recv,
    core_send, core_recv, row_send, row_recv, sum_send, sum_recv, store_sem,
):
    d = lax.axis_index("dp")
    m = lax.axis_index("mp")
    xl, y = d // NY, d % NY
    xh, z, k = m // 8, (m // 2) % 4, m % 2
    c = m // 2

    partner = (d, m + 1 - 2 * k)
    across = ((1 - xl) * NY + y, m)

    def along_y(j):
        return (xl * NY + (y + j) % NY, m)

    def chip_at(a, b):
        return ((xh + a) % 2) * 4 + (z + b) % 4

    def along_mp(a, b):
        return (d, chip_at(a, b) * 2 + k)

    def remote(src, dst, send, recv, device):
        return pltpu.make_async_remote_copy(
            src_ref=src, dst_ref=dst, send_sem=send, recv_sem=recv, device_id=device, device_id_type=MESH
        )

    parts = (part_up, part_down, part_cross)
    loads = [pltpu.make_async_copy(home_hbm, home, load_sem.at[0])]
    for i, (start, n) in enumerate(PARTS):
        loads.append(pltpu.make_async_copy(part_hbm.at[:, pl.ds(start, n)], parts[i], load_sem.at[1 + i]))
    others = ((lroot_hbm.at[c], lroot.at[c, k]), (rroot_hbm.at[c], rroot.at[c, k]), (first_hbm, first), (second_hbm, second))
    for i, (src, dst) in enumerate(others):
        loads.append(pltpu.make_async_copy(src, dst, load_sem.at[4 + i]))
    for load in loads[:4]:
        load.start()

    barrier = pltpu.get_barrier_semaphore()
    greeted = [partner, across] + [along_y(j) for j in (1, 2, 3)] + [along_mp(a, b) for a, b in PEERS]
    for device in greeted:
        pl.semaphore_signal(barrier, inc=1, device_id=device, device_id_type=MESH)
    pl.semaphore_wait(barrier, len(greeted))

    root_copies = []

    def send_roots(wanted):
        for i, (a, b) in enumerate(PEERS):
            if a == wanted:
                there = chip_at(a, b)
                for w, (src, dst) in enumerate(((lroot_hbm, lroot), (rroot_hbm, rroot))):
                    copy = remote(
                        src.at[there], dst.at[c, k], root_send.at[w, i], root_recv.at[w, i], along_mp(a, b)
                    )
                    copy.start()
                    root_copies.append(copy)

    def source(q):
        return functools.reduce(jnp.maximum, [jnp.where(home[r] == q, r, 0) for r in range(NB)])

    def own_piece(w, to_x, j):
        row = source(to_x * NY + (y + j) % NY)
        return lambda t, r: parts[w][row, pl.ds(r, STRIDE), pl.ds(t * LANES, LANES)]

    to_xs = (1 - xl, xl)
    along = (1, -1)
    ring = {}

    def send_ring(kind, w, o, to, step, arrived):
        n = (kind * 2 + w) * 2 + o
        own = own_piece(w, to_xs[o], to)
        if arrived:
            encode_piece(RING, sum_of(RING, own, arrived), ring_out.at[n], work)
        else:
            encode_piece(RING, own, ring_out.at[n])
        ring[kind, w, o] = remote(
            ring_out.at[n], ring_in.at[n], ring_send.at[n], ring_recv.at[n], along_y(step % NY)
        )
        ring[kind, w, o].start()

    def got(kind, w, o):
        ring[kind, w, o].wait_recv()
        return ring_in.at[(kind * 2 + w) * 2 + o]

    def send_far(w, o):
        send_ring(0, w, o, 2, along[w], [])

    def send_back(w, o):
        send_ring(1, w, o, -along[w], -along[w], [])

    def send_on(w, o):
        send_ring(2, w, o, along[w], along[w], [got(0, w, o)])

    send_roots(0)
    loads[0].wait()
    loads[1].wait()
    send_far(0, 0)
    loads[2].wait()
    send_far(1, 0)
    loads[3].wait()
    x1_copies, y2_copies, x2_copies = {}, {}, {}
    for j in (2, 1, 3, 0):
        encode_piece(CROSS, own_piece(2, 1 - xl, j), x1_out.at[j])
        x1_copies[j] = remote(x1_out.at[j], x1_in.at[j], x1_send.at[j], x1_recv.at[j], across)
        x1_copies[j].start()
        if j == 2:
            for w in range(2):
                send_far(w, 1)
    for load in loads[4:]:
        load.start()
    send_roots(1)
    send_back(1, 0)
    send_back(0, 0)
    send_on(0, 0)
    send_on(1, 0)
    send_back(1, 1)
    send_back(0, 1)
    send_on(0, 1)
    send_on(1, 1)
    for j in (2, 1, 3):
        x1_copies[j].wait_recv()
        read = sum_of(CROSS, own_piece(2, xl, j), [x1_in.at[j]])
        encode_piece(CROSS, read, y2_out.at[j - 1], work)
        y2_copies[j] = remote(y2_out.at[j - 1], y2_in.at[j - 1], s2_send.at[j], s2_recv.at[j], along_y(j))
        y2_copies[j].start()
    for w in range(2):
        read = sum_of(RING, own_piece(w, 1 - xl, 0), [got(1, w, 0), got(2, w, 0)])
        encode_piece(RING, read, x2_out.at[w], work)
        x2_copies[w] = remote(x2_out.at[w], x2_in.at[w], s2_send.at[4 * w], s2_recv.at[4 * w], across)
        x2_copies[w].start()

    for copy in root_copies:
        copy.wait_recv()
    loads[4].wait()
    loads[5].wait()
    core_copies = []
    for w, ref in enumerate((lroot, rroot)):
        copy = remote(ref.at[:, k], ref.at[:, k], core_send.at[w], core_recv.at[w], partner)
        copy.start()
        core_copies.append(copy)

    strip = pl.ds(pl.multiple_of(k * H, H), H)
    block_copies = {}

    def finish(w, arrived):
        start, n = PARTS[w]
        read = sum_of(n, own_piece(w, xl, 0), arrived)

        def step(i, carry):
            r = pl.multiple_of(i * STRIDE, STRIDE)
            for t in range(H // LANES):
                mine = pl.ds(pl.multiple_of(k * H + t * LANES, LANES), LANES)
                high, low = split(read(t, r))
                ghigh[pl.ds(start + r, STRIDE), mine] = high
                glow[pl.ds(start + r, STRIDE), mine] = low
            return carry

        lax.fori_loop(0, n // STRIDE, step, 0)
        for i, ref in enumerate((ghigh, glow)):
            here = ref.at[pl.ds(start, n), strip]
            n_sem = 2 + 2 * w + i
            block_copies[w, i] = remote(here, here, core_send.at[n_sem], core_recv.at[n_sem], partner)
            block_copies[w, i].start()

    def rows_for(there):
        return pl.ds(pl.multiple_of(there * 2 * S + k * S, S), S)

    def row_copy(there, slot):
        return remote(
            grow_out.at[there], grow_in.at[slot], row_send.at[0, there], row_recv.at[0, slot], (d, there * 2 + k)
        )

    def send_rows(w):
        for i in range(2):
            block_copies[w, i].wait_recv()
        start, n = PARTS[w]
        for there in range(start // (2 * S), (start + n) // (2 * S)):
            rows = rows_for(there)
            value = ghigh[rows, :].astype(F32) + glow[rows, :].astype(F32)
            code = encode_rows(value, T, grow_out.at[there], 0)
            grow_out[there, pl.ds(WIDE, T), :] = code.astype(I32).astype(I16)

            @pl.when(c != there)
            def _():
                row_copy(there, c).start()

    for w in range(2):
        x2_copies[w].wait_recv()
        finish(w, [got(1, w, 1), got(2, w, 1), x2_in.at[w]])
        if w:
            send_rows(0)
    x1_copies[0].wait_recv()
    for j in (2, 1, 3):
        y2_copies[j].wait_recv()
    finish(2, [x1_in.at[0]] + [y2_in.at[n] for n in range(3)])
    send_rows(1)
    send_rows(2)
    grow_in[c] = grow_out[c]

    high_rows = jnp.concatenate([ghigh[rows_for(t), :] for t in range(NB)], axis=0)
    low_rows = jnp.concatenate([glow[rows_for(t), :] for t in range(NB)], axis=0)
    nt = ((1,), (1,))
    pleft[...] = dot(high_rows, ghigh[...], nt) + (dot(high_rows, glow[...], nt) + dot(low_rows, ghigh[...], nt))
    prod_copies = []

    def send_products(w, i, first, size):
        a, b = (PEERS + [(0, 0)])[i]
        here, there = prod_out.at[i, pl.ds(first, size)], prod_in.at[c, pl.ds(first, size)]
        if a or b:
            copy = remote(here, there, row_send.at[1 + w, i], row_recv.at[1 + w, i], along_mp(a, b))
            prod_copies.append(copy)
        else:
            copy = pltpu.make_async_copy(here, there, store_sem.at[w])
            stores.append(copy)
        copy.start()

    stores = []
    for i, (a, b) in enumerate(PEERS + [(0, 0)]):
        value = pleft[pl.ds(pl.multiple_of(chip_at(a, b) * S, S), S), :]
        left_codes[i] = encode_rows(value, T // 2, prod_out.at[i], 0)
        send_products(0, i, 0, WIDE)
    tn = ((0,), (0,))
    pright[...] = dot(ghigh[...], ghigh[...], tn) + (
        dot(ghigh[...], glow[...], tn) + dot(glow[...], ghigh[...], tn)
    )
    for i, (a, b) in enumerate(PEERS + [(0, 0)]):
        code = encode_rows(pright[rows_for(chip_at(a, b)), :], T // 2, prod_out.at[i], WIDE)
        codes = jnp.concatenate([left_codes[i], code], axis=0)
        prod_out[i, pl.ds(2 * WIDE, T), :] = codes.astype(I32).astype(I16)

    for i in range(NB):
        send_products(1, i, WIDE, WIDE + T)

    for copy in core_copies:
        copy.wait_recv()
    rcols = jnp.concatenate([rroot[a, b, :, strip] for a in range(NB) for b in range(2)], axis=0)
    inner = dot(ghigh[...], rcols) + dot(glow[...], rcols)
    inner_high, inner_low = split(inner)
    lrows = lroot[...].reshape(B, B)
    applied = dot(lrows, inner_high) + dot(lrows, inner_low)
    pright[:, pl.ds(0, H)] = applied
    pair_out[...] = fold(applied * applied)
    n = len(PEERS)
    pair_copy = remote(pair_out, pair_in, sum_send.at[n], sum_recv.at[n], partner)
    pair_copy.start()

    loads[6].wait()
    loads[7].wait()
    for a, b in PEERS + [(0, 0)]:
        slot = chip_at(-a, -b)
        if a or b:
            row_copy(slot, slot).wait_recv()
        total = jnp.zeros((8, LANES), F32)
        scale = scale_of(grow_in[slot, pl.ds(WIDE, T), :])
        for t, grad in enumerate(decode_rows(grow_in.at[slot], 0, scale)):
            cols = pl.ds(t * LANES, LANES)
            mean = FIRST_DECAY * first[slot, :, cols] + (1.0 - FIRST_DECAY) * grad
            square = SECOND_DECAY * second[slot, :, cols] + (1.0 - SECOND_DECAY) * grad * grad
            new_first[slot, :, cols] = mean
            new_second[slot, :, cols] = square
            adam = mean / (jnp.sqrt(square) + ADAM_EPS)
            total = total + fold(adam * adam)
        sums_out[slot] = total

    chip_copy = remote(sums_out, sums_other, sum_send.at[n + 1], sum_recv.at[n + 1], partner)
    chip_copy.start()
    chip_copy.wait_recv()
    sums_chip[...] = sums_out[...] + sums_other[...]
    sum_copies = []
    for i, (a, b) in enumerate(PEERS):
        copy = remote(sums_chip.at[chip_at(a, b)], sums_in.at[i], sum_send.at[i], sum_recv.at[i], along_mp(a, b))
        copy.start()
        sum_copies.append(copy)

    pair_copy.wait_recv()
    total = sums_chip[c]
    for i, copy in enumerate(sum_copies):
        copy.wait_recv()
        total = total + sums_in[i]
    norms = [jnp.sum(x, axis=(0, 1), keepdims=True) for x in (total, pair_out[...] + pair_in[...])]
    graft = jnp.sqrt(norms[0]) / (jnp.sqrt(norms[1]) + NORM_EPS)
    update[...] = (pright[:, pl.ds(0, H)] * graft).astype(BF16)

    for copy in prod_copies:
        copy.wait_recv()
    for a, b in PEERS:
        row_copy(chip_at(a, b), c).wait_send()
    for copies in (x1_copies, y2_copies, x2_copies, ring, block_copies):
        for copy in copies.values():
            copy.wait_send()
    for copy in [pair_copy, chip_copy] + root_copies + core_copies + prod_copies + sum_copies:
        copy.wait_send()
    for store in stores:
        store.wait()


def finish_kernel(
    prod, left, right, first, second, update,
    left_out, right_out, first_out, second_out, update_out,
    new_left, new_right, sem,
):
    through = [(first, first_out), (second, second_out), (update, update_out)]
    stats = [(new_left, left_out), (new_right, right_out)]
    stores = [pltpu.make_async_copy(src, dst, sem.at[i]) for i, (src, dst) in enumerate(stats + through)]
    for store in stores[2:]:
        store.start()
    for w, (old, new) in enumerate(((left, new_left), (right, new_right))):

        def add(slot, carry):
            code = prod[slot, pl.ds(2 * WIDE, T), :].astype(F32)[w * (T // 2) : (w + 1) * (T // 2)]
            scale = jnp.exp(code * STEP) * (1.0 / FULL)
            for t, value in enumerate(decode_rows(prod.at[slot], w * WIDE, scale)):
                cols = pl.ds(t * LANES, LANES)
                new[slot, :, cols] = old[slot, :, cols] + value
            return carry

        lax.fori_loop(0, NB, add, 0)
        stores[w].start()
    for store in stores:
        store.wait()


def on_device(
    grad_parts, home, left_stat, right_stat, left_root, right_root, first_moment, second_moment
):
    in_hbm = pl.BlockSpec(memory_space=pltpu.HBM)
    in_vmem = pl.BlockSpec(memory_space=pltpu.VMEM)
    n = len(PEERS)
    ring_piece = (H // LANES * RING + T, LANES)
    cross_piece = (H // LANES * CROSS + T, LANES)
    rows = (WIDE + T, LANES)
    products = (2 * WIDE + T, LANES)
    stat = pltpu.VMEM((NB, S, B), F32)
    tile = pltpu.VMEM((B, H), BF16)
    dma = pltpu.SemaphoreType.DMA
    scratch = [
        pltpu.SMEM((NB,), I32),
        *[pltpu.VMEM((NB, size, H), F32) for _, size in PARTS],
        *[stat] * 2,
        *[pltpu.VMEM((NB, 2, S, B), BF16)] * 2,
        *[pltpu.VMEM((12, *ring_piece), I16)] * 2,
        *[pltpu.VMEM((4, *cross_piece), I16)] * 2,
        *[pltpu.VMEM((3, *cross_piece), I16)] * 2,
        *[pltpu.VMEM((2, *ring_piece), I16)] * 2,
        pltpu.VMEM((B, H), F32),
        *[pltpu.VMEM((B, B), BF16)] * 2,
        *[pltpu.VMEM((NB, *rows), I16)] * 2,
        pltpu.VMEM((NB, *products), I16),
        pltpu.VMEM((NB, T // 2, LANES), F32),
        pltpu.VMEM((H, B), F32),
        pltpu.VMEM((B, B), F32),
        *[pltpu.VMEM((NB, 8, LANES), F32)] * 3,
        pltpu.VMEM((n, 8, LANES), F32),
        *[pltpu.VMEM((8, LANES), F32)] * 2,
        dma((8,)),
        *[dma((2, n))] * 2,
        *[dma((12,))] * 2,
        *[dma((4,))] * 2,
        *[dma((5,))] * 2,
        *[dma((8,))] * 2,
        *[dma((3, NB))] * 2,
        *[dma((n + 2,))] * 2,
        dma((2,)),
    ]
    made = pl.pallas_call(
        kernel,
        out_shape=(pltpu.VMEM((NB, *products), I16), stat, stat, tile),
        in_specs=[in_hbm] * 6,
        out_specs=[in_vmem] * 4,
        scratch_shapes=scratch,
        compiler_params=pltpu.CompilerParams(
            collective_id=0, has_side_effects=True, vmem_limit_bytes=40 * 2**20
        ),
        cost_estimate=pl.CostEstimate(flops=2 * 10**9, bytes_accessed=9 * 2**20, transcendentals=0),
        name="shampoo_step",
    )(
        *[
            pltpu.with_memory_space_constraint(x, pltpu.HBM)
            for x in (home, grad_parts.reshape(NB, B, H), left_root, right_root, first_moment, second_moment)
        ]
    )
    stat_out = jax.ShapeDtypeStruct((NB, S, B), F32)
    return pl.pallas_call(
        finish_kernel,
        out_shape=(stat_out,) * 4 + (jax.ShapeDtypeStruct((B, H), BF16),),
        in_specs=[in_vmem] * 6,
        out_specs=[in_hbm] * 5,
        scratch_shapes=[stat, stat, dma((5,))],
        compiler_params=pltpu.CompilerParams(vmem_limit_bytes=16 * 2**20),
        name="finish_outputs",
    )(made[0], left_stat, right_stat, *made[1:])


def solution(mesh):
    rows = P("dp", "mp", None)
    in_specs = (P("dp", None, "mp"), P(), rows, rows, rows, rows, rows, rows)
    out_specs = (rows, rows, rows, rows, P("dp", "mp"))
    return jax.shard_map(
        on_device, mesh=mesh, in_specs=in_specs, out_specs=out_specs, check_vma=False
    )
```

```python
import functools
import math

import jax
import jax.numpy as jnp
from jax import lax
from jax.experimental import pallas as pl
from jax.experimental.pallas import tpu as pltpu
from jax.sharding import PartitionSpec as P

FIRST_DECAY = 0.9
SECOND_DECAY = 0.999
ADAM_EPS = 1e-08
NORM_EPS = 1e-06
MESH = pl.DeviceIdType.MESH
F32 = jnp.float32
BF16 = jnp.bfloat16
I16 = jnp.int16
I32 = jnp.int32

B = 512
H = 256
PARTS = ((0, 192), (192, 192), (384, 128))
RING = PARTS[0][1]
CROSS = PARTS[2][1]
S = 32
T = 16
STRIDE = 64
LANES = 128
WIDE = B // LANES * S
NB = 8
NY = 4
FULL = 32760.0
STEP = math.log(2.0) / 4.0
TINY = 1e-30

PEERS = [(1, 2), (1, 1), (1, 3), (0, 2), (1, 0), (0, 1), (0, 3)]


def code_of(peak):
    return jnp.ceil(jnp.log(jnp.maximum(peak, TINY)) * (1.0 / STEP))


def coded(x):
    return jnp.floor(x + 0.5).astype(I32).astype(I16)


def scale_of(code):
    return jnp.exp(code.astype(I32).astype(F32) * STEP) * (1.0 / FULL)


def decoded(values, scale):
    return values.astype(I32).astype(F32) * scale


def encode_piece(n, read, out, keep=None):
    tiles = range(H // LANES)

    def look(i, peak):
        r = pl.multiple_of(i * STRIDE, STRIDE)
        for t in tiles:
            x = read(t, r)
            if keep is not None:
                keep[pl.ds(r, STRIDE), pl.ds(t * LANES, LANES)] = x
            peak = jnp.maximum(peak, jnp.max(jnp.abs(x).reshape(STRIDE // T, T, LANES), axis=0))
        return peak

    code = code_of(lax.fori_loop(0, n // STRIDE, look, jnp.zeros((T, LANES), F32)))
    factor = jnp.exp(code * -STEP) * FULL

    def write(i, carry):
        r = pl.multiple_of(i * STRIDE, STRIDE)
        for t in tiles:
            x = read(t, r) if keep is None else keep[pl.ds(r, STRIDE), pl.ds(t * LANES, LANES)]
            x = x.reshape(STRIDE // T, T, LANES) * factor[None]
            out[pl.ds(t * n + r, STRIDE), :] = coded(x).reshape(STRIDE, LANES)
        return carry

    lax.fori_loop(0, n // STRIDE, write, 0)
    out[pl.ds(H // LANES * n, T), :] = code.astype(I32).astype(I16)


def sum_of(n, own, arrived):
    scales = [scale_of(ref[pl.ds(H // LANES * n, T), :])[None] for ref in arrived]

    def read(t, r):
        x = own(t, r)
        for ref, scale in zip(arrived, scales):
            values = ref[pl.ds(t * n + r, STRIDE), :].reshape(STRIDE // T, T, LANES)
            x = x + decoded(values, scale).reshape(STRIDE, LANES)
        return x

    return read


def encode_rows(x, group, out, first):
    n = B // LANES
    parts = [x[:, t * LANES : (t + 1) * LANES].reshape(S // group, group, LANES) for t in range(n)]
    code = code_of(functools.reduce(jnp.maximum, [jnp.max(jnp.abs(p), axis=0) for p in parts]))
    factor = jnp.exp(code * -STEP) * FULL
    for t in range(n):
        out[pl.ds(first + t * S, S), :] = coded(parts[t] * factor[None]).reshape(S, LANES)
    return code


def decode_rows(codes, first, scale):
    group = scale.shape[0]
    return [
        decoded(codes[pl.ds(first + t * S, S), :].reshape(S // group, group, LANES), scale[None]).reshape(S, LANES)
        for t in range(B // LANES)
    ]


def dot(a, b, dims=((1,), (0,))):
    return lax.dot_general(a, b, (dims, ((), ())), preferred_element_type=F32)


def split(x):
    high = x.astype(BF16)
    return high, (x - high.astype(F32)).astype(BF16)


def fold(x):
    r, c = x.shape
    x = jnp.sum(x.reshape(r // 8, 8, c), axis=0)
    return functools.reduce(jnp.add, [x[:, t * LANES : (t + 1) * LANES] for t in range(c // LANES)])


def kernel(
    home_hbm, part_hbm, lroot_hbm, rroot_hbm, first_hbm, second_hbm,
    prod_in, new_first, new_second, update,
    home, part_up, part_down, part_cross, first, second, lroot, rroot,
    ring_out, ring_in, x1_out, x1_in, y2_out, y2_in, x2_out, x2_in,
    work, ghigh, glow, grow_out, grow_in, prod_out, left_codes, pleft, pright,
    sums_out, sums_other, sums_chip, sums_in, pair_out, pair_in,
    load_sem, root_send, root_recv, ring_send, ring_recv, x1_send, x1_recv, s2_send, s2_recv,
    core_send, core_recv, row_send, row_recv, sum_send, sum_recv, store_sem, ready,
):
    d = lax.axis_index("dp")
    m = lax.axis_index("mp")
    xl, y = d // NY, d % NY
    xh, z, k = m // 8, (m // 2) % 4, m % 2
    c = m // 2

    partner = (d, m + 1 - 2 * k)
    across = ((1 - xl) * NY + y, m)

    def along_y(j):
        return (xl * NY + (y + j) % NY, m)

    def chip_at(a, b):
        return ((xh + a) % 2) * 4 + (z + b) % 4

    def along_mp(a, b):
        return (d, chip_at(a, b) * 2 + k)

    def remote(src, dst, send, recv, device):
        return pltpu.make_async_remote_copy(
            src_ref=src, dst_ref=dst, send_sem=send, recv_sem=recv, device_id=device, device_id_type=MESH
        )

    parts = (part_up, part_down, part_cross)
    loads = [pltpu.make_async_copy(home_hbm, home, load_sem.at[0])]
    for i, (start, n) in enumerate(PARTS):
        loads.append(pltpu.make_async_copy(part_hbm.at[:, pl.ds(start, n)], parts[i], load_sem.at[1 + i]))
    others = ((lroot_hbm.at[c], lroot.at[c, k]), (rroot_hbm.at[c], rroot.at[c, k]), (first_hbm, first), (second_hbm, second))
    for i, (src, dst) in enumerate(others):
        loads.append(pltpu.make_async_copy(src, dst, load_sem.at[4 + i]))
    for load in loads[:4]:
        load.start()

    rank = 2 * z + xh

    def rank_of(there):
        return 2 * (there % 4) + there // 4

    barrier = pltpu.get_barrier_semaphore()
    for device in [across, partner] + [along_y(j) for j in (1, 2, 3)]:
        pl.semaphore_signal(barrier, inc=1, device_id=device, device_id_type=MESH)
    for a, b in PEERS:

        @pl.when(rank_of(chip_at(a, b)) > rank)
        def _():
            pl.semaphore_signal(barrier, inc=1, device_id=along_mp(a, b), device_id_type=MESH)

    pl.semaphore_wait(barrier, 5 + rank)
    for a, b in PEERS:

        @pl.when(rank_of(chip_at(a, b)) < rank)
        def _():
            pl.semaphore_signal(ready, inc=1, device_id=along_mp(a, b), device_id_type=MESH)

    root_copies = []
    for i, (a, b) in enumerate(PEERS):
        there = chip_at(a, b)
        for w, (src, dst) in enumerate(((lroot_hbm, lroot), (rroot_hbm, rroot))):
            root_copies.append(
                remote(src.at[there], dst.at[c, k], root_send.at[w, i], root_recv.at[w, i], along_mp(a, b))
            )

    def send_roots(higher):
        for i, (a, b) in enumerate(PEERS):
            there = rank_of(chip_at(a, b))

            @pl.when(there > rank if higher else there < rank)
            def _():
                for copy in root_copies[2 * i : 2 * i + 2]:
                    copy.start()

    def source(q):
        return functools.reduce(jnp.maximum, [jnp.where(home[r] == q, r, 0) for r in range(NB)])

    def own_piece(w, to_x, j):
        row = source(to_x * NY + (y + j) % NY)
        return lambda t, r: parts[w][row, pl.ds(r, STRIDE), pl.ds(t * LANES, LANES)]

    to_xs = (1 - xl, xl)
    along = (1, -1)
    ring = {}

    def send_ring(kind, w, o, to, step, arrived):
        n = (kind * 2 + w) * 2 + o
        own = own_piece(w, to_xs[o], to)
        if arrived:
            encode_piece(RING, sum_of(RING, own, arrived), ring_out.at[n], work)
        else:
            encode_piece(RING, own, ring_out.at[n])
        ring[kind, w, o] = remote(
            ring_out.at[n], ring_in.at[n], ring_send.at[n], ring_recv.at[n], along_y(step % NY)
        )
        ring[kind, w, o].start()

    def got(kind, w, o):
        ring[kind, w, o].wait_recv()
        return ring_in.at[(kind * 2 + w) * 2 + o]

    def send_far(w, o):
        send_ring(0, w, o, 2, along[w], [])

    def send_back(w, o):
        send_ring(1, w, o, -along[w], -along[w], [])

    def send_on(w, o):
        send_ring(2, w, o, along[w], along[w], [got(0, w, o)])

    loads[0].wait()
    loads[1].wait()
    send_far(0, 0)
    loads[2].wait()
    send_far(1, 0)
    loads[3].wait()
    x1_copies, y2_copies, x2_copies = {}, {}, {}
    for j in (2, 1, 3, 0):
        encode_piece(CROSS, own_piece(2, 1 - xl, j), x1_out.at[j])
        x1_copies[j] = remote(x1_out.at[j], x1_in.at[j], x1_send.at[j], x1_recv.at[j], across)
        x1_copies[j].start()
        if j == 2:
            for w in range(2):
                send_far(w, 1)
    for load in loads[4:]:
        load.start()
    send_roots(False)
    send_back(1, 0)
    send_back(0, 0)
    send_on(0, 0)
    send_on(1, 0)
    send_back(1, 1)
    send_back(0, 1)
    send_on(0, 1)
    send_on(1, 1)
    for j in (2, 1, 3):
        x1_copies[j].wait_recv()
        read = sum_of(CROSS, own_piece(2, xl, j), [x1_in.at[j]])
        encode_piece(CROSS, read, y2_out.at[j - 1], work)
        y2_copies[j] = remote(y2_out.at[j - 1], y2_in.at[j - 1], s2_send.at[j], s2_recv.at[j], along_y(j))
        y2_copies[j].start()

    @pl.when(rank < NB - 1)
    def _():
        pl.semaphore_wait(ready, NB - 1 - rank)

    send_roots(True)
    for w in range(2):
        read = sum_of(RING, own_piece(w, 1 - xl, 0), [got(1, w, 0), got(2, w, 0)])
        encode_piece(RING, read, x2_out.at[w], work)
        x2_copies[w] = remote(x2_out.at[w], x2_in.at[w], s2_send.at[4 * w], s2_recv.at[4 * w], across)
        x2_copies[w].start()

    for copy in root_copies:
        copy.wait_recv()
    loads[4].wait()
    loads[5].wait()
    core_copies = []
    for w, ref in enumerate((lroot, rroot)):
        copy = remote(ref.at[:, k], ref.at[:, k], core_send.at[w], core_recv.at[w], partner)
        copy.start()
        core_copies.append(copy)

    strip = pl.ds(pl.multiple_of(k * H, H), H)
    block_copies = {}

    def finish(w, arrived):
        start, n = PARTS[w]
        read = sum_of(n, own_piece(w, xl, 0), arrived)

        def step(i, carry):
            r = pl.multiple_of(i * STRIDE, STRIDE)
            for t in range(H // LANES):
                mine = pl.ds(pl.multiple_of(k * H + t * LANES, LANES), LANES)
                high, low = split(read(t, r))
                ghigh[pl.ds(start + r, STRIDE), mine] = high
                glow[pl.ds(start + r, STRIDE), mine] = low
            return carry

        lax.fori_loop(0, n // STRIDE, step, 0)
        for i, ref in enumerate((ghigh, glow)):
            here = ref.at[pl.ds(start, n), strip]
            n_sem = 2 + 2 * w + i
            block_copies[w, i] = remote(here, here, core_send.at[n_sem], core_recv.at[n_sem], partner)
            block_copies[w, i].start()

    def rows_for(there):
        return pl.ds(pl.multiple_of(there * 2 * S + k * S, S), S)

    def row_copy(there, slot):
        return remote(
            grow_out.at[there], grow_in.at[slot], row_send.at[0, there], row_recv.at[0, slot], (d, there * 2 + k)
        )

    def send_rows(w):
        for i in range(2):
            block_copies[w, i].wait_recv()
        start, n = PARTS[w]
        for there in range(start // (2 * S), (start + n) // (2 * S)):
            rows = rows_for(there)
            value = ghigh[rows, :].astype(F32) + glow[rows, :].astype(F32)
            code = encode_rows(value, T, grow_out.at[there], 0)
            grow_out[there, pl.ds(WIDE, T), :] = code.astype(I32).astype(I16)

            @pl.when(c != there)
            def _():
                row_copy(there, c).start()

    for w in range(2):
        x2_copies[w].wait_recv()
        finish(w, [got(1, w, 1), got(2, w, 1), x2_in.at[w]])
        if w:
            send_rows(0)
    x1_copies[0].wait_recv()
    for j in (2, 1, 3):
        y2_copies[j].wait_recv()
    finish(2, [x1_in.at[0]] + [y2_in.at[n] for n in range(3)])
    send_rows(1)
    send_rows(2)
    grow_in[c] = grow_out[c]

    high_rows = jnp.concatenate([ghigh[rows_for(t), :] for t in range(NB)], axis=0)
    low_rows = jnp.concatenate([glow[rows_for(t), :] for t in range(NB)], axis=0)
    nt = ((1,), (1,))
    pleft[...] = dot(high_rows, ghigh[...], nt) + (dot(high_rows, glow[...], nt) + dot(low_rows, ghigh[...], nt))
    prod_copies = []

    def send_products(w, i, first, size):
        a, b = (PEERS + [(0, 0)])[i]
        here, there = prod_out.at[i, pl.ds(first, size)], prod_in.at[c, pl.ds(first, size)]
        if a or b:
            copy = remote(here, there, row_send.at[1 + w, i], row_recv.at[1 + w, i], along_mp(a, b))
            prod_copies.append(copy)
        else:
            copy = pltpu.make_async_copy(here, there, store_sem.at[w])
            stores.append(copy)
        copy.start()

    stores = []
    for i, (a, b) in enumerate(PEERS + [(0, 0)]):
        value = pleft[pl.ds(pl.multiple_of(chip_at(a, b) * S, S), S), :]
        left_codes[i] = encode_rows(value, T // 2, prod_out.at[i], 0)
        send_products(0, i, 0, WIDE)
    tn = ((0,), (0,))
    pright[...] = dot(ghigh[...], ghigh[...], tn) + (
        dot(ghigh[...], glow[...], tn) + dot(glow[...], ghigh[...], tn)
    )
    for i, (a, b) in enumerate(PEERS + [(0, 0)]):
        code = encode_rows(pright[rows_for(chip_at(a, b)), :], T // 2, prod_out.at[i], WIDE)
        codes = jnp.concatenate([left_codes[i], code], axis=0)
        prod_out[i, pl.ds(2 * WIDE, T), :] = codes.astype(I32).astype(I16)

    for i in range(NB):
        send_products(1, i, WIDE, WIDE + T)

    for copy in core_copies:
        copy.wait_recv()
    rcols = jnp.concatenate([rroot[a, b, :, strip] for a in range(NB) for b in range(2)], axis=0)
    inner = dot(ghigh[...], rcols) + dot(glow[...], rcols)
    inner_high, inner_low = split(inner)
    lrows = lroot[...].reshape(B, B)
    applied = dot(lrows, inner_high) + dot(lrows, inner_low)
    pright[:, pl.ds(0, H)] = applied
    pair_out[...] = fold(applied * applied)
    n = len(PEERS)
    pair_copy = remote(pair_out, pair_in, sum_send.at[n], sum_recv.at[n], partner)
    pair_copy.start()

    loads[6].wait()
    loads[7].wait()
    for a, b in PEERS + [(0, 0)]:
        slot = chip_at(-a, -b)
        if a or b:
            row_copy(slot, slot).wait_recv()
        total = jnp.zeros((8, LANES), F32)
        scale = scale_of(grow_in[slot, pl.ds(WIDE, T), :])
        for t, grad in enumerate(decode_rows(grow_in.at[slot], 0, scale)):
            cols = pl.ds(t * LANES, LANES)
            mean = FIRST_DECAY * first[slot, :, cols] + (1.0 - FIRST_DECAY) * grad
            square = SECOND_DECAY * second[slot, :, cols] + (1.0 - SECOND_DECAY) * grad * grad
            new_first[slot, :, cols] = mean
            new_second[slot, :, cols] = square
            adam = mean / (jnp.sqrt(square) + ADAM_EPS)
            total = total + fold(adam * adam)
        sums_out[slot] = total

    chip_copy = remote(sums_out, sums_other, sum_send.at[n + 1], sum_recv.at[n + 1], partner)
    chip_copy.start()
    chip_copy.wait_recv()
    sums_chip[...] = sums_out[...] + sums_other[...]
    sum_copies = []
    for i, (a, b) in enumerate(PEERS):
        copy = remote(sums_chip.at[chip_at(a, b)], sums_in.at[i], sum_send.at[i], sum_recv.at[i], along_mp(a, b))
        copy.start()
        sum_copies.append(copy)

    pair_copy.wait_recv()
    total = sums_chip[c]
    for i, copy in enumerate(sum_copies):
        copy.wait_recv()
        total = total + sums_in[i]
    norms = [jnp.sum(x, axis=(0, 1), keepdims=True) for x in (total, pair_out[...] + pair_in[...])]
    graft = jnp.sqrt(norms[0]) / (jnp.sqrt(norms[1]) + NORM_EPS)
    update[...] = (pright[:, pl.ds(0, H)] * graft).astype(BF16)

    for copy in prod_copies:
        copy.wait_recv()
    for a, b in PEERS:
        row_copy(chip_at(a, b), c).wait_send()
    for copies in (x1_copies, y2_copies, x2_copies, ring, block_copies):
        for copy in copies.values():
            copy.wait_send()
    for copy in [pair_copy, chip_copy] + root_copies + core_copies + prod_copies + sum_copies:
        copy.wait_send()
    for store in stores:
        store.wait()


def finish_kernel(
    prod, left, right, first, second, update,
    left_out, right_out, first_out, second_out, update_out,
    new_left, new_right, sem,
):
    through = [(first, first_out), (second, second_out), (update, update_out)]
    stats = [(new_left, left_out), (new_right, right_out)]
    stores = [pltpu.make_async_copy(src, dst, sem.at[i]) for i, (src, dst) in enumerate(stats + through)]
    for store in stores[2:]:
        store.start()
    for w, (old, new) in enumerate(((left, new_left), (right, new_right))):

        def add(slot, carry):
            code = prod[slot, pl.ds(2 * WIDE, T), :].astype(F32)[w * (T // 2) : (w + 1) * (T // 2)]
            scale = jnp.exp(code * STEP) * (1.0 / FULL)
            for t, value in enumerate(decode_rows(prod.at[slot], w * WIDE, scale)):
                cols = pl.ds(t * LANES, LANES)
                new[slot, :, cols] = old[slot, :, cols] + value
            return carry

        lax.fori_loop(0, NB, add, 0)
        stores[w].start()
    for store in stores:
        store.wait()


def on_device(
    grad_parts, home, left_stat, right_stat, left_root, right_root, first_moment, second_moment
):
    in_hbm = pl.BlockSpec(memory_space=pltpu.HBM)
    in_vmem = pl.BlockSpec(memory_space=pltpu.VMEM)
    n = len(PEERS)
    ring_piece = (H // LANES * RING + T, LANES)
    cross_piece = (H // LANES * CROSS + T, LANES)
    rows = (WIDE + T, LANES)
    products = (2 * WIDE + T, LANES)
    stat = pltpu.VMEM((NB, S, B), F32)
    tile = pltpu.VMEM((B, H), BF16)
    dma = pltpu.SemaphoreType.DMA
    scratch = [
        pltpu.SMEM((NB,), I32),
        *[pltpu.VMEM((NB, size, H), F32) for _, size in PARTS],
        *[stat] * 2,
        *[pltpu.VMEM((NB, 2, S, B), BF16)] * 2,
        *[pltpu.VMEM((12, *ring_piece), I16)] * 2,
        *[pltpu.VMEM((4, *cross_piece), I16)] * 2,
        *[pltpu.VMEM((3, *cross_piece), I16)] * 2,
        *[pltpu.VMEM((2, *ring_piece), I16)] * 2,
        pltpu.VMEM((B, H), F32),
        *[pltpu.VMEM((B, B), BF16)] * 2,
        *[pltpu.VMEM((NB, *rows), I16)] * 2,
        pltpu.VMEM((NB, *products), I16),
        pltpu.VMEM((NB, T // 2, LANES), F32),
        pltpu.VMEM((H, B), F32),
        pltpu.VMEM((B, B), F32),
        *[pltpu.VMEM((NB, 8, LANES), F32)] * 3,
        pltpu.VMEM((n, 8, LANES), F32),
        *[pltpu.VMEM((8, LANES), F32)] * 2,
        dma((8,)),
        *[dma((2, n))] * 2,
        *[dma((12,))] * 2,
        *[dma((4,))] * 2,
        *[dma((5,))] * 2,
        *[dma((8,))] * 2,
        *[dma((3, NB))] * 2,
        *[dma((n + 2,))] * 2,
        dma((2,)),
        pltpu.SemaphoreType.REGULAR,
    ]
    made = pl.pallas_call(
        kernel,
        out_shape=(pltpu.VMEM((NB, *products), I16), stat, stat, tile),
        in_specs=[in_hbm] * 6,
        out_specs=[in_vmem] * 4,
        scratch_shapes=scratch,
        compiler_params=pltpu.CompilerParams(
            collective_id=0, has_side_effects=True, vmem_limit_bytes=40 * 2**20
        ),
        cost_estimate=pl.CostEstimate(flops=2 * 10**9, bytes_accessed=9 * 2**20, transcendentals=0),
        name="shampoo_step",
    )(
        *[
            pltpu.with_memory_space_constraint(x, pltpu.HBM)
            for x in (home, grad_parts.reshape(NB, B, H), left_root, right_root, first_moment, second_moment)
        ]
    )
    stat_out = jax.ShapeDtypeStruct((NB, S, B), F32)
    return pl.pallas_call(
        finish_kernel,
        out_shape=(stat_out,) * 4 + (jax.ShapeDtypeStruct((B, H), BF16),),
        in_specs=[in_vmem] * 6,
        out_specs=[in_hbm] * 5,
        scratch_shapes=[stat, stat, dma((5,))],
        compiler_params=pltpu.CompilerParams(vmem_limit_bytes=16 * 2**20),
        name="finish_outputs",
    )(made[0], left_stat, right_stat, *made[1:])


def solution(mesh):
    rows = P("dp", "mp", None)
    in_specs = (P("dp", None, "mp"), P(), rows, rows, rows, rows, rows, rows)
    out_specs = (rows, rows, rows, rows, P("dp", "mp"))
    return jax.shard_map(
        on_device, mesh=mesh, in_specs=in_specs, out_specs=out_specs, check_vma=False
    )
```

```python
import functools
import math

import jax
import jax.numpy as jnp
from jax import lax
from jax.experimental import pallas as pl
from jax.experimental.pallas import tpu as pltpu
from jax.sharding import PartitionSpec as P

FIRST_DECAY = 0.9
SECOND_DECAY = 0.999
ADAM_EPS = 1e-08
NORM_EPS = 1e-06
MESH = pl.DeviceIdType.MESH
F32 = jnp.float32
BF16 = jnp.bfloat16
I16 = jnp.int16
I32 = jnp.int32

B = 512
H = 256
PARTS = ((0, 192), (192, 192), (384, 128))
RING = PARTS[0][1]
CROSS = PARTS[2][1]
S = 32
T = 16
STRIDE = 64
LANES = 128
WIDE = B // LANES * S
NB = 8
NY = 4
FULL = 32760.0
STEP = math.log(2.0) / 4.0
TINY = 1e-30

PEERS = [(1, 2), (1, 1), (1, 3), (0, 2), (1, 0), (0, 1), (0, 3)]


def code_of(peak):
    return jnp.ceil(jnp.log(jnp.maximum(peak, TINY)) * (1.0 / STEP))


def coded(x):
    return jnp.floor(x + 0.5).astype(I32).astype(I16)


def scale_of(code):
    return jnp.exp(code.astype(I32).astype(F32) * STEP) * (1.0 / FULL)


def decoded(values, scale):
    return values.astype(I32).astype(F32) * scale


def encode_piece(n, read, out, keep=None):
    tiles = range(H // LANES)

    def look(i, peak):
        r = pl.multiple_of(i * STRIDE, STRIDE)
        for t in tiles:
            x = read(t, r)
            if keep is not None:
                keep[pl.ds(r, STRIDE), pl.ds(t * LANES, LANES)] = x
            peak = jnp.maximum(peak, jnp.max(jnp.abs(x).reshape(STRIDE // T, T, LANES), axis=0))
        return peak

    code = code_of(lax.fori_loop(0, n // STRIDE, look, jnp.zeros((T, LANES), F32)))
    factor = jnp.exp(code * -STEP) * FULL

    def write(i, carry):
        r = pl.multiple_of(i * STRIDE, STRIDE)
        for t in tiles:
            x = read(t, r) if keep is None else keep[pl.ds(r, STRIDE), pl.ds(t * LANES, LANES)]
            x = x.reshape(STRIDE // T, T, LANES) * factor[None]
            out[pl.ds(t * n + r, STRIDE), :] = coded(x).reshape(STRIDE, LANES)
        return carry

    lax.fori_loop(0, n // STRIDE, write, 0)
    out[pl.ds(H // LANES * n, T), :] = code.astype(I32).astype(I16)


def sum_of(n, own, arrived):
    scales = [scale_of(ref[pl.ds(H // LANES * n, T), :])[None] for ref in arrived]

    def read(t, r):
        x = own(t, r)
        for ref, scale in zip(arrived, scales):
            values = ref[pl.ds(t * n + r, STRIDE), :].reshape(STRIDE // T, T, LANES)
            x = x + decoded(values, scale).reshape(STRIDE, LANES)
        return x

    return read


def encode_rows(x, group, out, first):
    n = B // LANES
    parts = [x[:, t * LANES : (t + 1) * LANES].reshape(S // group, group, LANES) for t in range(n)]
    code = code_of(functools.reduce(jnp.maximum, [jnp.max(jnp.abs(p), axis=0) for p in parts]))
    factor = jnp.exp(code * -STEP) * FULL
    for t in range(n):
        out[pl.ds(first + t * S, S), :] = coded(parts[t] * factor[None]).reshape(S, LANES)
    return code


def decode_rows(codes, first, scale):
    group = scale.shape[0]
    return [
        decoded(codes[pl.ds(first + t * S, S), :].reshape(S // group, group, LANES), scale[None]).reshape(S, LANES)
        for t in range(B // LANES)
    ]


def dot(a, b, dims=((1,), (0,))):
    return lax.dot_general(a, b, (dims, ((), ())), preferred_element_type=F32)


def split(x):
    high = x.astype(BF16)
    return high, (x - high.astype(F32)).astype(BF16)


def fold(x):
    r, c = x.shape
    x = jnp.sum(x.reshape(r // 8, 8, c), axis=0)
    return functools.reduce(jnp.add, [x[:, t * LANES : (t + 1) * LANES] for t in range(c // LANES)])


def kernel(
    home_hbm, part_hbm, lroot_hbm, rroot_hbm, first_hbm, second_hbm,
    prod_in, new_first, new_second, update,
    home, part_up, part_down, part_cross, first, second, lroot, rroot,
    ring_out, ring_in, x1_out, x1_in, y2_out, y2_in, x2_out, x2_in,
    work, ghigh, glow, grow_out, grow_in, prod_out, left_codes, pleft, pright,
    sums_out, sums_other, sums_chip, sums_in, pair_out, pair_in,
    load_sem, root_send, root_recv, ring_send, ring_recv, x1_send, x1_recv, s2_send, s2_recv,
    core_send, core_recv, row_send, row_recv, sum_send, sum_recv, store_sem, ready,
):
    d = lax.axis_index("dp")
    m = lax.axis_index("mp")
    xl, y = d // NY, d % NY
    xh, z, k = m // 8, (m // 2) % 4, m % 2
    c = m // 2

    partner = (d, m + 1 - 2 * k)
    across = ((1 - xl) * NY + y, m)

    def along_y(j):
        return (xl * NY + (y + j) % NY, m)

    def chip_at(a, b):
        return ((xh + a) % 2) * 4 + (z + b) % 4

    def along_mp(a, b):
        return (d, chip_at(a, b) * 2 + k)

    def remote(src, dst, send, recv, device):
        return pltpu.make_async_remote_copy(
            src_ref=src, dst_ref=dst, send_sem=send, recv_sem=recv, device_id=device, device_id_type=MESH
        )

    parts = (part_up, part_down, part_cross)
    loads = [pltpu.make_async_copy(home_hbm, home, load_sem.at[0])]
    for i, (start, n) in enumerate(PARTS):
        loads.append(pltpu.make_async_copy(part_hbm.at[:, pl.ds(start, n)], parts[i], load_sem.at[1 + i]))
    others = ((lroot_hbm.at[c], lroot.at[c, k]), (rroot_hbm.at[c], rroot.at[c, k]), (first_hbm, first), (second_hbm, second))
    for i, (src, dst) in enumerate(others):
        loads.append(pltpu.make_async_copy(src, dst, load_sem.at[4 + i]))
    for load in loads[:4]:
        load.start()

    rank = 2 * z + xh

    def rank_of(there):
        return 2 * (there % 4) + there // 4

    barrier = pltpu.get_barrier_semaphore()
    for device in [across, partner] + [along_y(j) for j in (1, 2, 3)]:
        pl.semaphore_signal(barrier, inc=1, device_id=device, device_id_type=MESH)
    for a, b in PEERS:

        @pl.when(rank_of(chip_at(a, b)) > rank)
        def _():
            pl.semaphore_signal(barrier, inc=1, device_id=along_mp(a, b), device_id_type=MESH)

    pl.semaphore_wait(barrier, 5 + rank)
    for a, b in PEERS:

        @pl.when(rank_of(chip_at(a, b)) < rank)
        def _():
            pl.semaphore_signal(ready, inc=1, device_id=along_mp(a, b), device_id_type=MESH)

    root_copies = []
    for i, (a, b) in enumerate(PEERS):
        there = chip_at(a, b)
        for w, (src, dst) in enumerate(((lroot_hbm, lroot), (rroot_hbm, rroot))):
            root_copies.append(
                remote(src.at[there], dst.at[c, k], root_send.at[w, i], root_recv.at[w, i], along_mp(a, b))
            )

    def send_roots(early):
        for i, (a, b) in enumerate(PEERS):
            lower = rank_of(chip_at(a, b)) < rank
            for w in range(2):

                @pl.when(lower if early else jnp.logical_not(lower))
                def _():
                    if not (early and a and w):
                        root_copies[2 * i + w].start()

                if not early and a and w:

                    @pl.when(lower)
                    def _():
                        root_copies[2 * i + w].start()

    def source(q):
        return functools.reduce(jnp.maximum, [jnp.where(home[r] == q, r, 0) for r in range(NB)])

    def own_piece(w, to_x, j):
        row = source(to_x * NY + (y + j) % NY)
        return lambda t, r: parts[w][row, pl.ds(r, STRIDE), pl.ds(t * LANES, LANES)]

    to_xs = (1 - xl, xl)
    along = (1, -1)
    ring = {}

    def send_ring(kind, w, o, to, step, arrived):
        n = (kind * 2 + w) * 2 + o
        own = own_piece(w, to_xs[o], to)
        if arrived:
            encode_piece(RING, sum_of(RING, own, arrived), ring_out.at[n], work)
        else:
            encode_piece(RING, own, ring_out.at[n])
        ring[kind, w, o] = remote(
            ring_out.at[n], ring_in.at[n], ring_send.at[n], ring_recv.at[n], along_y(step % NY)
        )
        ring[kind, w, o].start()

    def got(kind, w, o):
        ring[kind, w, o].wait_recv()
        return ring_in.at[(kind * 2 + w) * 2 + o]

    def send_far(w, o):
        send_ring(0, w, o, 2, along[w], [])

    def send_back(w, o):
        send_ring(1, w, o, -along[w], -along[w], [])

    def send_on(w, o):
        send_ring(2, w, o, along[w], along[w], [got(0, w, o)])

    loads[0].wait()
    loads[1].wait()
    send_far(0, 0)
    loads[2].wait()
    send_far(1, 0)
    loads[3].wait()
    x1_copies, y2_copies, x2_copies = {}, {}, {}
    for j in (2, 1, 3, 0):
        encode_piece(CROSS, own_piece(2, 1 - xl, j), x1_out.at[j])
        x1_copies[j] = remote(x1_out.at[j], x1_in.at[j], x1_send.at[j], x1_recv.at[j], across)
        x1_copies[j].start()
        if j == 2:
            for w in range(2):
                send_far(w, 1)
    for load in loads[4:]:
        load.start()
    send_roots(True)
    send_back(1, 0)
    send_back(0, 0)
    send_on(0, 0)
    send_on(1, 0)
    send_back(1, 1)
    send_back(0, 1)
    send_on(0, 1)
    send_on(1, 1)
    for j in (2, 1, 3):
        x1_copies[j].wait_recv()
        read = sum_of(CROSS, own_piece(2, xl, j), [x1_in.at[j]])
        encode_piece(CROSS, read, y2_out.at[j - 1], work)
        y2_copies[j] = remote(y2_out.at[j - 1], y2_in.at[j - 1], s2_send.at[j], s2_recv.at[j], along_y(j))
        y2_copies[j].start()
    for w in range(2):
        read = sum_of(RING, own_piece(w, 1 - xl, 0), [got(1, w, 0), got(2, w, 0)])
        encode_piece(RING, read, x2_out.at[w], work)
        x2_copies[w] = remote(x2_out.at[w], x2_in.at[w], s2_send.at[4 * w], s2_recv.at[4 * w], across)
        x2_copies[w].start()

    @pl.when(rank < NB - 1)
    def _():
        pl.semaphore_wait(ready, NB - 1 - rank)

    send_roots(False)

    strip = pl.ds(pl.multiple_of(k * H, H), H)
    block_copies = {}

    def finish(w, arrived):
        start, n = PARTS[w]
        read = sum_of(n, own_piece(w, xl, 0), arrived)

        def step(i, carry):
            r = pl.multiple_of(i * STRIDE, STRIDE)
            for t in range(H // LANES):
                mine = pl.ds(pl.multiple_of(k * H + t * LANES, LANES), LANES)
                high, low = split(read(t, r))
                ghigh[pl.ds(start + r, STRIDE), mine] = high
                glow[pl.ds(start + r, STRIDE), mine] = low
            return carry

        lax.fori_loop(0, n // STRIDE, step, 0)
        for i, ref in enumerate((ghigh, glow)):
            here = ref.at[pl.ds(start, n), strip]
            n_sem = 2 + 2 * w + i
            block_copies[w, i] = remote(here, here, core_send.at[n_sem], core_recv.at[n_sem], partner)
            block_copies[w, i].start()

    def rows_for(there):
        return pl.ds(pl.multiple_of(there * 2 * S + k * S, S), S)

    def row_copy(there, slot):
        return remote(
            grow_out.at[there], grow_in.at[slot], row_send.at[0, there], row_recv.at[0, slot], (d, there * 2 + k)
        )

    def send_rows(w):
        for i in range(2):
            block_copies[w, i].wait_recv()
        start, n = PARTS[w]
        for there in range(start // (2 * S), (start + n) // (2 * S)):
            rows = rows_for(there)
            value = ghigh[rows, :].astype(F32) + glow[rows, :].astype(F32)
            code = encode_rows(value, T, grow_out.at[there], 0)
            grow_out[there, pl.ds(WIDE, T), :] = code.astype(I32).astype(I16)

            @pl.when(c != there)
            def _():
                row_copy(there, c).start()

    for w in range(2):
        x2_copies[w].wait_recv()
        finish(w, [got(1, w, 1), got(2, w, 1), x2_in.at[w]])
        if w:
            send_rows(0)
    x1_copies[0].wait_recv()
    for j in (2, 1, 3):
        y2_copies[j].wait_recv()
    finish(2, [x1_in.at[0]] + [y2_in.at[n] for n in range(3)])
    send_rows(1)
    send_rows(2)
    grow_in[c] = grow_out[c]

    high_rows = jnp.concatenate([ghigh[rows_for(t), :] for t in range(NB)], axis=0)
    low_rows = jnp.concatenate([glow[rows_for(t), :] for t in range(NB)], axis=0)
    nt = ((1,), (1,))
    pleft[...] = dot(high_rows, ghigh[...], nt) + (dot(high_rows, glow[...], nt) + dot(low_rows, ghigh[...], nt))
    prod_copies = []

    def send_products(w, i, first, size):
        a, b = (PEERS + [(0, 0)])[i]
        here, there = prod_out.at[i, pl.ds(first, size)], prod_in.at[c, pl.ds(first, size)]
        if a or b:
            copy = remote(here, there, row_send.at[1 + w, i], row_recv.at[1 + w, i], along_mp(a, b))
            prod_copies.append(copy)
        else:
            copy = pltpu.make_async_copy(here, there, store_sem.at[w])
            stores.append(copy)
        copy.start()

    stores = []
    for i, (a, b) in enumerate(PEERS + [(0, 0)]):
        value = pleft[pl.ds(pl.multiple_of(chip_at(a, b) * S, S), S), :]
        left_codes[i] = encode_rows(value, T // 2, prod_out.at[i], 0)
        send_products(0, i, 0, WIDE)
    tn = ((0,), (0,))
    pright[...] = dot(ghigh[...], ghigh[...], tn) + (
        dot(ghigh[...], glow[...], tn) + dot(glow[...], ghigh[...], tn)
    )
    for i, (a, b) in enumerate(PEERS + [(0, 0)]):
        code = encode_rows(pright[rows_for(chip_at(a, b)), :], T // 2, prod_out.at[i], WIDE)
        codes = jnp.concatenate([left_codes[i], code], axis=0)
        prod_out[i, pl.ds(2 * WIDE, T), :] = codes.astype(I32).astype(I16)

    for i in range(NB):
        send_products(1, i, WIDE, WIDE + T)

    for copy in root_copies:
        copy.wait_recv()
    loads[4].wait()
    loads[5].wait()
    core_copies = []
    for w, ref in enumerate((lroot, rroot)):
        copy = remote(ref.at[:, k], ref.at[:, k], core_send.at[w], core_recv.at[w], partner)
        copy.start()
        core_copies.append(copy)

    for copy in core_copies:
        copy.wait_recv()
    rcols = jnp.concatenate([rroot[a, b, :, strip] for a in range(NB) for b in range(2)], axis=0)
    inner = dot(ghigh[...], rcols) + dot(glow[...], rcols)
    inner_high, inner_low = split(inner)
    lrows = lroot[...].reshape(B, B)
    applied = dot(lrows, inner_high) + dot(lrows, inner_low)
    pright[:, pl.ds(0, H)] = applied
    pair_out[...] = fold(applied * applied)
    n = len(PEERS)
    pair_copy = remote(pair_out, pair_in, sum_send.at[n], sum_recv.at[n], partner)
    pair_copy.start()

    loads[6].wait()
    loads[7].wait()
    for a, b in PEERS + [(0, 0)]:
        slot = chip_at(-a, -b)
        if a or b:
            row_copy(slot, slot).wait_recv()
        total = jnp.zeros((8, LANES), F32)
        scale = scale_of(grow_in[slot, pl.ds(WIDE, T), :])
        for t, grad in enumerate(decode_rows(grow_in.at[slot], 0, scale)):
            cols = pl.ds(t * LANES, LANES)
            mean = FIRST_DECAY * first[slot, :, cols] + (1.0 - FIRST_DECAY) * grad
            square = SECOND_DECAY * second[slot, :, cols] + (1.0 - SECOND_DECAY) * grad * grad
            new_first[slot, :, cols] = mean
            new_second[slot, :, cols] = square
            adam = mean / (jnp.sqrt(square) + ADAM_EPS)
            total = total + fold(adam * adam)
        sums_out[slot] = total

    chip_copy = remote(sums_out, sums_other, sum_send.at[n + 1], sum_recv.at[n + 1], partner)
    chip_copy.start()
    chip_copy.wait_recv()
    sums_chip[...] = sums_out[...] + sums_other[...]
    sum_copies = []
    for i, (a, b) in enumerate(PEERS):
        copy = remote(sums_chip.at[chip_at(a, b)], sums_in.at[i], sum_send.at[i], sum_recv.at[i], along_mp(a, b))
        copy.start()
        sum_copies.append(copy)

    pair_copy.wait_recv()
    total = sums_chip[c]
    for i, copy in enumerate(sum_copies):
        copy.wait_recv()
        total = total + sums_in[i]
    norms = [jnp.sum(x, axis=(0, 1), keepdims=True) for x in (total, pair_out[...] + pair_in[...])]
    graft = jnp.sqrt(norms[0]) / (jnp.sqrt(norms[1]) + NORM_EPS)
    update[...] = (pright[:, pl.ds(0, H)] * graft).astype(BF16)

    for copy in prod_copies:
        copy.wait_recv()
    for a, b in PEERS:
        row_copy(chip_at(a, b), c).wait_send()
    for copies in (x1_copies, y2_copies, x2_copies, ring, block_copies):
        for copy in copies.values():
            copy.wait_send()
    for copy in [pair_copy, chip_copy] + root_copies + core_copies + prod_copies + sum_copies:
        copy.wait_send()
    for store in stores:
        store.wait()


def finish_kernel(
    prod, left, right, first, second, update,
    left_out, right_out, first_out, second_out, update_out,
    new_left, new_right, sem,
):
    through = [(first, first_out), (second, second_out), (update, update_out)]
    stats = [(new_left, left_out), (new_right, right_out)]
    stores = [pltpu.make_async_copy(src, dst, sem.at[i]) for i, (src, dst) in enumerate(stats + through)]
    for store in stores[2:]:
        store.start()
    for w, (old, new) in enumerate(((left, new_left), (right, new_right))):

        def add(slot, carry):
            code = prod[slot, pl.ds(2 * WIDE, T), :].astype(F32)[w * (T // 2) : (w + 1) * (T // 2)]
            scale = jnp.exp(code * STEP) * (1.0 / FULL)
            for t, value in enumerate(decode_rows(prod.at[slot], w * WIDE, scale)):
                cols = pl.ds(t * LANES, LANES)
                new[slot, :, cols] = old[slot, :, cols] + value
            return carry

        lax.fori_loop(0, NB, add, 0)
        stores[w].start()
    for store in stores:
        store.wait()


def on_device(
    grad_parts, home, left_stat, right_stat, left_root, right_root, first_moment, second_moment
):
    in_hbm = pl.BlockSpec(memory_space=pltpu.HBM)
    in_vmem = pl.BlockSpec(memory_space=pltpu.VMEM)
    n = len(PEERS)
    ring_piece = (H // LANES * RING + T, LANES)
    cross_piece = (H // LANES * CROSS + T, LANES)
    rows = (WIDE + T, LANES)
    products = (2 * WIDE + T, LANES)
    stat = pltpu.VMEM((NB, S, B), F32)
    tile = pltpu.VMEM((B, H), BF16)
    dma = pltpu.SemaphoreType.DMA
    scratch = [
        pltpu.SMEM((NB,), I32),
        *[pltpu.VMEM((NB, size, H), F32) for _, size in PARTS],
        *[stat] * 2,
        *[pltpu.VMEM((NB, 2, S, B), BF16)] * 2,
        *[pltpu.VMEM((12, *ring_piece), I16)] * 2,
        *[pltpu.VMEM((4, *cross_piece), I16)] * 2,
        *[pltpu.VMEM((3, *cross_piece), I16)] * 2,
        *[pltpu.VMEM((2, *ring_piece), I16)] * 2,
        pltpu.VMEM((B, H), F32),
        *[pltpu.VMEM((B, B), BF16)] * 2,
        *[pltpu.VMEM((NB, *rows), I16)] * 2,
        pltpu.VMEM((NB, *products), I16),
        pltpu.VMEM((NB, T // 2, LANES), F32),
        pltpu.VMEM((H, B), F32),
        pltpu.VMEM((B, B), F32),
        *[pltpu.VMEM((NB, 8, LANES), F32)] * 3,
        pltpu.VMEM((n, 8, LANES), F32),
        *[pltpu.VMEM((8, LANES), F32)] * 2,
        dma((8,)),
        *[dma((2, n))] * 2,
        *[dma((12,))] * 2,
        *[dma((4,))] * 2,
        *[dma((5,))] * 2,
        *[dma((8,))] * 2,
        *[dma((3, NB))] * 2,
        *[dma((n + 2,))] * 2,
        dma((2,)),
        pltpu.SemaphoreType.REGULAR,
    ]
    made = pl.pallas_call(
        kernel,
        out_shape=(pltpu.VMEM((NB, *products), I16), stat, stat, tile),
        in_specs=[in_hbm] * 6,
        out_specs=[in_vmem] * 4,
        scratch_shapes=scratch,
        compiler_params=pltpu.CompilerParams(
            collective_id=0, has_side_effects=True, vmem_limit_bytes=40 * 2**20
        ),
        cost_estimate=pl.CostEstimate(flops=2 * 10**9, bytes_accessed=9 * 2**20, transcendentals=0),
        name="shampoo_step",
    )(
        *[
            pltpu.with_memory_space_constraint(x, pltpu.HBM)
            for x in (home, grad_parts.reshape(NB, B, H), left_root, right_root, first_moment, second_moment)
        ]
    )
    stat_out = jax.ShapeDtypeStruct((NB, S, B), F32)
    return pl.pallas_call(
        finish_kernel,
        out_shape=(stat_out,) * 4 + (jax.ShapeDtypeStruct((B, H), BF16),),
        in_specs=[in_vmem] * 6,
        out_specs=[in_hbm] * 5,
        scratch_shapes=[stat, stat, dma((5,))],
        compiler_params=pltpu.CompilerParams(vmem_limit_bytes=16 * 2**20),
        name="finish_outputs",
    )(made[0], left_stat, right_stat, *made[1:])


def solution(mesh):
    rows = P("dp", "mp", None)
    in_specs = (P("dp", None, "mp"), P(), rows, rows, rows, rows, rows, rows)
    out_specs = (rows, rows, rows, rows, P("dp", "mp"))
    return jax.shard_map(
        on_device, mesh=mesh, in_specs=in_specs, out_specs=out_specs, check_vma=False
    )
```

```python
import functools
import math

import jax
import jax.numpy as jnp
from jax import lax
from jax.experimental import pallas as pl
from jax.experimental.pallas import tpu as pltpu
from jax.sharding import PartitionSpec as P

FIRST_DECAY = 0.9
SECOND_DECAY = 0.999
ADAM_EPS = 1e-08
NORM_EPS = 1e-06
MESH = pl.DeviceIdType.MESH
F32 = jnp.float32
BF16 = jnp.bfloat16
I16 = jnp.int16
I32 = jnp.int32

B = 512
H = 256
PARTS = ((0, 192), (192, 192), (384, 128))
RING = PARTS[0][1]
CROSS = PARTS[2][1]
S = 32
T = 16
STRIDE = 64
LANES = 128
WIDE = B // LANES * S
NB = 8
NY = 4
FULL = 32760.0
STEP = math.log(2.0) / 4.0
TINY = 1e-30

PEERS = [(1, 2), (1, 1), (1, 3), (0, 2), (1, 0), (0, 1), (0, 3)]


def code_of(peak):
    return jnp.ceil(jnp.log(jnp.maximum(peak, TINY)) * (1.0 / STEP))


def coded(x):
    return jnp.floor(x + 0.5).astype(I32).astype(I16)


def scale_of(code):
    return jnp.exp(code.astype(I32).astype(F32) * STEP) * (1.0 / FULL)


def decoded(values, scale):
    return values.astype(I32).astype(F32) * scale


def encode_piece(n, read, out, keep=None):
    tiles = range(H // LANES)

    def look(i, peak):
        r = pl.multiple_of(i * STRIDE, STRIDE)
        for t in tiles:
            x = read(t, r)
            if keep is not None:
                keep[pl.ds(r, STRIDE), pl.ds(t * LANES, LANES)] = x
            peak = jnp.maximum(peak, jnp.max(jnp.abs(x).reshape(STRIDE // T, T, LANES), axis=0))
        return peak

    code = code_of(lax.fori_loop(0, n // STRIDE, look, jnp.zeros((T, LANES), F32)))
    factor = jnp.exp(code * -STEP) * FULL

    def write(i, carry):
        r = pl.multiple_of(i * STRIDE, STRIDE)
        for t in tiles:
            x = read(t, r) if keep is None else keep[pl.ds(r, STRIDE), pl.ds(t * LANES, LANES)]
            x = x.reshape(STRIDE // T, T, LANES) * factor[None]
            out[pl.ds(t * n + r, STRIDE), :] = coded(x).reshape(STRIDE, LANES)
        return carry

    lax.fori_loop(0, n // STRIDE, write, 0)
    out[pl.ds(H // LANES * n, T), :] = code.astype(I32).astype(I16)


def sum_of(n, own, arrived):
    scales = [scale_of(ref[pl.ds(H // LANES * n, T), :])[None] for ref in arrived]

    def read(t, r):
        x = own(t, r)
        for ref, scale in zip(arrived, scales):
            values = ref[pl.ds(t * n + r, STRIDE), :].reshape(STRIDE // T, T, LANES)
            x = x + decoded(values, scale).reshape(STRIDE, LANES)
        return x

    return read


def encode_rows(x, group, out, first):
    n = B // LANES
    parts = [x[:, t * LANES : (t + 1) * LANES].reshape(S // group, group, LANES) for t in range(n)]
    code = code_of(functools.reduce(jnp.maximum, [jnp.max(jnp.abs(p), axis=0) for p in parts]))
    factor = jnp.exp(code * -STEP) * FULL
    for t in range(n):
        out[pl.ds(first + t * S, S), :] = coded(parts[t] * factor[None]).reshape(S, LANES)
    return code


def decode_rows(codes, first, scale):
    group = scale.shape[0]
    return [
        decoded(codes[pl.ds(first + t * S, S), :].reshape(S // group, group, LANES), scale[None]).reshape(S, LANES)
        for t in range(B // LANES)
    ]


def dot(a, b, dims=((1,), (0,))):
    return lax.dot_general(a, b, (dims, ((), ())), preferred_element_type=F32)


def split(x):
    high = x.astype(BF16)
    return high, (x - high.astype(F32)).astype(BF16)


def fold(x):
    r, c = x.shape
    x = jnp.sum(x.reshape(r // 8, 8, c), axis=0)
    return functools.reduce(jnp.add, [x[:, t * LANES : (t + 1) * LANES] for t in range(c // LANES)])


def kernel(
    home_hbm, part_hbm, lroot_hbm, rroot_hbm, first_hbm, second_hbm,
    prod_in, new_first, new_second, update,
    home, part_up, part_down, part_cross, first, second, lroot, rroot,
    ring_out, ring_in, x1_out, x1_in, y2_out, y2_in, x2_out, x2_in,
    work, ghigh, glow, grow_out, grow_in, prod_out, left_codes, pleft, pright,
    sums_out, sums_other, sums_chip, sums_in, pair_out, pair_in,
    load_sem, root_send, root_recv, ring_send, ring_recv, x1_send, x1_recv, s2_send, s2_recv,
    core_send, core_recv, row_send, row_recv, sum_send, sum_recv, store_sem, ready,
):
    d = lax.axis_index("dp")
    m = lax.axis_index("mp")
    xl, y = d // NY, d % NY
    xh, z, k = m // 8, (m // 2) % 4, m % 2
    c = m // 2

    partner = (d, m + 1 - 2 * k)
    across = ((1 - xl) * NY + y, m)

    def along_y(j):
        return (xl * NY + (y + j) % NY, m)

    def chip_at(a, b):
        return ((xh + a) % 2) * 4 + (z + b) % 4

    def along_mp(a, b):
        return (d, chip_at(a, b) * 2 + k)

    def remote(src, dst, send, recv, device):
        return pltpu.make_async_remote_copy(
            src_ref=src, dst_ref=dst, send_sem=send, recv_sem=recv, device_id=device, device_id_type=MESH
        )

    parts = (part_up, part_down, part_cross)
    loads = [pltpu.make_async_copy(home_hbm, home, load_sem.at[0])]
    for i, (start, n) in enumerate(PARTS):
        loads.append(pltpu.make_async_copy(part_hbm.at[:, pl.ds(start, n)], parts[i], load_sem.at[1 + i]))
    others = ((lroot_hbm.at[c], lroot.at[c, k]), (rroot_hbm.at[c], rroot.at[c, k]), (first_hbm, first), (second_hbm, second))
    for i, (src, dst) in enumerate(others):
        loads.append(pltpu.make_async_copy(src, dst, load_sem.at[4 + i]))
    for load in loads[:4]:
        load.start()

    rank = 2 * z + xh

    def rank_of(there):
        return 2 * (there % 4) + there // 4

    barrier = pltpu.get_barrier_semaphore()
    for device in [across, partner] + [along_y(j) for j in (1, 2, 3)]:
        pl.semaphore_signal(barrier, inc=1, device_id=device, device_id_type=MESH)
    for a, b in PEERS:

        @pl.when(rank_of(chip_at(a, b)) > rank)
        def _():
            pl.semaphore_signal(barrier, inc=1, device_id=along_mp(a, b), device_id_type=MESH)

    pl.semaphore_wait(barrier, 5 + rank)
    for a, b in PEERS:

        @pl.when(rank_of(chip_at(a, b)) < rank)
        def _():
            pl.semaphore_signal(ready, inc=1, device_id=along_mp(a, b), device_id_type=MESH)

    root_copies = []
    for i, (a, b) in enumerate(PEERS):
        there = chip_at(a, b)
        for w, (src, dst) in enumerate(((lroot_hbm, lroot), (rroot_hbm, rroot))):
            root_copies.append(
                remote(src.at[there], dst.at[c, k], root_send.at[w, i], root_recv.at[w, i], along_mp(a, b))
            )

    def send_roots(early):
        for i, (a, b) in enumerate(PEERS):
            lower = rank_of(chip_at(a, b)) < rank
            for w in range(2):

                @pl.when(lower if early else jnp.logical_not(lower))
                def _():
                    if not (early and a and w):
                        root_copies[2 * i + w].start()

                if not early and a and w:

                    @pl.when(lower)
                    def _():
                        root_copies[2 * i + w].start()

    def source(q):
        return functools.reduce(jnp.maximum, [jnp.where(home[r] == q, r, 0) for r in range(NB)])

    def own_piece(w, to_x, j):
        row = source(to_x * NY + (y + j) % NY)
        return lambda t, r: parts[w][row, pl.ds(r, STRIDE), pl.ds(t * LANES, LANES)]

    to_xs = (1 - xl, xl)
    along = (1, -1)
    ring = {}

    def send_ring(kind, w, o, to, step, arrived):
        n = (kind * 2 + w) * 2 + o
        own = own_piece(w, to_xs[o], to)
        if arrived:
            encode_piece(RING, sum_of(RING, own, arrived), ring_out.at[n], work)
        else:
            encode_piece(RING, own, ring_out.at[n])
        ring[kind, w, o] = remote(
            ring_out.at[n], ring_in.at[n], ring_send.at[n], ring_recv.at[n], along_y(step % NY)
        )
        ring[kind, w, o].start()

    def got(kind, w, o):
        ring[kind, w, o].wait_recv()
        return ring_in.at[(kind * 2 + w) * 2 + o]

    def send_far(w, o):
        send_ring(0, w, o, 2, along[w], [])

    def send_back(w, o):
        send_ring(1, w, o, -along[w], -along[w], [])

    def send_on(w, o):
        send_ring(2, w, o, along[w], along[w], [got(0, w, o)])

    loads[0].wait()
    loads[1].wait()
    send_far(0, 0)
    loads[2].wait()
    send_far(1, 0)
    loads[3].wait()
    x1_copies, y2_copies, x2_copies = {}, {}, {}
    for j in (2, 1, 3, 0):
        encode_piece(CROSS, own_piece(2, 1 - xl, j), x1_out.at[j])
        x1_copies[j] = remote(x1_out.at[j], x1_in.at[j], x1_send.at[j], x1_recv.at[j], across)
        x1_copies[j].start()
        if j == 2:
            for w in range(2):
                send_far(w, 1)
    for load in loads[4:]:
        load.start()
    send_roots(True)
    send_back(1, 0)
    send_back(0, 0)
    send_on(0, 0)
    send_on(1, 0)
    send_back(1, 1)
    send_back(0, 1)
    send_on(0, 1)
    send_on(1, 1)
    for j in (2, 1, 3):
        x1_copies[j].wait_recv()
        read = sum_of(CROSS, own_piece(2, xl, j), [x1_in.at[j]])
        encode_piece(CROSS, read, y2_out.at[j - 1], work)
        y2_copies[j] = remote(y2_out.at[j - 1], y2_in.at[j - 1], s2_send.at[j], s2_recv.at[j], along_y(j))
        y2_copies[j].start()
    for w in range(2):
        read = sum_of(RING, own_piece(w, 1 - xl, 0), [got(1, w, 0), got(2, w, 0)])
        encode_piece(RING, read, x2_out.at[w], work)
        x2_copies[w] = remote(x2_out.at[w], x2_in.at[w], s2_send.at[4 * w], s2_recv.at[4 * w], across)
        x2_copies[w].start()

    @pl.when(rank < NB - 1)
    def _():
        pl.semaphore_wait(ready, NB - 1 - rank)

    send_roots(False)

    strip = pl.ds(pl.multiple_of(k * H, H), H)
    block_copies = {}

    def finish(w, arrived):
        start, n = PARTS[w]
        read = sum_of(n, own_piece(w, xl, 0), arrived)

        def step(i, carry):
            r = pl.multiple_of(i * STRIDE, STRIDE)
            for t in range(H // LANES):
                mine = pl.ds(pl.multiple_of(k * H + t * LANES, LANES), LANES)
                high, low = split(read(t, r))
                ghigh[pl.ds(start + r, STRIDE), mine] = high
                glow[pl.ds(start + r, STRIDE), mine] = low
            return carry

        lax.fori_loop(0, n // STRIDE, step, 0)
        for i, ref in enumerate((ghigh, glow)):
            here = ref.at[pl.ds(start, n), strip]
            n_sem = 2 + 2 * w + i
            block_copies[w, i] = remote(here, here, core_send.at[n_sem], core_recv.at[n_sem], partner)
            block_copies[w, i].start()

    def rows_for(there):
        return pl.ds(pl.multiple_of(there * 2 * S + k * S, S), S)

    def row_copy(there, slot):
        return remote(
            grow_out.at[there], grow_in.at[slot], row_send.at[0, there], row_recv.at[0, slot], (d, there * 2 + k)
        )

    def send_rows(w):
        for i in range(2):
            block_copies[w, i].wait_recv()
        start, n = PARTS[w]
        for there in range(start // (2 * S), (start + n) // (2 * S)):
            rows = rows_for(there)
            value = ghigh[rows, :].astype(F32) + glow[rows, :].astype(F32)
            code = encode_rows(value, T, grow_out.at[there], 0)
            grow_out[there, pl.ds(WIDE, T), :] = code.astype(I32).astype(I16)

            @pl.when(c != there)
            def _():
                row_copy(there, c).start()

    for w in range(2):
        x2_copies[w].wait_recv()
        finish(w, [got(1, w, 1), got(2, w, 1), x2_in.at[w]])
        if w:
            send_rows(0)
    x1_copies[0].wait_recv()
    for j in (2, 1, 3):
        y2_copies[j].wait_recv()
    finish(2, [x1_in.at[0]] + [y2_in.at[n] for n in range(3)])
    send_rows(1)
    send_rows(2)
    grow_in[c] = grow_out[c]

    high_rows = jnp.concatenate([ghigh[rows_for(t), :] for t in range(NB)], axis=0)
    low_rows = jnp.concatenate([glow[rows_for(t), :] for t in range(NB)], axis=0)
    nt = ((1,), (1,))
    pleft[...] = dot(high_rows, ghigh[...], nt) + (dot(high_rows, glow[...], nt) + dot(low_rows, ghigh[...], nt))
    prod_copies = []

    def send_products(w, i, first, size):
        a, b = (PEERS + [(0, 0)])[i]
        here, there = prod_out.at[i, pl.ds(first, size)], prod_in.at[c, pl.ds(first, size)]
        if a or b:
            copy = remote(here, there, row_send.at[1 + w, i], row_recv.at[1 + w, i], along_mp(a, b))
            prod_copies.append(copy)
        else:
            copy = pltpu.make_async_copy(here, there, store_sem.at[w])
            stores.append(copy)
        copy.start()

    stores = []
    for i, (a, b) in enumerate(PEERS + [(0, 0)]):
        value = pleft[pl.ds(pl.multiple_of(chip_at(a, b) * S, S), S), :]
        left_codes[i] = encode_rows(value, T // 2, prod_out.at[i], 0)
        send_products(0, i, 0, WIDE)
    tn = ((0,), (0,))
    pright[...] = dot(ghigh[...], ghigh[...], tn) + (
        dot(ghigh[...], glow[...], tn) + dot(glow[...], ghigh[...], tn)
    )
    for i, (a, b) in enumerate(PEERS + [(0, 0)]):
        code = encode_rows(pright[rows_for(chip_at(a, b)), :], T // 2, prod_out.at[i], WIDE)
        codes = jnp.concatenate([left_codes[i], code], axis=0)
        prod_out[i, pl.ds(2 * WIDE, T), :] = codes.astype(I32).astype(I16)

    for i, (a, b) in enumerate(PEERS + [(0, 0)]):
        if a or not b:
            send_products(1, i, WIDE, WIDE + T)

    for copy in root_copies:
        copy.wait_recv()
    loads[4].wait()
    loads[5].wait()
    core_copies = []
    for w, ref in enumerate((lroot, rroot)):
        copy = remote(ref.at[:, k], ref.at[:, k], core_send.at[w], core_recv.at[w], partner)
        copy.start()
        core_copies.append(copy)

    for copy in core_copies:
        copy.wait_recv()
    rcols = jnp.concatenate([rroot[a, b, :, strip] for a in range(NB) for b in range(2)], axis=0)
    inner = dot(ghigh[...], rcols) + dot(glow[...], rcols)
    inner_high, inner_low = split(inner)
    lrows = lroot[...].reshape(B, B)
    applied = dot(lrows, inner_high) + dot(lrows, inner_low)
    pright[:, pl.ds(0, H)] = applied
    pair_out[...] = fold(applied * applied)
    n = len(PEERS)
    pair_copy = remote(pair_out, pair_in, sum_send.at[n], sum_recv.at[n], partner)
    pair_copy.start()

    loads[6].wait()
    loads[7].wait()
    for a, b in PEERS + [(0, 0)]:
        slot = chip_at(-a, -b)
        if a or b:
            row_copy(slot, slot).wait_recv()
        total = jnp.zeros((8, LANES), F32)
        scale = scale_of(grow_in[slot, pl.ds(WIDE, T), :])
        for t, grad in enumerate(decode_rows(grow_in.at[slot], 0, scale)):
            cols = pl.ds(t * LANES, LANES)
            mean = FIRST_DECAY * first[slot, :, cols] + (1.0 - FIRST_DECAY) * grad
            square = SECOND_DECAY * second[slot, :, cols] + (1.0 - SECOND_DECAY) * grad * grad
            new_first[slot, :, cols] = mean
            new_second[slot, :, cols] = square
            adam = mean / (jnp.sqrt(square) + ADAM_EPS)
            total = total + fold(adam * adam)
        sums_out[slot] = total

    chip_copy = remote(sums_out, sums_other, sum_send.at[n + 1], sum_recv.at[n + 1], partner)
    chip_copy.start()
    chip_copy.wait_recv()
    sums_chip[...] = sums_out[...] + sums_other[...]
    sum_copies = []
    for i, (a, b) in enumerate(PEERS):
        copy = remote(sums_chip.at[chip_at(a, b)], sums_in.at[i], sum_send.at[i], sum_recv.at[i], along_mp(a, b))
        copy.start()
        sum_copies.append(copy)
    for i, (a, b) in enumerate(PEERS):
        if not a:
            send_products(1, i, WIDE, WIDE + T)

    pair_copy.wait_recv()
    total = sums_chip[c]
    for i, copy in enumerate(sum_copies):
        copy.wait_recv()
        total = total + sums_in[i]
    norms = [jnp.sum(x, axis=(0, 1), keepdims=True) for x in (total, pair_out[...] + pair_in[...])]
    graft = jnp.sqrt(norms[0]) / (jnp.sqrt(norms[1]) + NORM_EPS)
    update[...] = (pright[:, pl.ds(0, H)] * graft).astype(BF16)

    for copy in prod_copies:
        copy.wait_recv()
    for a, b in PEERS:
        row_copy(chip_at(a, b), c).wait_send()
    for copies in (x1_copies, y2_copies, x2_copies, ring, block_copies):
        for copy in copies.values():
            copy.wait_send()
    for copy in [pair_copy, chip_copy] + root_copies + core_copies + prod_copies + sum_copies:
        copy.wait_send()
    for store in stores:
        store.wait()


def finish_kernel(
    prod, left, right, first, second, update,
    left_out, right_out, first_out, second_out, update_out,
    new_left, new_right, sem,
):
    through = [(first, first_out), (second, second_out), (update, update_out)]
    stats = [(new_left, left_out), (new_right, right_out)]
    stores = [pltpu.make_async_copy(src, dst, sem.at[i]) for i, (src, dst) in enumerate(stats + through)]
    for store in stores[2:]:
        store.start()
    for w, (old, new) in enumerate(((left, new_left), (right, new_right))):

        def add(slot, carry):
            code = prod[slot, pl.ds(2 * WIDE, T), :].astype(F32)[w * (T // 2) : (w + 1) * (T // 2)]
            scale = jnp.exp(code * STEP) * (1.0 / FULL)
            for t, value in enumerate(decode_rows(prod.at[slot], w * WIDE, scale)):
                cols = pl.ds(t * LANES, LANES)
                new[slot, :, cols] = old[slot, :, cols] + value
            return carry

        lax.fori_loop(0, NB, add, 0)
        stores[w].start()
    for store in stores:
        store.wait()


def on_device(
    grad_parts, home, left_stat, right_stat, left_root, right_root, first_moment, second_moment
):
    in_hbm = pl.BlockSpec(memory_space=pltpu.HBM)
    in_vmem = pl.BlockSpec(memory_space=pltpu.VMEM)
    n = len(PEERS)
    ring_piece = (H // LANES * RING + T, LANES)
    cross_piece = (H // LANES * CROSS + T, LANES)
    rows = (WIDE + T, LANES)
    products = (2 * WIDE + T, LANES)
    stat = pltpu.VMEM((NB, S, B), F32)
    tile = pltpu.VMEM((B, H), BF16)
    dma = pltpu.SemaphoreType.DMA
    scratch = [
        pltpu.SMEM((NB,), I32),
        *[pltpu.VMEM((NB, size, H), F32) for _, size in PARTS],
        *[stat] * 2,
        *[pltpu.VMEM((NB, 2, S, B), BF16)] * 2,
        *[pltpu.VMEM((12, *ring_piece), I16)] * 2,
        *[pltpu.VMEM((4, *cross_piece), I16)] * 2,
        *[pltpu.VMEM((3, *cross_piece), I16)] * 2,
        *[pltpu.VMEM((2, *ring_piece), I16)] * 2,
        pltpu.VMEM((B, H), F32),
        *[pltpu.VMEM((B, B), BF16)] * 2,
        *[pltpu.VMEM((NB, *rows), I16)] * 2,
        pltpu.VMEM((NB, *products), I16),
        pltpu.VMEM((NB, T // 2, LANES), F32),
        pltpu.VMEM((H, B), F32),
        pltpu.VMEM((B, B), F32),
        *[pltpu.VMEM((NB, 8, LANES), F32)] * 3,
        pltpu.VMEM((n, 8, LANES), F32),
        *[pltpu.VMEM((8, LANES), F32)] * 2,
        dma((8,)),
        *[dma((2, n))] * 2,
        *[dma((12,))] * 2,
        *[dma((4,))] * 2,
        *[dma((5,))] * 2,
        *[dma((8,))] * 2,
        *[dma((3, NB))] * 2,
        *[dma((n + 2,))] * 2,
        dma((2,)),
        pltpu.SemaphoreType.REGULAR,
    ]
    made = pl.pallas_call(
        kernel,
        out_shape=(pltpu.VMEM((NB, *products), I16), stat, stat, tile),
        in_specs=[in_hbm] * 6,
        out_specs=[in_vmem] * 4,
        scratch_shapes=scratch,
        compiler_params=pltpu.CompilerParams(
            collective_id=0, has_side_effects=True, vmem_limit_bytes=40 * 2**20
        ),
        cost_estimate=pl.CostEstimate(flops=2 * 10**9, bytes_accessed=9 * 2**20, transcendentals=0),
        name="shampoo_step",
    )(
        *[
            pltpu.with_memory_space_constraint(x, pltpu.HBM)
            for x in (home, grad_parts.reshape(NB, B, H), left_root, right_root, first_moment, second_moment)
        ]
    )
    stat_out = jax.ShapeDtypeStruct((NB, S, B), F32)
    return pl.pallas_call(
        finish_kernel,
        out_shape=(stat_out,) * 4 + (jax.ShapeDtypeStruct((B, H), BF16),),
        in_specs=[in_vmem] * 6,
        out_specs=[in_hbm] * 5,
        scratch_shapes=[stat, stat, dma((5,))],
        compiler_params=pltpu.CompilerParams(vmem_limit_bytes=16 * 2**20),
        name="finish_outputs",
    )(made[0], left_stat, right_stat, *made[1:])


def solution(mesh):
    rows = P("dp", "mp", None)
    in_specs = (P("dp", None, "mp"), P(), rows, rows, rows, rows, rows, rows)
    out_specs = (rows, rows, rows, rows, P("dp", "mp"))
    return jax.shard_map(
        on_device, mesh=mesh, in_specs=in_specs, out_specs=out_specs, check_vma=False
    )
```

```python
import functools
import math

import jax
import jax.numpy as jnp
from jax import lax
from jax.experimental import pallas as pl
from jax.experimental.pallas import tpu as pltpu
from jax.sharding import PartitionSpec as P

FIRST_DECAY = 0.9
SECOND_DECAY = 0.999
ADAM_EPS = 1e-08
NORM_EPS = 1e-06
MESH = pl.DeviceIdType.MESH
F32 = jnp.float32
BF16 = jnp.bfloat16
I16 = jnp.int16
I32 = jnp.int32

B = 512
H = 256
PARTS = ((0, 192), (192, 192), (384, 128))
RING = PARTS[0][1]
CROSS = PARTS[2][1]
S = 32
T = 16
STRIDE = 64
LANES = 128
WIDE = B // LANES * S
NB = 8
NY = 4
FULL = 32760.0
STEP = math.log(2.0) / 4.0
TINY = 1e-30

PEERS = [(1, 2), (1, 1), (1, 3), (0, 2), (1, 0), (0, 1), (0, 3)]


def code_of(peak):
    return jnp.ceil(jnp.log(jnp.maximum(peak, TINY)) * (1.0 / STEP))


def coded(x):
    return jnp.floor(x + 0.5).astype(I32).astype(I16)


def scale_of(code):
    return jnp.exp(code.astype(I32).astype(F32) * STEP) * (1.0 / FULL)


def decoded(values, scale):
    return values.astype(I32).astype(F32) * scale


def encode_piece(n, read, out, keep=None):
    tiles = range(H // LANES)

    def look(i, peak):
        r = pl.multiple_of(i * STRIDE, STRIDE)
        for t in tiles:
            x = read(t, r)
            if keep is not None:
                keep[pl.ds(r, STRIDE), pl.ds(t * LANES, LANES)] = x
            peak = jnp.maximum(peak, jnp.max(jnp.abs(x).reshape(STRIDE // T, T, LANES), axis=0))
        return peak

    code = code_of(lax.fori_loop(0, n // STRIDE, look, jnp.zeros((T, LANES), F32)))
    factor = jnp.exp(code * -STEP) * FULL

    def write(i, carry):
        r = pl.multiple_of(i * STRIDE, STRIDE)
        for t in tiles:
            x = read(t, r) if keep is None else keep[pl.ds(r, STRIDE), pl.ds(t * LANES, LANES)]
            x = x.reshape(STRIDE // T, T, LANES) * factor[None]
            out[pl.ds(t * n + r, STRIDE), :] = coded(x).reshape(STRIDE, LANES)
        return carry

    lax.fori_loop(0, n // STRIDE, write, 0)
    out[pl.ds(H // LANES * n, T), :] = code.astype(I32).astype(I16)


def sum_of(n, own, arrived):
    scales = [scale_of(ref[pl.ds(H // LANES * n, T), :])[None] for ref in arrived]

    def read(t, r):
        x = own(t, r)
        for ref, scale in zip(arrived, scales):
            values = ref[pl.ds(t * n + r, STRIDE), :].reshape(STRIDE // T, T, LANES)
            x = x + decoded(values, scale).reshape(STRIDE, LANES)
        return x

    return read


def encode_rows(x, group, out, first):
    n = B // LANES
    parts = [x[:, t * LANES : (t + 1) * LANES].reshape(S // group, group, LANES) for t in range(n)]
    code = code_of(functools.reduce(jnp.maximum, [jnp.max(jnp.abs(p), axis=0) for p in parts]))
    factor = jnp.exp(code * -STEP) * FULL
    for t in range(n):
        out[pl.ds(first + t * S, S), :] = coded(parts[t] * factor[None]).reshape(S, LANES)
    return code


def decode_rows(codes, first, scale):
    group = scale.shape[0]
    return [
        decoded(codes[pl.ds(first + t * S, S), :].reshape(S // group, group, LANES), scale[None]).reshape(S, LANES)
        for t in range(B // LANES)
    ]


def dot(a, b, dims=((1,), (0,))):
    return lax.dot_general(a, b, (dims, ((), ())), preferred_element_type=F32)


def split(x):
    high = x.astype(BF16)
    return high, (x - high.astype(F32)).astype(BF16)


def fold(x):
    r, c = x.shape
    x = jnp.sum(x.reshape(r // 8, 8, c), axis=0)
    return functools.reduce(jnp.add, [x[:, t * LANES : (t + 1) * LANES] for t in range(c // LANES)])


def kernel(
    home_hbm, part_hbm, lroot_hbm, rroot_hbm, first_hbm, second_hbm,
    prod_in, new_first, new_second, update,
    home, part_up, part_down, part_cross, first, second, lroot, rroot,
    ring_out, ring_in, x1_out, x1_in, y2_out, y2_in, x2_out, x2_in,
    work, ghigh, glow, grow_out, grow_in, prod_out, left_codes, pleft, pright,
    sums_out, sums_in, pair_out, pair_in,
    load_sem, root_send, root_recv, ring_send, ring_recv, x1_send, x1_recv, s2_send, s2_recv,
    core_send, core_recv, row_send, row_recv, sum_send, sum_recv, store_sem, ready,
):
    d = lax.axis_index("dp")
    m = lax.axis_index("mp")
    xl, y = d // NY, d % NY
    xh, z, k = m // 8, (m // 2) % 4, m % 2
    c = m // 2

    partner = (d, m + 1 - 2 * k)
    across = ((1 - xl) * NY + y, m)

    def along_y(j):
        return (xl * NY + (y + j) % NY, m)

    def chip_at(a, b):
        return ((xh + a) % 2) * 4 + (z + b) % 4

    def along_mp(a, b, q=0):
        return (d, chip_at(a, b) * 2 + k + q * (1 - 2 * k))

    def remote(src, dst, send, recv, device):
        return pltpu.make_async_remote_copy(
            src_ref=src, dst_ref=dst, send_sem=send, recv_sem=recv, device_id=device, device_id_type=MESH
        )

    parts = (part_up, part_down, part_cross)
    loads = [pltpu.make_async_copy(home_hbm, home, load_sem.at[0])]
    for i, (start, n) in enumerate(PARTS):
        loads.append(pltpu.make_async_copy(part_hbm.at[:, pl.ds(start, n)], parts[i], load_sem.at[1 + i]))
    others = ((lroot_hbm.at[c], lroot.at[c, k]), (rroot_hbm.at[c], rroot.at[c, k]), (first_hbm, first), (second_hbm, second))
    for i, (src, dst) in enumerate(others):
        loads.append(pltpu.make_async_copy(src, dst, load_sem.at[4 + i]))
    for load in loads[:4]:
        load.start()

    rank = 2 * z + xh

    def rank_of(there):
        return 2 * (there % 4) + there // 4

    barrier = pltpu.get_barrier_semaphore()
    for device in [across, partner] + [along_y(j) for j in (1, 2, 3)]:
        pl.semaphore_signal(barrier, inc=1, device_id=device, device_id_type=MESH)
    for a, b in PEERS:

        @pl.when(rank_of(chip_at(a, b)) > rank)
        def _():
            for q in range(2):
                pl.semaphore_signal(barrier, inc=1, device_id=along_mp(a, b, q), device_id_type=MESH)

    pl.semaphore_wait(barrier, 5 + 2 * rank)
    for a, b in PEERS:

        @pl.when(rank_of(chip_at(a, b)) < rank)
        def _():
            for q in range(2):
                pl.semaphore_signal(ready, inc=1, device_id=along_mp(a, b, q), device_id_type=MESH)

    root_copies = []
    for i, (a, b) in enumerate(PEERS):
        there = chip_at(a, b)
        for w, (src, dst) in enumerate(((lroot_hbm, lroot), (rroot_hbm, rroot))):
            root_copies.append(
                remote(src.at[there], dst.at[c, k], root_send.at[w, i], root_recv.at[w, i], along_mp(a, b))
            )

    def send_roots(early):
        for i, (a, b) in enumerate(PEERS):
            lower = rank_of(chip_at(a, b)) < rank
            for w in range(2):

                @pl.when(lower if early else jnp.logical_not(lower))
                def _():
                    if not (early and a and w):
                        root_copies[2 * i + w].start()

                if not early and a and w:

                    @pl.when(lower)
                    def _():
                        root_copies[2 * i + w].start()

    def source(q):
        return functools.reduce(jnp.maximum, [jnp.where(home[r] == q, r, 0) for r in range(NB)])

    def own_piece(w, to_x, j):
        row = source(to_x * NY + (y + j) % NY)
        return lambda t, r: parts[w][row, pl.ds(r, STRIDE), pl.ds(t * LANES, LANES)]

    to_xs = (1 - xl, xl)
    along = (1, -1)
    ring = {}

    def send_ring(kind, w, o, to, step, arrived):
        n = (kind * 2 + w) * 2 + o
        own = own_piece(w, to_xs[o], to)
        if arrived:
            encode_piece(RING, sum_of(RING, own, arrived), ring_out.at[n], work)
        else:
            encode_piece(RING, own, ring_out.at[n])
        ring[kind, w, o] = remote(
            ring_out.at[n], ring_in.at[n], ring_send.at[n], ring_recv.at[n], along_y(step % NY)
        )
        ring[kind, w, o].start()

    def got(kind, w, o):
        ring[kind, w, o].wait_recv()
        return ring_in.at[(kind * 2 + w) * 2 + o]

    def send_far(w, o):
        send_ring(0, w, o, 2, along[w], [])

    def send_back(w, o):
        send_ring(1, w, o, -along[w], -along[w], [])

    def send_on(w, o):
        send_ring(2, w, o, along[w], along[w], [got(0, w, o)])

    loads[0].wait()
    loads[1].wait()
    send_far(0, 0)
    loads[2].wait()
    send_far(1, 0)
    loads[3].wait()
    x1_copies, y2_copies, x2_copies = {}, {}, {}
    for j in (2, 1, 3, 0):
        encode_piece(CROSS, own_piece(2, 1 - xl, j), x1_out.at[j])
        x1_copies[j] = remote(x1_out.at[j], x1_in.at[j], x1_send.at[j], x1_recv.at[j], across)
        x1_copies[j].start()
        if j == 2:
            for w in range(2):
                send_far(w, 1)
    for load in loads[4:]:
        load.start()
    send_roots(True)
    send_back(1, 0)
    send_back(0, 0)
    send_on(0, 0)
    send_on(1, 0)
    send_back(1, 1)
    send_back(0, 1)
    send_on(0, 1)
    send_on(1, 1)
    for j in (2, 1, 3):
        x1_copies[j].wait_recv()
        read = sum_of(CROSS, own_piece(2, xl, j), [x1_in.at[j]])
        encode_piece(CROSS, read, y2_out.at[j - 1], work)
        y2_copies[j] = remote(y2_out.at[j - 1], y2_in.at[j - 1], s2_send.at[j], s2_recv.at[j], along_y(j))
        y2_copies[j].start()
    for w in range(2):
        read = sum_of(RING, own_piece(w, 1 - xl, 0), [got(1, w, 0), got(2, w, 0)])
        encode_piece(RING, read, x2_out.at[w], work)
        x2_copies[w] = remote(x2_out.at[w], x2_in.at[w], s2_send.at[4 * w], s2_recv.at[4 * w], across)
        x2_copies[w].start()

    @pl.when(rank < NB - 1)
    def _():
        pl.semaphore_wait(ready, 2 * (NB - 1 - rank))

    send_roots(False)

    strip = pl.ds(pl.multiple_of(k * H, H), H)
    block_copies = {}

    def finish(w, arrived):
        start, n = PARTS[w]
        read = sum_of(n, own_piece(w, xl, 0), arrived)

        def step(i, carry):
            r = pl.multiple_of(i * STRIDE, STRIDE)
            for t in range(H // LANES):
                mine = pl.ds(pl.multiple_of(k * H + t * LANES, LANES), LANES)
                high, low = split(read(t, r))
                ghigh[pl.ds(start + r, STRIDE), mine] = high
                glow[pl.ds(start + r, STRIDE), mine] = low
            return carry

        lax.fori_loop(0, n // STRIDE, step, 0)
        for i, ref in enumerate((ghigh, glow)):
            here = ref.at[pl.ds(start, n), strip]
            n_sem = 2 + 2 * w + i
            block_copies[w, i] = remote(here, here, core_send.at[n_sem], core_recv.at[n_sem], partner)
            block_copies[w, i].start()

    def rows_for(there):
        return pl.ds(pl.multiple_of(there * 2 * S + k * S, S), S)

    def row_copy(there, slot):
        return remote(
            grow_out.at[there], grow_in.at[slot], row_send.at[0, there], row_recv.at[0, slot], (d, there * 2 + k)
        )

    def send_rows(w):
        for i in range(2):
            block_copies[w, i].wait_recv()
        start, n = PARTS[w]
        for there in range(start // (2 * S), (start + n) // (2 * S)):
            rows = rows_for(there)
            value = ghigh[rows, :].astype(F32) + glow[rows, :].astype(F32)
            code = encode_rows(value, T, grow_out.at[there], 0)
            grow_out[there, pl.ds(WIDE, T), :] = code.astype(I32).astype(I16)

            @pl.when(c != there)
            def _():
                row_copy(there, c).start()

    for w in range(2):
        x2_copies[w].wait_recv()
        finish(w, [got(1, w, 1), got(2, w, 1), x2_in.at[w]])
        if w:
            send_rows(0)
    x1_copies[0].wait_recv()
    for j in (2, 1, 3):
        y2_copies[j].wait_recv()
    finish(2, [x1_in.at[0]] + [y2_in.at[n] for n in range(3)])
    send_rows(1)
    send_rows(2)
    grow_in[c] = grow_out[c]

    high_rows = jnp.concatenate([ghigh[rows_for(t), :] for t in range(NB)], axis=0)
    low_rows = jnp.concatenate([glow[rows_for(t), :] for t in range(NB)], axis=0)
    nt = ((1,), (1,))
    pleft[...] = dot(high_rows, ghigh[...], nt) + (dot(high_rows, glow[...], nt) + dot(low_rows, ghigh[...], nt))
    prod_copies = []

    def send_products(w, i, first, size):
        a, b = (PEERS + [(0, 0)])[i]
        here, there = prod_out.at[i, pl.ds(first, size)], prod_in.at[c, pl.ds(first, size)]
        if a or b:
            copy = remote(here, there, row_send.at[1 + w, i], row_recv.at[1 + w, i], along_mp(a, b))
            prod_copies.append(copy)
        else:
            copy = pltpu.make_async_copy(here, there, store_sem.at[w])
            stores.append(copy)
        copy.start()

    stores = []
    for i, (a, b) in enumerate(PEERS + [(0, 0)]):
        value = pleft[pl.ds(pl.multiple_of(chip_at(a, b) * S, S), S), :]
        left_codes[i] = encode_rows(value, T // 2, prod_out.at[i], 0)
        send_products(0, i, 0, WIDE)
    tn = ((0,), (0,))
    pright[...] = dot(ghigh[...], ghigh[...], tn) + (
        dot(ghigh[...], glow[...], tn) + dot(glow[...], ghigh[...], tn)
    )
    for i, (a, b) in enumerate(PEERS + [(0, 0)]):
        code = encode_rows(pright[rows_for(chip_at(a, b)), :], T // 2, prod_out.at[i], WIDE)
        codes = jnp.concatenate([left_codes[i], code], axis=0)
        prod_out[i, pl.ds(2 * WIDE, T), :] = codes.astype(I32).astype(I16)

    for i, (a, b) in enumerate(PEERS + [(0, 0)]):
        if a or not b:
            send_products(1, i, WIDE, WIDE + T)

    for copy in root_copies:
        copy.wait_recv()
    loads[4].wait()
    loads[5].wait()
    core_copies = []
    for w, ref in enumerate((lroot, rroot)):
        copy = remote(ref.at[:, k], ref.at[:, k], core_send.at[w], core_recv.at[w], partner)
        copy.start()
        core_copies.append(copy)

    for copy in core_copies:
        copy.wait_recv()
    rcols = jnp.concatenate([rroot[a, b, :, strip] for a in range(NB) for b in range(2)], axis=0)
    inner = dot(ghigh[...], rcols) + dot(glow[...], rcols)
    inner_high, inner_low = split(inner)
    lrows = lroot[...].reshape(B, B)
    applied = dot(lrows, inner_high) + dot(lrows, inner_low)
    pright[:, pl.ds(0, H)] = applied
    pair_out[...] = fold(applied * applied)
    n = len(PEERS)
    pair_copy = remote(pair_out, pair_in, sum_send.at[2 * n], sum_recv.at[2 * n], partner)
    pair_copy.start()

    loads[6].wait()
    loads[7].wait()
    sum_copies = []
    for i, (a, b) in reversed(list(enumerate(PEERS + [(0, 0)]))):
        slot = chip_at(-a, -b)
        if a or b:
            row_copy(slot, slot).wait_recv()
        total = jnp.zeros((8, LANES), F32)
        scale = scale_of(grow_in[slot, pl.ds(WIDE, T), :])
        for t, grad in enumerate(decode_rows(grow_in.at[slot], 0, scale)):
            cols = pl.ds(t * LANES, LANES)
            mean = FIRST_DECAY * first[slot, :, cols] + (1.0 - FIRST_DECAY) * grad
            square = SECOND_DECAY * second[slot, :, cols] + (1.0 - SECOND_DECAY) * grad * grad
            new_first[slot, :, cols] = mean
            new_second[slot, :, cols] = square
            adam = mean / (jnp.sqrt(square) + ADAM_EPS)
            total = total + fold(adam * adam)
        sums_out[i] = total
        for q in range(2):
            if a or b or q:
                copy = remote(
                    sums_out.at[i], sums_in.at[2 * i + q], sum_send.at[2 * i + q], sum_recv.at[2 * i + q],
                    along_mp(-a, -b, q),
                )
                copy.start()
                sum_copies.append(copy)
    for i, (a, b) in enumerate(PEERS):
        if not a:
            send_products(1, i, WIDE, WIDE + T)

    pair_copy.wait_recv()
    for copy in sum_copies:
        copy.wait_recv()
    total = sums_out[n]
    for i in range(2 * NB):
        if i != 2 * n:
            total = total + sums_in[i]
    norms = [jnp.sum(x, axis=(0, 1), keepdims=True) for x in (total, pair_out[...] + pair_in[...])]
    graft = jnp.sqrt(norms[0]) / (jnp.sqrt(norms[1]) + NORM_EPS)
    update[...] = (pright[:, pl.ds(0, H)] * graft).astype(BF16)

    for copy in prod_copies:
        copy.wait_recv()
    for a, b in PEERS:
        row_copy(chip_at(a, b), c).wait_send()
    for copies in (x1_copies, y2_copies, x2_copies, ring, block_copies):
        for copy in copies.values():
            copy.wait_send()
    for copy in [pair_copy] + root_copies + core_copies + prod_copies + sum_copies:
        copy.wait_send()
    for store in stores:
        store.wait()


def finish_kernel(
    prod, left, right, first, second, update,
    left_out, right_out, first_out, second_out, update_out,
    new_left, new_right, sem,
):
    through = [(first, first_out), (second, second_out), (update, update_out)]
    stats = [(new_left, left_out), (new_right, right_out)]
    stores = [pltpu.make_async_copy(src, dst, sem.at[i]) for i, (src, dst) in enumerate(stats + through)]
    for store in stores[2:]:
        store.start()
    for w, (old, new) in enumerate(((left, new_left), (right, new_right))):

        def add(slot, carry):
            code = prod[slot, pl.ds(2 * WIDE, T), :].astype(F32)[w * (T // 2) : (w + 1) * (T // 2)]
            scale = jnp.exp(code * STEP) * (1.0 / FULL)
            for t, value in enumerate(decode_rows(prod.at[slot], w * WIDE, scale)):
                cols = pl.ds(t * LANES, LANES)
                new[slot, :, cols] = old[slot, :, cols] + value
            return carry

        lax.fori_loop(0, NB, add, 0)
        stores[w].start()
    for store in stores:
        store.wait()


def on_device(
    grad_parts, home, left_stat, right_stat, left_root, right_root, first_moment, second_moment
):
    in_hbm = pl.BlockSpec(memory_space=pltpu.HBM)
    in_vmem = pl.BlockSpec(memory_space=pltpu.VMEM)
    n = len(PEERS)
    ring_piece = (H // LANES * RING + T, LANES)
    cross_piece = (H // LANES * CROSS + T, LANES)
    rows = (WIDE + T, LANES)
    products = (2 * WIDE + T, LANES)
    stat = pltpu.VMEM((NB, S, B), F32)
    tile = pltpu.VMEM((B, H), BF16)
    dma = pltpu.SemaphoreType.DMA
    scratch = [
        pltpu.SMEM((NB,), I32),
        *[pltpu.VMEM((NB, size, H), F32) for _, size in PARTS],
        *[stat] * 2,
        *[pltpu.VMEM((NB, 2, S, B), BF16)] * 2,
        *[pltpu.VMEM((12, *ring_piece), I16)] * 2,
        *[pltpu.VMEM((4, *cross_piece), I16)] * 2,
        *[pltpu.VMEM((3, *cross_piece), I16)] * 2,
        *[pltpu.VMEM((2, *ring_piece), I16)] * 2,
        pltpu.VMEM((B, H), F32),
        *[pltpu.VMEM((B, B), BF16)] * 2,
        *[pltpu.VMEM((NB, *rows), I16)] * 2,
        pltpu.VMEM((NB, *products), I16),
        pltpu.VMEM((NB, T // 2, LANES), F32),
        pltpu.VMEM((H, B), F32),
        pltpu.VMEM((B, B), F32),
        pltpu.VMEM((NB, 8, LANES), F32),
        pltpu.VMEM((2 * NB, 8, LANES), F32),
        *[pltpu.VMEM((8, LANES), F32)] * 2,
        dma((8,)),
        *[dma((2, n))] * 2,
        *[dma((12,))] * 2,
        *[dma((4,))] * 2,
        *[dma((5,))] * 2,
        *[dma((8,))] * 2,
        *[dma((3, NB))] * 2,
        *[dma((2 * NB,))] * 2,
        dma((2,)),
        pltpu.SemaphoreType.REGULAR,
    ]
    made = pl.pallas_call(
        kernel,
        out_shape=(pltpu.VMEM((NB, *products), I16), stat, stat, tile),
        in_specs=[in_hbm] * 6,
        out_specs=[in_vmem] * 4,
        scratch_shapes=scratch,
        compiler_params=pltpu.CompilerParams(
            collective_id=0, has_side_effects=True, vmem_limit_bytes=40 * 2**20
        ),
        cost_estimate=pl.CostEstimate(flops=2 * 10**9, bytes_accessed=9 * 2**20, transcendentals=0),
        name="shampoo_step",
    )(
        *[
            pltpu.with_memory_space_constraint(x, pltpu.HBM)
            for x in (home, grad_parts.reshape(NB, B, H), left_root, right_root, first_moment, second_moment)
        ]
    )
    stat_out = jax.ShapeDtypeStruct((NB, S, B), F32)
    return pl.pallas_call(
        finish_kernel,
        out_shape=(stat_out,) * 4 + (jax.ShapeDtypeStruct((B, H), BF16),),
        in_specs=[in_vmem] * 6,
        out_specs=[in_hbm] * 5,
        scratch_shapes=[stat, stat, dma((5,))],
        compiler_params=pltpu.CompilerParams(vmem_limit_bytes=16 * 2**20),
        name="finish_outputs",
    )(made[0], left_stat, right_stat, *made[1:])


def solution(mesh):
    rows = P("dp", "mp", None)
    in_specs = (P("dp", None, "mp"), P(), rows, rows, rows, rows, rows, rows)
    out_specs = (rows, rows, rows, rows, P("dp", "mp"))
    return jax.shard_map(
        on_device, mesh=mesh, in_specs=in_specs, out_specs=out_specs, check_vma=False
    )
```

```python
import functools
import math

import jax
import jax.numpy as jnp
from jax import lax
from jax.experimental import pallas as pl
from jax.experimental.pallas import tpu as pltpu
from jax.sharding import PartitionSpec as P

FIRST_DECAY = 0.9
SECOND_DECAY = 0.999
ADAM_EPS = 1e-08
NORM_EPS = 1e-06
MESH = pl.DeviceIdType.MESH
F32 = jnp.float32
BF16 = jnp.bfloat16
I16 = jnp.int16
I32 = jnp.int32

B = 512
H = 256
PARTS = ((0, 192), (192, 192), (384, 128))
RING = PARTS[0][1]
CROSS = PARTS[2][1]
S = 32
T = 16
STRIDE = 64
LANES = 128
WIDE = B // LANES * S
NB = 8
NY = 4
FULL = 32760.0
STEP = math.log(2.0) / 4.0
TINY = 1e-30

PEERS = [(1, 2), (1, 1), (1, 3), (0, 2), (1, 0), (0, 1), (0, 3)]
BY_RANK = (0, 4, 1, 5, 2, 6, 3, 7)


def code_of(peak):
    return jnp.ceil(jnp.log(jnp.maximum(peak, TINY)) * (1.0 / STEP))


def coded(x):
    return jnp.floor(x + 0.5).astype(I32).astype(I16)


def scale_of(code):
    return jnp.exp(code.astype(I32).astype(F32) * STEP) * (1.0 / FULL)


def decoded(values, scale):
    return values.astype(I32).astype(F32) * scale


def encode_piece(n, read, out, keep=None):
    tiles = range(H // LANES)

    def look(i, peak):
        r = pl.multiple_of(i * STRIDE, STRIDE)
        for t in tiles:
            x = read(t, r)
            if keep is not None:
                keep[pl.ds(r, STRIDE), pl.ds(t * LANES, LANES)] = x
            peak = jnp.maximum(peak, jnp.max(jnp.abs(x).reshape(STRIDE // T, T, LANES), axis=0))
        return peak

    code = code_of(lax.fori_loop(0, n // STRIDE, look, jnp.zeros((T, LANES), F32)))
    factor = jnp.exp(code * -STEP) * FULL

    def write(i, carry):
        r = pl.multiple_of(i * STRIDE, STRIDE)
        for t in tiles:
            x = read(t, r) if keep is None else keep[pl.ds(r, STRIDE), pl.ds(t * LANES, LANES)]
            x = x.reshape(STRIDE // T, T, LANES) * factor[None]
            out[pl.ds(t * n + r, STRIDE), :] = coded(x).reshape(STRIDE, LANES)
        return carry

    lax.fori_loop(0, n // STRIDE, write, 0)
    out[pl.ds(H // LANES * n, T), :] = code.astype(I32).astype(I16)


def sum_of(n, own, arrived):
    scales = [scale_of(ref[pl.ds(H // LANES * n, T), :])[None] for ref in arrived]

    def read(t, r):
        x = own(t, r)
        for ref, scale in zip(arrived, scales):
            values = ref[pl.ds(t * n + r, STRIDE), :].reshape(STRIDE // T, T, LANES)
            x = x + decoded(values, scale).reshape(STRIDE, LANES)
        return x

    return read


def encode_rows(x, group, out, first):
    n = B // LANES
    parts = [x[:, t * LANES : (t + 1) * LANES].reshape(S // group, group, LANES) for t in range(n)]
    code = code_of(functools.reduce(jnp.maximum, [jnp.max(jnp.abs(p), axis=0) for p in parts]))
    factor = jnp.exp(code * -STEP) * FULL
    for t in range(n):
        out[pl.ds(first + t * S, S), :] = coded(parts[t] * factor[None]).reshape(S, LANES)
    return code


def decode_rows(codes, first, scale):
    group = scale.shape[0]
    return [
        decoded(codes[pl.ds(first + t * S, S), :].reshape(S // group, group, LANES), scale[None]).reshape(S, LANES)
        for t in range(B // LANES)
    ]


def dot(a, b, dims=((1,), (0,))):
    return lax.dot_general(a, b, (dims, ((), ())), preferred_element_type=F32)


def split(x):
    high = x.astype(BF16)
    return high, (x - high.astype(F32)).astype(BF16)


def fold(x):
    r, c = x.shape
    x = jnp.sum(x.reshape(r // 8, 8, c), axis=0)
    return functools.reduce(jnp.add, [x[:, t * LANES : (t + 1) * LANES] for t in range(c // LANES)])


def kernel(
    home_hbm, part_hbm, lroot_hbm, rroot_hbm, first_hbm, second_hbm,
    prod_in, new_first, new_second, update,
    home, part_up, part_down, part_cross, first, second, lroot, rroot,
    ring_out, ring_in, x1_out, x1_in, y2_out, y2_in, x2_out, x2_in,
    work, ghigh, glow, grow_out, grow_in, prod_out, left_codes, pleft, pright,
    sums_out, sums_other, sums_chip, sums_in, pair_out, pair_in,
    load_sem, root_send, root_recv, ring_send, ring_recv, x1_send, x1_recv, s2_send, s2_recv,
    core_send, core_recv, row_send, row_recv, sum_send, sum_recv, store_sem, ready,
):
    d = lax.axis_index("dp")
    m = lax.axis_index("mp")
    xl, y = d // NY, d % NY
    xh, z, k = m // 8, (m // 2) % 4, m % 2
    c = m // 2

    partner = (d, m + 1 - 2 * k)
    across = ((1 - xl) * NY + y, m)

    def along_y(j):
        return (xl * NY + (y + j) % NY, m)

    def chip_at(a, b):
        return ((xh + a) % 2) * 4 + (z + b) % 4

    def along_mp(a, b):
        return (d, chip_at(a, b) * 2 + k)

    def remote(src, dst, send, recv, device):
        return pltpu.make_async_remote_copy(
            src_ref=src, dst_ref=dst, send_sem=send, recv_sem=recv, device_id=device, device_id_type=MESH
        )

    parts = (part_up, part_down, part_cross)
    loads = [pltpu.make_async_copy(home_hbm, home, load_sem.at[0])]
    for i, (start, n) in enumerate(PARTS):
        loads.append(pltpu.make_async_copy(part_hbm.at[:, pl.ds(start, n)], parts[i], load_sem.at[1 + i]))
    others = ((lroot_hbm.at[c], lroot.at[c, k]), (rroot_hbm.at[c], rroot.at[c, k]), (first_hbm, first), (second_hbm, second))
    for i, (src, dst) in enumerate(others):
        loads.append(pltpu.make_async_copy(src, dst, load_sem.at[4 + i]))
    for load in loads[:4]:
        load.start()

    rank = 2 * z + xh

    def rank_of(there):
        return 2 * (there % 4) + there // 4

    barrier = pltpu.get_barrier_semaphore()
    for device in [across, partner] + [along_y(j) for j in (1, 2, 3)]:
        pl.semaphore_signal(barrier, inc=1, device_id=device, device_id_type=MESH)
    for a, b in PEERS:

        @pl.when(rank_of(chip_at(a, b)) > rank)
        def _():
            pl.semaphore_signal(barrier, inc=1, device_id=along_mp(a, b), device_id_type=MESH)

    pl.semaphore_wait(barrier, 5 + rank)
    for a, b in PEERS:

        @pl.when(rank_of(chip_at(a, b)) < rank)
        def _():
            pl.semaphore_signal(ready, inc=1, device_id=along_mp(a, b), device_id_type=MESH)

    root_copies = []
    for i, (a, b) in enumerate(PEERS):
        there = chip_at(a, b)
        for w, (src, dst) in enumerate(((lroot_hbm, lroot), (rroot_hbm, rroot))):
            root_copies.append(
                remote(src.at[there], dst.at[c, k], root_send.at[w, i], root_recv.at[w, i], along_mp(a, b))
            )

    def send_roots(early):
        for i, (a, b) in enumerate(PEERS):
            lower = rank_of(chip_at(a, b)) < rank
            for w in range(2):

                @pl.when(lower if early else jnp.logical_not(lower))
                def _():
                    if not (early and a and w):
                        root_copies[2 * i + w].start()

                if not early and a and w:

                    @pl.when(lower)
                    def _():
                        root_copies[2 * i + w].start()

    def source(q):
        return functools.reduce(jnp.maximum, [jnp.where(home[r] == q, r, 0) for r in range(NB)])

    def own_piece(w, to_x, j):
        row = source(to_x * NY + (y + j) % NY)
        return lambda t, r: parts[w][row, pl.ds(r, STRIDE), pl.ds(t * LANES, LANES)]

    to_xs = (1 - xl, xl)
    along = (1, -1)
    ring = {}

    def send_ring(kind, w, o, to, step, arrived):
        n = (kind * 2 + w) * 2 + o
        own = own_piece(w, to_xs[o], to)
        if arrived:
            encode_piece(RING, sum_of(RING, own, arrived), ring_out.at[n], work)
        else:
            encode_piece(RING, own, ring_out.at[n])
        ring[kind, w, o] = remote(
            ring_out.at[n], ring_in.at[n], ring_send.at[n], ring_recv.at[n], along_y(step % NY)
        )
        ring[kind, w, o].start()

    def got(kind, w, o):
        ring[kind, w, o].wait_recv()
        return ring_in.at[(kind * 2 + w) * 2 + o]

    def send_far(w, o):
        send_ring(0, w, o, 2, along[w], [])

    def send_back(w, o):
        send_ring(1, w, o, -along[w], -along[w], [])

    def send_on(w, o):
        send_ring(2, w, o, along[w], along[w], [got(0, w, o)])

    loads[0].wait()
    loads[1].wait()
    send_far(0, 0)
    loads[2].wait()
    send_far(1, 0)
    loads[3].wait()
    x1_copies, y2_copies, x2_copies = {}, {}, {}
    for j in (2, 1, 3, 0):
        encode_piece(CROSS, own_piece(2, 1 - xl, j), x1_out.at[j])
        x1_copies[j] = remote(x1_out.at[j], x1_in.at[j], x1_send.at[j], x1_recv.at[j], across)
        x1_copies[j].start()
        if j == 2:
            for w in range(2):
                send_far(w, 1)
    for load in loads[4:]:
        load.start()
    send_back(1, 0)
    send_back(0, 0)
    send_on(0, 0)
    send_on(1, 0)
    send_back(1, 1)
    send_back(0, 1)
    send_roots(True)
    send_on(0, 1)
    send_on(1, 1)
    for j in (2, 1, 3):
        x1_copies[j].wait_recv()
        read = sum_of(CROSS, own_piece(2, xl, j), [x1_in.at[j]])
        encode_piece(CROSS, read, y2_out.at[j - 1], work)
        y2_copies[j] = remote(y2_out.at[j - 1], y2_in.at[j - 1], s2_send.at[j], s2_recv.at[j], along_y(j))
        y2_copies[j].start()
    for w in range(2):
        read = sum_of(RING, own_piece(w, 1 - xl, 0), [got(1, w, 0), got(2, w, 0)])
        encode_piece(RING, read, x2_out.at[w], work)
        x2_copies[w] = remote(x2_out.at[w], x2_in.at[w], s2_send.at[4 * w], s2_recv.at[4 * w], across)
        x2_copies[w].start()

    @pl.when(rank < NB - 1)
    def _():
        pl.semaphore_wait(ready, NB - 1 - rank)

    send_roots(False)

    strip = pl.ds(pl.multiple_of(k * H, H), H)
    block_copies = {}

    def finish(w, arrived):
        start, n = PARTS[w]
        read = sum_of(n, own_piece(w, xl, 0), arrived)

        def step(i, carry):
            r = pl.multiple_of(i * STRIDE, STRIDE)
            for t in range(H // LANES):
                mine = pl.ds(pl.multiple_of(k * H + t * LANES, LANES), LANES)
                high, low = split(read(t, r))
                ghigh[pl.ds(start + r, STRIDE), mine] = high
                glow[pl.ds(start + r, STRIDE), mine] = low
            return carry

        lax.fori_loop(0, n // STRIDE, step, 0)
        for i, ref in enumerate((ghigh, glow)):
            here = ref.at[pl.ds(start, n), strip]
            n_sem = 2 + 2 * w + i
            block_copies[w, i] = remote(here, here, core_send.at[n_sem], core_recv.at[n_sem], partner)
            block_copies[w, i].start()

    def rows_for(there):
        return pl.ds(pl.multiple_of(there * 2 * S + k * S, S), S)

    def row_copy(there, slot):
        return remote(
            grow_out.at[there], grow_in.at[slot], row_send.at[0, there], row_recv.at[0, slot], (d, there * 2 + k)
        )

    def send_rows(w):
        for i in range(2):
            block_copies[w, i].wait_recv()
        start, n = PARTS[w]
        for there in range(start // (2 * S), (start + n) // (2 * S)):
            rows = rows_for(there)
            value = ghigh[rows, :].astype(F32) + glow[rows, :].astype(F32)
            code = encode_rows(value, T, grow_out.at[there], 0)
            grow_out[there, pl.ds(WIDE, T), :] = code.astype(I32).astype(I16)

            @pl.when(c != there)
            def _():
                row_copy(there, c).start()

    for w in range(2):
        x2_copies[w].wait_recv()
        finish(w, [got(1, w, 1), got(2, w, 1), x2_in.at[w]])
        if w:
            send_rows(0)
    x1_copies[0].wait_recv()
    for j in (2, 1, 3):
        y2_copies[j].wait_recv()
    finish(2, [x1_in.at[0]] + [y2_in.at[n] for n in range(3)])
    send_rows(1)
    send_rows(2)
    grow_in[c] = grow_out[c]

    high_rows = jnp.concatenate([ghigh[rows_for(t), :] for t in range(NB)], axis=0)
    low_rows = jnp.concatenate([glow[rows_for(t), :] for t in range(NB)], axis=0)
    nt = ((1,), (1,))
    pleft[...] = dot(high_rows, ghigh[...], nt) + (dot(high_rows, glow[...], nt) + dot(low_rows, ghigh[...], nt))
    prod_copies = []

    def send_products(w, i, first, size):
        a, b = (PEERS + [(0, 0)])[i]
        here, there = prod_out.at[i, pl.ds(first, size)], prod_in.at[c, pl.ds(first, size)]
        if a or b:
            copy = remote(here, there, row_send.at[1 + w, i], row_recv.at[1 + w, i], along_mp(a, b))
            prod_copies.append(copy)
        else:
            copy = pltpu.make_async_copy(here, there, store_sem.at[w])
            stores.append(copy)
        copy.start()

    stores = []
    for i, (a, b) in enumerate(PEERS + [(0, 0)]):
        value = pleft[pl.ds(pl.multiple_of(chip_at(a, b) * S, S), S), :]
        left_codes[i] = encode_rows(value, T // 2, prod_out.at[i], 0)
        send_products(0, i, 0, WIDE)
    tn = ((0,), (0,))
    pright[...] = dot(ghigh[...], ghigh[...], tn) + (
        dot(ghigh[...], glow[...], tn) + dot(glow[...], ghigh[...], tn)
    )
    for i, (a, b) in enumerate(PEERS + [(0, 0)]):
        code = encode_rows(pright[rows_for(chip_at(a, b)), :], T // 2, prod_out.at[i], WIDE)
        codes = jnp.concatenate([left_codes[i], code], axis=0)
        prod_out[i, pl.ds(2 * WIDE, T), :] = codes.astype(I32).astype(I16)

    for i, (a, b) in enumerate(PEERS + [(0, 0)]):
        if a or not b:
            send_products(1, i, WIDE, WIDE + T)

    for copy in root_copies:
        copy.wait_recv()
    loads[4].wait()
    loads[5].wait()
    core_copies = []
    for w, ref in enumerate((lroot, rroot)):
        copy = remote(ref.at[:, k], ref.at[:, k], core_send.at[w], core_recv.at[w], partner)
        copy.start()
        core_copies.append(copy)

    for copy in core_copies:
        copy.wait_recv()
    rcols = jnp.concatenate([rroot[a, b, :, strip] for a in range(NB) for b in range(2)], axis=0)
    inner = dot(ghigh[...], rcols) + dot(glow[...], rcols)
    inner_high, inner_low = split(inner)
    lrows = lroot[...].reshape(B, B)
    applied = dot(lrows, inner_high) + dot(lrows, inner_low)
    pright[:, pl.ds(0, H)] = applied
    pair_out[...] = fold(applied * applied)
    n = len(PEERS)
    pair_copy = remote(pair_out, pair_in, sum_send.at[n], sum_recv.at[n], partner)
    pair_copy.start()

    for copies in (x1_copies, y2_copies, x2_copies, ring, block_copies):
        for copy in copies.values():
            copy.wait_send()
    for copy in root_copies + core_copies:
        copy.wait_send()

    loads[6].wait()
    loads[7].wait()
    for slot in BY_RANK:

        @pl.when(c != slot)
        def _():
            row_copy(slot, slot).wait_recv()

        total = jnp.zeros((8, LANES), F32)
        scale = scale_of(grow_in[slot, pl.ds(WIDE, T), :])
        for t, grad in enumerate(decode_rows(grow_in.at[slot], 0, scale)):
            cols = pl.ds(t * LANES, LANES)
            mean = FIRST_DECAY * first[slot, :, cols] + (1.0 - FIRST_DECAY) * grad
            square = SECOND_DECAY * second[slot, :, cols] + (1.0 - SECOND_DECAY) * grad * grad
            new_first[slot, :, cols] = mean
            new_second[slot, :, cols] = square
            adam = mean / (jnp.sqrt(square) + ADAM_EPS)
            total = total + fold(adam * adam)
        sums_out[slot] = total

    chip_copy = remote(sums_out, sums_other, sum_send.at[n + 1], sum_recv.at[n + 1], partner)
    chip_copy.start()
    chip_copy.wait_recv()
    sums_chip[...] = sums_out[...] + sums_other[...]
    sum_copies = []
    for i, (a, b) in enumerate(PEERS):
        copy = remote(sums_chip.at[chip_at(a, b)], sums_in.at[i], sum_send.at[i], sum_recv.at[i], along_mp(a, b))
        copy.start()
        sum_copies.append(copy)
    for i, (a, b) in enumerate(PEERS):
        if not a:
            send_products(1, i, WIDE, WIDE + T)

    pair_copy.wait_recv()
    total = sums_chip[c]
    for i, copy in enumerate(sum_copies):
        copy.wait_recv()
        total = total + sums_in[i]
    norms = [jnp.sum(x, axis=(0, 1), keepdims=True) for x in (total, pair_out[...] + pair_in[...])]
    graft = jnp.sqrt(norms[0]) / (jnp.sqrt(norms[1]) + NORM_EPS)
    update[...] = (pright[:, pl.ds(0, H)] * graft).astype(BF16)

    for copy in prod_copies:
        copy.wait_recv()
    for a, b in PEERS:
        row_copy(chip_at(a, b), c).wait_send()
    for copy in [pair_copy, chip_copy] + prod_copies + sum_copies:
        copy.wait_send()
    for store in stores:
        store.wait()


def finish_kernel(
    prod, left, right, first, second, update,
    left_out, right_out, first_out, second_out, update_out,
    new_left, new_right, sem,
):
    through = [(first, first_out), (second, second_out), (update, update_out)]
    stats = [(new_left, left_out), (new_right, right_out)]
    stores = [pltpu.make_async_copy(src, dst, sem.at[i]) for i, (src, dst) in enumerate(stats + through)]
    for store in stores[2:]:
        store.start()
    for w, (old, new) in enumerate(((left, new_left), (right, new_right))):

        def add(slot, carry):
            code = prod[slot, pl.ds(2 * WIDE, T), :].astype(F32)[w * (T // 2) : (w + 1) * (T // 2)]
            scale = jnp.exp(code * STEP) * (1.0 / FULL)
            for t, value in enumerate(decode_rows(prod.at[slot], w * WIDE, scale)):
                cols = pl.ds(t * LANES, LANES)
                new[slot, :, cols] = old[slot, :, cols] + value
            return carry

        lax.fori_loop(0, NB, add, 0)
        stores[w].start()
    for store in stores:
        store.wait()


def on_device(
    grad_parts, home, left_stat, right_stat, left_root, right_root, first_moment, second_moment
):
    in_hbm = pl.BlockSpec(memory_space=pltpu.HBM)
    in_vmem = pl.BlockSpec(memory_space=pltpu.VMEM)
    n = len(PEERS)
    ring_piece = (H // LANES * RING + T, LANES)
    cross_piece = (H // LANES * CROSS + T, LANES)
    rows = (WIDE + T, LANES)
    products = (2 * WIDE + T, LANES)
    stat = pltpu.VMEM((NB, S, B), F32)
    tile = pltpu.VMEM((B, H), BF16)
    dma = pltpu.SemaphoreType.DMA
    scratch = [
        pltpu.SMEM((NB,), I32),
        *[pltpu.VMEM((NB, size, H), F32) for _, size in PARTS],
        *[stat] * 2,
        *[pltpu.VMEM((NB, 2, S, B), BF16)] * 2,
        *[pltpu.VMEM((12, *ring_piece), I16)] * 2,
        *[pltpu.VMEM((4, *cross_piece), I16)] * 2,
        *[pltpu.VMEM((3, *cross_piece), I16)] * 2,
        *[pltpu.VMEM((2, *ring_piece), I16)] * 2,
        pltpu.VMEM((B, H), F32),
        *[pltpu.VMEM((B, B), BF16)] * 2,
        *[pltpu.VMEM((NB, *rows), I16)] * 2,
        pltpu.VMEM((NB, *products), I16),
        pltpu.VMEM((NB, T // 2, LANES), F32),
        pltpu.VMEM((H, B), F32),
        pltpu.VMEM((B, B), F32),
        *[pltpu.VMEM((NB, 8, LANES), F32)] * 3,
        pltpu.VMEM((n, 8, LANES), F32),
        *[pltpu.VMEM((8, LANES), F32)] * 2,
        dma((8,)),
        *[dma((2, n))] * 2,
        *[dma((12,))] * 2,
        *[dma((4,))] * 2,
        *[dma((5,))] * 2,
        *[dma((8,))] * 2,
        *[dma((3, NB))] * 2,
        *[dma((n + 2,))] * 2,
        dma((2,)),
        pltpu.SemaphoreType.REGULAR,
    ]
    made = pl.pallas_call(
        kernel,
        out_shape=(pltpu.VMEM((NB, *products), I16), stat, stat, tile),
        in_specs=[in_hbm] * 6,
        out_specs=[in_vmem] * 4,
        scratch_shapes=scratch,
        compiler_params=pltpu.CompilerParams(
            collective_id=0, has_side_effects=True, vmem_limit_bytes=40 * 2**20
        ),
        cost_estimate=pl.CostEstimate(flops=2 * 10**9, bytes_accessed=9 * 2**20, transcendentals=0),
        name="shampoo_step",
    )(
        *[
            pltpu.with_memory_space_constraint(x, pltpu.HBM)
            for x in (home, grad_parts.reshape(NB, B, H), left_root, right_root, first_moment, second_moment)
        ]
    )
    stat_out = jax.ShapeDtypeStruct((NB, S, B), F32)
    return pl.pallas_call(
        finish_kernel,
        out_shape=(stat_out,) * 4 + (jax.ShapeDtypeStruct((B, H), BF16),),
        in_specs=[in_vmem] * 6,
        out_specs=[in_hbm] * 5,
        scratch_shapes=[stat, stat, dma((5,))],
        compiler_params=pltpu.CompilerParams(vmem_limit_bytes=16 * 2**20),
        name="finish_outputs",
    )(made[0], left_stat, right_stat, *made[1:])


def solution(mesh):
    rows = P("dp", "mp", None)
    in_specs = (P("dp", None, "mp"), P(), rows, rows, rows, rows, rows, rows)
    out_specs = (rows, rows, rows, rows, P("dp", "mp"))
    return jax.shard_map(
        on_device, mesh=mesh, in_specs=in_specs, out_specs=out_specs, check_vma=False
    )
```
